32 devices in a mesh: fsdp: 2 (over x), ctx: 4 (over z), tp: 4 (over y, core).
Axes of the slice: x: 2, y: 2, z: 4, core: 2. Of those that a mesh axis runs over, the one named last changes fastest.
Arguments:
- block_input: bfloat16 [2, 2048, 2048], P('fsdp', 'ctx'), may hold values from -6 to 6
- segment_ids: int32 [2, 2048], P('fsdp'), may hold values from 0 to 4, as said below
- attention_gain: bfloat16 [2048], P('fsdp'), may hold values from 0.25 to 1.75
- query_weight: bfloat16 [2048, 2048], P('fsdp', 'tp'), may hold values from -0.125 to 0.125
- key_weight: bfloat16 [2048, 512], P('fsdp', 'tp'), may hold values from -0.125 to 0.125
- value_weight: bfloat16 [2048, 512], P('fsdp', 'tp'), may hold values from -0.125 to 0.125
- out_weight: bfloat16 [2048, 2048], P('tp', 'fsdp'), may hold values from -0.5 to 0.5
- feed_gain: bfloat16 [2048], P('fsdp'), may hold values from 0.25 to 1.75
- gate_weight: bfloat16 [2048, 8192], P('fsdp', 'tp'), may hold values from -0.125 to 0.125
- up_weight: bfloat16 [2048, 8192], P('fsdp', 'tp'), may hold values from -0.125 to 0.125
- down_weight: bfloat16 [8192, 2048], P('tp', 'fsdp'), may hold values from -0.0625 to 0.0625
- cotangent: bfloat16 [2, 2048, 2048], P('fsdp', 'ctx'), may hold values from -6 to 6
Outputs:
- block_out: bfloat16 [2, 2048, 2048], P('fsdp', 'ctx')
- input_grad: bfloat16 [2, 2048, 2048], P('fsdp', 'ctx')
- attention_gain_grad: float32 [2048], P('fsdp')
- query_grad: float32 [2048, 2048], P('fsdp', 'tp')
- key_grad: float32 [2048, 512], P('fsdp', 'tp')
- value_grad: float32 [2048, 512], P('fsdp', 'tp')
- out_weight_grad: float32 [2048, 2048], P('tp', 'fsdp')
- feed_gain_grad: float32 [2048], P('fsdp')
- gate_grad: float32 [2048, 8192], P('fsdp', 'tp')
- up_grad: float32 [2048, 8192], P('fsdp', 'tp')
- down_grad: float32 [8192, 2048], P('tp', 'fsdp')
The draws below stay inside these ranges and needn't reach their ends.
Inputs may be any that keep to these rules, and one draw needn't show every extreme that they name: `segment_ids`: along each sequence the ids never fall and begin at 0; id 4 is the padding, which ends every sequence.
All inputs are finite; a program needn't handle non-finite values.
Results may differ from the reference program's by a relative error of at most 0.014.
Values may be sent and summed in bfloat16 or wider, within the bound.
A program may use at most 256 MiB of HBM per device.

```python
import jax
import jax.numpy as jnp
from jax import lax

D = 2048
HQ = 32
HK = 8
HD = 64
FF = 8192
SEQ_LEN = 2048
WINDOW = 1024
SEQ_DEV = 1
SEQS = 2


def draw_segment_ids(key, part):
    key = jax.random.fold_in(key, 7)
    key_pad, key_cut, key_pick = jax.random.split(key, 3)
    pad_len = jax.random.randint(key_pad, (SEQS, 1), SEQ_LEN // 32, SEQ_LEN // 16)
    real_len = SEQ_LEN - pad_len
    cut_frac = jax.random.randint(key_cut, (SEQS, 3), 0, 4096)
    cut_pos = 1 + cut_frac * (real_len - 1) // 4096
    long_pick = jax.random.randint(key_pick, (SEQS // SEQ_DEV,), 0, SEQ_DEV)
    seq_rank = jnp.arange(SEQS, dtype=jnp.int32)
    is_long = seq_rank % SEQ_DEV == jnp.repeat(long_pick, SEQ_DEV)
    cut_pos = jnp.where(is_long[:, None], SEQ_LEN, cut_pos)
    position = jnp.arange(SEQ_LEN, dtype=jnp.int32)
    seg_ids = jnp.sum((cut_pos[:, None, :] <= position[None, :, None]).astype(jnp.int32), axis=-1)
    return jnp.where(position[None, :] >= real_len, 4, seg_ids).astype(jnp.int32)


def block_levels(key, extent, cuts, low, largest):
    gain, own = 1.0, jax.random.fold_in(key, 6)
    for axis_at, blocks in cuts:
        steps = jnp.exp(jax.random.uniform(jax.random.fold_in(own, axis_at), (blocks,), jnp.float32, low / len(cuts), largest / len(cuts)))
        gain = gain * jnp.repeat(steps, extent[axis_at] // blocks).reshape([-1 if axis == axis_at else 1 for axis in range(len(extent))])
    return gain


def gaussian(stream_key, shape, width, limit, cuts=(), kind=jnp.bfloat16):
    level = block_levels(stream_key, shape, cuts, -0.22, 0.18) if cuts else 1.0
    drawn = jax.random.normal(stream_key, shape, jnp.float32) * width * level
    return jnp.minimum(jnp.maximum(drawn, -limit), limit).astype(kind)


def setup_inputs(seed: int = 0) -> dict:
    arg_keys = jax.random.split(jax.random.key(seed), 13)
    return {
        "block_input": gaussian(arg_keys[0], (SEQS, SEQ_LEN, D), 1.0, 6.0, ((0, 2), (1, 4))),
        "segment_ids": draw_segment_ids(jax.random.fold_in(arg_keys[12], 71), 0),
        "attention_gain": jnp.clip(1.0 + 0.15 * jax.random.normal(arg_keys[2], (D,), jnp.float32), 0.25, 1.75).astype(jnp.bfloat16),
        "query_weight": gaussian(arg_keys[3], (D, HQ * HD), D ** -0.5, 0.125, ((0, 2), (1, 4))),
        "key_weight": gaussian(arg_keys[4], (D, HK * HD), D ** -0.5, 0.125, ((0, 2), (1, 4))),
        "value_weight": gaussian(arg_keys[5], (D, HK * HD), D ** -0.5, 0.125, ((0, 2), (1, 4))),
        "out_weight": gaussian(arg_keys[6], (HQ * HD, D), (HQ * HD // 16) ** -0.5, 0.5, ((0, 4), (1, 2))),
        "feed_gain": jnp.clip(1.0 + 0.15 * jax.random.normal(arg_keys[7], (D,), jnp.float32), 0.25, 1.75).astype(jnp.bfloat16),
        "gate_weight": gaussian(arg_keys[8], (D, FF), D ** -0.5, 0.125, ((0, 2), (1, 4))),
        "up_weight": gaussian(arg_keys[9], (D, FF), D ** -0.5, 0.125, ((0, 2), (1, 4))),
        "down_weight": gaussian(arg_keys[10], (FF, D), FF ** -0.5, 0.0625, ((0, 4), (1, 2))),
        "cotangent": gaussian(arg_keys[11], (SEQS, SEQ_LEN, D), 1.0, 6.0, ((0, 2), (1, 4))),
    }


@jax.custom_vjp
def low(v):
    return lax.optimization_barrier(v.astype(jnp.bfloat16)).astype(jnp.float32)

@jax.custom_vjp
def low_back(v):
    return v

def low_keep(v):
    return (low(v), None)

def low_pass(kept, grad):
    return (grad,)

def back_keep(v):
    return (v, None)

def back_low(kept, grad):
    return (low(grad),)
low.defvjp(low_keep, low_pass)
low_back.defvjp(back_keep, back_low)
NORM_EPS = 1e-05
ROPE_BASE = 500000.0
MASK_FILL = -1e+30
HIGHEST = lax.Precision.HIGHEST

def matmul(matrix, other_side):
    return jnp.dot(matrix, other_side, precision=HIGHEST, preferred_element_type=jnp.float32)

def rms_normed(values):
    row_scale = lax.rsqrt(lax.optimization_barrier(jnp.mean(values * values, axis=-1, keepdims=True)) + NORM_EPS)
    return values * row_scale

def start_positions(seg_row):
    index_row = jnp.arange(seg_row.shape[0], dtype=jnp.int32)
    begins = jnp.concatenate([jnp.ones((1,), dtype=bool), seg_row[1:] != seg_row[:-1]])
    return index_row - lax.cummax(jnp.where(begins, index_row, 0), axis=0)

def rope_tables(positions, head_size):
    half_size = head_size // 2
    frequency = ROPE_BASE ** (-(jnp.arange(half_size, dtype=jnp.float32) * 2.0 / head_size))
    angles = positions.astype(jnp.float32)[..., None] * frequency
    return (jnp.cos(angles), jnp.sin(angles))

def rotate(vectors, cosine, sine_val):
    half_size = vectors.shape[-1] // 2
    front_half = vectors[..., :half_size]
    back_half = vectors[..., half_size:]
    cosine_wide = cosine[..., None, :]
    sine_wide = sine_val[..., None, :]
    return jnp.concatenate([front_half * cosine_wide - back_half * sine_wide, back_half * cosine_wide + front_half * sine_wide], axis=-1)

def sequence_forward(inputs, seg_row, params):
    gain_a, query_w, key_w, value_w, out_w, gain_m, gate_w, up_w, down_w = params
    length = inputs.shape[0]
    group_size = HQ // HK
    hidden_a = low(rms_normed(inputs) * gain_a)
    query_raw = matmul(hidden_a, query_w).reshape(length, HQ, HD)
    key_raw = matmul(hidden_a, key_w).reshape(length, HK, HD)
    value_raw = matmul(hidden_a, value_w).reshape(length, HK, HD)
    cosine, sine_val = rope_tables(start_positions(seg_row), HD)
    query_rot = low(rotate(low_back(query_raw), cosine, sine_val)).reshape(length, HK, group_size, HD)
    key_rot = low(rotate(low_back(key_raw), cosine, sine_val))
    values = low(low_back(value_raw))
    key_index = jnp.arange(length, dtype=jnp.int32)
    block_rows = min(512, length)
    score_scale = HD ** (-0.5)

    def attend_block(block_start):
        query_block = lax.dynamic_slice_in_dim(query_rot, block_start, block_rows, 0)
        seg_block = lax.dynamic_slice_in_dim(seg_row, block_start, block_rows, 0)
        row_index = block_start + jnp.arange(block_rows, dtype=jnp.int32)
        distance = row_index[:, None] - key_index[None, :]
        allowed = (seg_block[:, None] == seg_row[None, :]) & (distance >= 0) & (distance < WINDOW)
        scores = low_back(score_scale * jnp.einsum('qkgd,lkd->kgql', query_block, key_rot, precision=HIGHEST))
        scores = jnp.where(allowed, scores, MASK_FILL)
        row_max = lax.optimization_barrier(jnp.max(scores, axis=-1, keepdims=True))
        exponent = jnp.exp(scores - row_max)
        attention_weights = low(exponent / lax.optimization_barrier(jnp.sum(exponent, axis=-1, keepdims=True)))
        return jnp.einsum('kgql,lkd->qkgd', attention_weights, values, precision=HIGHEST)
    block_starts = jnp.arange(length // block_rows, dtype=jnp.int32) * block_rows
    heads_out = lax.map(jax.checkpoint(attend_block), block_starts)
    mixed = low(low_back(heads_out.reshape(length, HQ * HD)))
    middle = inputs + low_back(matmul(mixed, out_w))
    hidden_m = low(rms_normed(middle) * gain_m)
    gate_value = low_back(matmul(hidden_m, gate_w))
    up_value = low_back(matmul(hidden_m, up_w))
    activated = low(jax.nn.silu(gate_value) * up_value)
    return middle + low_back(matmul(activated, down_w))

def reference(block_input, segment_ids, attention_gain, query_weight, key_weight, value_weight, out_weight, feed_gain, gate_weight, up_weight, down_weight, cotangent):
    params = (attention_gain.astype(jnp.float32), query_weight.astype(jnp.float32), key_weight.astype(jnp.float32), value_weight.astype(jnp.float32), out_weight.astype(jnp.float32), feed_gain.astype(jnp.float32), gate_weight.astype(jnp.float32), up_weight.astype(jnp.float32), down_weight.astype(jnp.float32))
    inputs = block_input.astype(jnp.float32)

    def forward(all_inputs, all_params):

        def one_sequence(seq_pair):
            return sequence_forward(seq_pair[0], seq_pair[1], all_params)
        return lax.map(one_sequence, (all_inputs, segment_ids))
    outputs, pullback = jax.vjp(forward, inputs, params)
    input_grad, param_grads = pullback(cotangent.astype(jnp.float32))
    return (outputs.astype(jnp.bfloat16), input_grad.astype(jnp.bfloat16), param_grads[0], param_grads[1], param_grads[2], param_grads[3], param_grads[4], param_grads[5], param_grads[6], param_grads[7], param_grads[8])
```

```python
import functools

import jax
import jax.numpy as jnp
from jax import lax
from jax.experimental import pallas as pl
from jax.experimental.pallas import tpu as pltpu
from jax.sharding import PartitionSpec as P

HD = 64
WINDOW = 1024
NORM_EPS = 1e-05
ROPE_BASE = 500000.0
MASK_FILL = -1e30
LANES = 128
F32 = jnp.float32
BF16 = jnp.bfloat16


def dot_rows(matrix, other_side):
    return jnp.dot(matrix, other_side, preferred_element_type=F32)


def dot_back(matrix, other_side):
    return lax.dot_general(matrix, other_side, (((1,), (1,)), ((), ())), preferred_element_type=F32)


def dot_outer(matrix, other_side):
    return lax.dot_general(matrix, other_side, (((0,), (0,)), ((), ())), preferred_element_type=F32)


def tie(*values):
    return lax.optimization_barrier(values)


def take(array, start, size, axis):
    return lax.dynamic_slice_in_dim(array, start, size, axis)


def doc_positions(segments):
    seq_count, seq_length = segments.shape
    index_grid = jnp.broadcast_to(jnp.arange(seq_length, dtype=jnp.int32)[None, :], segments.shape)
    begins = jnp.concatenate(
        [jnp.ones((seq_count, 1), dtype=bool), segments[:, 1:] != segments[:, :-1]], axis=1
    )
    return index_grid - lax.cummax(jnp.where(begins, index_grid, 0), axis=1)


def rope_tables(positions):
    half_size = HD // 2
    frequency = ROPE_BASE ** (-(jnp.arange(half_size, dtype=F32) * 2.0 / HD))
    angles = positions.astype(F32)[:, None] * frequency
    cosine, sine = jnp.cos(angles), jnp.sin(angles)
    return jnp.concatenate([cosine] * 4, axis=1), jnp.concatenate([-sine, sine] * 2, axis=1)


def rotate(vectors, cosine, signed_sine):
    width = vectors.shape[1]
    half = HD // 2
    ahead = jnp.concatenate([vectors[:, half:], vectors[:, :half]], axis=1)
    behind = jnp.concatenate([vectors[:, -half:], vectors[:, :-half]], axis=1)
    first = (jnp.arange(width) % HD < half)[None, :]
    reps = width // LANES
    return vectors * jnp.tile(cosine, (1, reps)) + jnp.where(first, ahead, behind) * jnp.tile(
        signed_sine, (1, reps)
    )


def row_scale_of(values):
    return lax.rsqrt(jnp.mean(values * values, axis=-1, keepdims=True) + NORM_EPS)


def norm_back(grad_hidden, gain, normed, row_scale, residual_grad):
    grad_normed = grad_hidden * gain
    return residual_grad + row_scale * (
        grad_normed - normed * jnp.mean(grad_normed * normed, axis=-1, keepdims=True)
    )


def attend_forward_body(lead, heads, group, q_ref, kv_ref, qseg_ref, kseg_ref, mixed_ref, lse_ref):
    block = q_ref.shape[1]
    reach = kseg_ref.shape[-1]
    start = pl.multiple_of(pl.program_id(1) * block, block)
    window = kv_ref.at[0, pl.ds(start, reach), :]
    distance = (
        lax.broadcasted_iota(jnp.int32, (block, reach), 0)
        + lead
        - lax.broadcasted_iota(jnp.int32, (block, reach), 1)
    )
    allowed = (qseg_ref[0] == kseg_ref[0, 0]) & (distance >= 0) & (distance < WINDOW)
    bias = jnp.where(allowed, 0.0, MASK_FILL)
    lane = lax.broadcasted_iota(jnp.int32, (block, LANES), 1)
    log_sums = jnp.zeros((block, LANES), F32)
    kv_width = heads // group * HD
    outs = []
    for head in range(heads):
        shared = head // group * HD
        keys = window[:, shared : shared + HD]
        values = window[:, kv_width + shared : kv_width + shared + HD]
        scores = dot_back(q_ref[0, :, head * HD : (head + 1) * HD], keys) + bias
        row_max = jnp.max(scores, axis=-1, keepdims=True)
        exponent = jnp.exp(scores - row_max)
        row_total = jnp.sum(exponent, axis=-1, keepdims=True)
        probs = (exponent * (1.0 / row_total)).astype(BF16)
        outs.append(dot_rows(probs, values))
        log_sums = jnp.where(lane == head, row_max + jnp.log(row_total), log_sums)
    mixed_ref[0] = jnp.concatenate(outs, axis=1).astype(BF16)
    lse_ref[0] = log_sums


def attend_backward_body(
    lead, heads, group, q_ref, kv_ref, grad_ref, lse_ref, qseg_ref, kseg_ref, dq_ref, dkv_ref
):
    block = q_ref.shape[1]
    reach = block + lead
    step = pl.program_id(1)
    start = pl.multiple_of(step * block, block)
    window = kv_ref.at[0, pl.ds(start, reach), :]

    @pl.when(step == 0)
    def _():
        dkv_ref[...] = jnp.zeros_like(dkv_ref)

    distance = (
        lax.broadcasted_iota(jnp.int32, (reach, block), 1)
        + lead
        - lax.broadcasted_iota(jnp.int32, (reach, block), 0)
    )
    same = kseg_ref[0, pl.ds(start, reach), :] == qseg_ref[0]
    bias = jnp.where(same & (distance >= 0) & (distance < WINDOW), 0.0, MASK_FILL)
    kv_width = heads // group * HD
    key_grads, value_grads, query_grads = [], [], []
    for shared in range(heads // group):
        keys = window[:, shared * HD : (shared + 1) * HD]
        values = window[:, kv_width + shared * HD : kv_width + (shared + 1) * HD]
        key_sum = value_sum = None
        for member in range(group):
            head = shared * group + member
            query = q_ref[0, :, head * HD : (head + 1) * HD]
            grad = grad_ref[0, :, head * HD : (head + 1) * HD]
            probs = jnp.exp(dot_back(keys, query) + bias - lse_ref[0, head : head + 1, :])
            grad_probs = dot_back(values, grad)
            spread = jnp.sum(probs * grad_probs, axis=0, keepdims=True)
            grad_scores = (probs * (grad_probs - spread)).astype(BF16)
            value_part = dot_rows(probs.astype(BF16), grad)
            key_part = dot_rows(grad_scores, query)
            query_grads.append(dot_outer(grad_scores, keys) * HD**-0.5)
            value_sum = value_part if value_sum is None else value_sum + value_part
            key_sum = key_part if key_sum is None else key_sum + key_part
        key_grads.append(key_sum)
        value_grads.append(value_sum)
    dq_ref[0] = jnp.concatenate(query_grads, axis=1)
    dkv_ref[0, pl.ds(start, reach), :] += jnp.concatenate(key_grads + value_grads, axis=1)


def attention_plan(span, window):
    blocks_back = -(-(window - 1) // span)
    base = (blocks_back * span - (window - 1)) // LANES * LANES
    return blocks_back, base, blocks_back * span - base


def key_tiles(key_segments, base, lead, block, span):
    return jnp.stack(
        [
            key_segments[:, base + at : base + at + block + lead]
            for at in range(0, span, block)
        ],
        axis=1,
    )[:, :, None, :]


def attend_forward(query, keys_values, query_segments, key_segments, base, lead, group):
    seqs, span, width = query.shape
    block = min(LANES, span)
    heads = width // HD
    reach = block + lead
    keys_used = keys_values[:, base:]
    return pl.pallas_call(
        functools.partial(attend_forward_body, lead, heads, group),
        grid=(seqs, span // block),
        in_specs=[
            pl.BlockSpec((1, block, width), lambda s, i: (s, i, 0)),
            pl.BlockSpec((1,) + keys_used.shape[1:], lambda s, i: (s, 0, 0)),
            pl.BlockSpec((1, block, 1), lambda s, i: (s, i, 0)),
            pl.BlockSpec((1, 1, 1, reach), lambda s, i: (s, i, 0, 0)),
        ],
        out_specs=[
            pl.BlockSpec((1, block, width), lambda s, i: (s, i, 0)),
            pl.BlockSpec((1, block, LANES), lambda s, i: (s, i, 0)),
        ],
        out_shape=[
            jax.ShapeDtypeStruct(query.shape, BF16),
            jax.ShapeDtypeStruct((seqs, span, LANES), F32),
        ],
        compiler_params=pltpu.CompilerParams(vmem_limit_bytes=40 << 20),
        cost_estimate=pl.CostEstimate(
            flops=4 * seqs * span * reach * width, bytes_accessed=4 << 20, transcendentals=0
        ),
        name="attend_forward",
    )(query, keys_used, query_segments[:, :, None], key_tiles(key_segments, base, lead, block, span))


def attend_backward(
    query, keys_values, grad_mixed, log_sums, query_segments, key_segments, base, lead, group
):
    seqs, span, width = query.shape
    block = min(LANES, span)
    heads = width // HD
    reach = block + lead
    keys_used = keys_values[:, base:]
    whole_keys = pl.BlockSpec((1,) + keys_used.shape[1:], lambda s, i: (s, 0, 0))
    rows = pl.BlockSpec((1, block, width), lambda s, i: (s, i, 0))
    grad_query, grad_keys_values = pl.pallas_call(
        functools.partial(attend_backward_body, lead, heads, group),
        grid=(seqs, span // block),
        in_specs=[
            rows,
            whole_keys,
            rows,
            pl.BlockSpec((1, heads, block), lambda s, i: (s, 0, i)),
            pl.BlockSpec((1, 1, block), lambda s, i: (s, 0, i)),
            pl.BlockSpec((1, keys_used.shape[1], 1), lambda s, i: (s, 0, 0)),
        ],
        out_specs=[rows, whole_keys],
        out_shape=[
            jax.ShapeDtypeStruct(query.shape, F32),
            jax.ShapeDtypeStruct(keys_used.shape, F32),
        ],
        compiler_params=pltpu.CompilerParams(vmem_limit_bytes=40 << 20),
        cost_estimate=pl.CostEstimate(
            flops=10 * seqs * span * reach * width, bytes_accessed=6 << 20, transcendentals=0
        ),
        name="attend_backward",
    )(
        query,
        keys_used,
        grad_mixed,
        log_sums,
        query_segments[:, None, :],
        key_segments[:, base:, None],
    )
    return grad_query, jnp.pad(grad_keys_values, ((0, 0), (base, 0), (0, 0)))


def swap(value, axis, size, bit):
    return lax.ppermute(value, axis, [(i, i ^ bit) for i in range(size)])


def shift(value, axis, size, by):
    if abs(by) >= size:
        return jnp.zeros_like(value)
    return lax.ppermute(
        value, axis, [(i, i + by) for i in range(size) if 0 <= i + by < size]
    )


class Lane:
    def __init__(self, move, depth=2):
        self.move, self.depth, self.done = move, depth, []

    def send(self, value):
        if len(self.done) >= self.depth:
            value, self.done[-self.depth] = tie(value, self.done[-self.depth])
        self.done.append(self.move(value))
        return len(self.done) - 1

    def get(self, at):
        return self.done[at]


class LineSum:
    def __init__(self, axis):
        self.axis = axis
        index = lax.axis_index(axis)
        self.edge = (index == 0) | (index == 3)
        self.partial = None
        self.total = None
        self.outs = []

    def add(self, own):
        total, self.total = self.total, None
        if own is not None and total is not None and own.shape == total.shape:
            out_first = jnp.where(self.edge, own, total)
            sends = [out_first]
        else:
            sends = [v for v in (own, total) if v is not None]
        if self.partial is not None:
            sends.append(self.partial)
        sends = list(tie(*sends)) if len(sends) > 1 else sends
        partial = sends.pop() if self.partial is not None else None
        inward, outward = [(0, 1), (3, 2)], [(1, 0), (2, 3)]
        got_in = got_out = middle = None
        if len(sends) == 1 and own is not None and total is not None:
            got_in = got_out = lax.ppermute(sends[0], self.axis, inward + outward)
        else:
            if own is not None:
                got_in = lax.ppermute(sends.pop(0), self.axis, inward)
            if total is not None:
                got_out = lax.ppermute(sends.pop(0), self.axis, outward)
        if partial is not None:
            middle = lax.ppermute(partial, self.axis, [(1, 2), (2, 1)])
        got = [v for v in (got_in if got_in is not None else got_out, middle) if v is not None]
        if len(got) == 2:
            first, middle = tie(*got)
            if got_in is not None:
                got_out = first if got_out is got_in else got_out
                got_in = first
            else:
                got_out = first
        if total is not None:
            self.outs.append(jnp.where(self.edge, got_out, total).astype(F32))
        if partial is not None:
            self.total = (partial.astype(F32) + middle.astype(F32)).astype(BF16)
        self.partial = None
        if own is not None:
            self.partial = (own.astype(F32) + got_in.astype(F32)).astype(BF16)

    def finish(self):
        while self.partial is not None or self.total is not None:
            self.add(None)
        return self.outs


class WholeSum:
    def __init__(self, axis):
        self.axis, self.outs = axis, []

    def add(self, own):
        self.outs.append(lax.psum(own.astype(F32), self.axis))

    def finish(self):
        return self.outs


def shards(
    sizes,
    block_input,
    segment_ids,
    attention_gain,
    query_weight,
    key_weight,
    value_weight,
    out_weight,
    feed_gain,
    gate_weight,
    up_weight,
    down_weight,
    cotangent,
):
    shard_count, ctx_count, tp_count = sizes
    seqs, span, width = block_input.shape
    rows = seqs * span
    seq_length = segment_ids.shape[1]
    half = width // 2
    part = half // 2
    q_width = query_weight.shape[1]
    kv_width = key_weight.shape[1]
    feed_width = gate_weight.shape[1]
    group = q_width // kv_width
    shard, ctx, tp = (lax.axis_index(name) for name in ("fsdp", "ctx", "tp"))
    odd = ctx % 2
    sibling = tp % 2

    own_at = shard * half
    near_at = (1 - shard) * half + odd * part
    far_at = (1 - shard) * half + (1 - odd) * part

    def to_local(value):
        return jnp.concatenate(
            [
                take(value, own_at, half, 1),
                take(value, near_at, part, 1),
                take(value, far_at, part, 1),
            ],
            axis=1,
        )

    def other_half(value):
        return jnp.concatenate(
            [
                take(value, half + odd * part, part, 1),
                take(value, half + (1 - odd) * part, part, 1),
            ],
            axis=1,
        )

    def from_local(value):
        own, other = value[:, :half], other_half(value)
        return jnp.where(
            shard == 0,
            jnp.concatenate([own, other], axis=1),
            jnp.concatenate([other, own], axis=1),
        )

    fsdp_lane = Lane(lambda value: swap(value, "fsdp", shard_count, 1))

    def fetch(weight, axis):
        at = fsdp_lane.send(take(weight, odd * part, part, axis))
        return lambda: (fsdp_lane.get(at), swap(fsdp_lane.get(at), "ctx", ctx_count, 1))

    def swap_half(value):
        mine = take(value, sibling * (rows // 2), rows // 2, 0)
        at = fsdp_lane.send(mine)

        def land():
            got = fsdp_lane.get(at)
            other = swap(got, "tp", tp_count, 1)
            return jnp.where(
                sibling == 0,
                jnp.concatenate([got, other], axis=0),
                jnp.concatenate([other, got], axis=0),
            )

        return land

    def tp_sum(first, second):
        if tp_count != 4:
            whole = jnp.where(
                sibling == 0,
                jnp.concatenate([second, first], axis=0),
                jnp.concatenate([first, second], axis=0),
            )
            return lax.psum(whole, "tp")
        chip = (second + swap(first.astype(BF16), "tp", tp_count, 1).astype(F32)).astype(BF16)
        total = (chip.astype(F32) + swap(chip, "tp", tp_count, 2).astype(F32)).astype(BF16)
        other = swap(total, "tp", tp_count, 1)
        return jnp.where(
            sibling == 0,
            jnp.concatenate([total, other], axis=0),
            jnp.concatenate([other, total], axis=0),
        ).astype(F32)

    def row_halves(value):
        return (
            take(value, (1 - sibling) * (rows // 2), rows // 2, 0),
            take(value, sibling * (rows // 2), rows // 2, 0),
        )

    gains_own = jnp.stack([attention_gain, feed_gain])
    gains_other = swap(gains_own, "fsdp", shard_count, 1)
    gains = jnp.concatenate(
        [gains_own, take(gains_other, odd * part, part, 1), take(gains_other, (1 - odd) * part, part, 1)],
        axis=1,
    ).astype(F32)
    gain_a, gain_m = gains[0:1], gains[1:2]

    qkv_own = jnp.concatenate([query_weight, key_weight, value_weight], axis=1)
    qkv_fetch = fetch(qkv_own, 0)
    out_fetch = fetch(out_weight, 1)
    feed_cuts = 2
    feed_part = feed_width // feed_cuts
    feed_fetch = []
    for cut in range(feed_cuts):
        columns = slice(cut * feed_part, (cut + 1) * feed_part)
        feed_fetch.append((fetch(gate_weight[:, columns], 0), fetch(up_weight[:, columns], 0)))

    span_start = ctx * span
    positions = take(doc_positions(segment_ids), span_start, span, 1).reshape(rows)
    query_segments = take(segment_ids, span_start, span, 1)
    cosine, sine = rope_tables(positions)
    blocks_back, base, lead = attention_plan(span, WINDOW)
    key_segments = take(
        jnp.pad(segment_ids, ((0, 0), (blocks_back * span, 0)), constant_values=-1),
        span_start,
        (blocks_back + 1) * span,
        1,
    )

    inputs = to_local(block_input.reshape(rows, width)).astype(F32)
    grad_rows = to_local(cotangent.reshape(rows, width))
    scale_a = row_scale_of(inputs)
    normed_a = inputs * scale_a
    hidden_a = (normed_a * gain_a).astype(BF16)

    def dot_pieces(matrix, own, pieces):
        near, far = pieces
        return (
            dot_rows(matrix[:, :half], own)
            + dot_rows(matrix[:, half : half + part], near)
            + dot_rows(matrix[:, half + part :], far)
        )

    def back_pieces(matrix, own, pieces):
        near, far = pieces
        return jnp.concatenate(
            [dot_back(matrix, own), dot_back(matrix, near), dot_back(matrix, far)], axis=1
        )

    qkv_pieces = qkv_fetch()
    qkv = dot_pieces(hidden_a, qkv_own, qkv_pieces)
    key_low = rotate(qkv[:, q_width : q_width + kv_width], cosine, sine).astype(BF16)
    value_low = qkv[:, q_width + kv_width :].astype(BF16)
    keys_values = jnp.concatenate([key_low, value_low], axis=1).reshape(seqs, span, 2 * kv_width)
    keys_values = jnp.concatenate(
        [shift(keys_values, "ctx", ctx_count, back) for back in range(blocks_back, 0, -1)]
        + [keys_values],
        axis=1,
    )
    query_low = (rotate(qkv[:, :q_width], cosine, sine).astype(BF16) * HD**-0.5).reshape(
        seqs, span, q_width
    )
    mixed, log_sums = attend_forward(
        query_low, keys_values, query_segments, key_segments, base, lead, group
    )
    mixed_low = mixed.reshape(rows, q_width)
    out_pieces = out_fetch()

    def out_project(matrix):
        return jnp.concatenate(
            [dot_rows(matrix, out_weight)] + [dot_rows(matrix, piece) for piece in out_pieces],
            axis=1,
        )

    branch_a = tp_sum(*(out_project(value) for value in row_halves(mixed_low)))
    middle = inputs + branch_a

    scale_m = row_scale_of(middle)
    normed_m = middle * scale_m
    hidden_m = (normed_m * gain_m).astype(BF16)
    feed_pieces = [(gate(), up()) for gate, up in feed_fetch]
    gate_cuts, up_cuts, act_cuts, act_other = [], [], [], []
    for cut in range(feed_cuts):
        columns = slice(cut * feed_part, (cut + 1) * feed_part)
        gate_value = dot_pieces(hidden_m, gate_weight[:, columns], feed_pieces[cut][0])
        up_value = dot_pieces(hidden_m, up_weight[:, columns], feed_pieces[cut][1])
        activated = (jax.nn.silu(gate_value) * up_value).astype(BF16)
        gate_cuts.append(gate_value)
        up_cuts.append(up_value)
        act_cuts.append(activated)

    grad_land = swap_half(other_half(grad_rows))
    act_at = [fsdp_lane.send(act_cuts[0])]
    down_fetch = [fetch(down_weight[:feed_part], 1)]
    act_at.append(fsdp_lane.send(act_cuts[1]))
    down_fetch.append(fetch(down_weight[feed_part:], 1))
    hidden_m_land = swap_half(other_half(hidden_m))

    line = [LineSum("ctx") if ctx_count == 4 else WholeSum("ctx") for _ in range(2)]
    made = []

    def reduce_over_ctx(own):
        at = len(made)
        made.append(own)
        line[at % 2].add(own)

    grad_own, grad_other = grad_rows[:, :half], grad_land()
    for cut in range(feed_cuts):
        other = fsdp_lane.get(act_at[cut])
        for piece in range(2):
            columns = slice(piece * feed_part // 2, (piece + 1) * feed_part // 2)
            reduce_over_ctx(
                (
                    dot_outer(act_cuts[cut][:, columns], grad_own)
                    + dot_outer(other[:, columns], grad_other)
                ).astype(BF16)
            )

    down_pieces = [land() for land in down_fetch]
    grad_gate_cuts, grad_up_cuts, gate_at, up_at = [], [], [], []
    for cut in range(feed_cuts):
        columns = slice(cut * feed_part, (cut + 1) * feed_part)
        near, far = down_pieces[cut]
        grad_act = (
            dot_back(grad_rows[:, :half], down_weight[columns])
            + dot_back(grad_rows[:, half : half + part], near)
            + dot_back(grad_rows[:, half + part :], far)
        )
        gate_value, up_value = gate_cuts[cut], up_cuts[cut]
        sigmoid_gate = jax.nn.sigmoid(gate_value)
        grad_gate = (
            grad_act * up_value * sigmoid_gate * (1.0 + gate_value * (1.0 - sigmoid_gate))
        ).astype(BF16)
        grad_up = (grad_act * gate_value * sigmoid_gate).astype(BF16)
        gate_at.append(fsdp_lane.send(grad_gate))
        up_at.append(fsdp_lane.send(grad_up))
        grad_gate_cuts.append(grad_gate)
        grad_up_cuts.append(grad_up)

    def feed_back(which):
        total = None
        for cut in range(feed_cuts):
            columns = slice(cut * feed_part, (cut + 1) * feed_part)
            gate_rows = row_halves(grad_gate_cuts[cut])[which]
            up_rows = row_halves(grad_up_cuts[cut])[which]
            value = back_pieces(gate_rows, gate_weight[:, columns], feed_pieces[cut][0])
            value += back_pieces(up_rows, up_weight[:, columns], feed_pieces[cut][1])
            total = value if total is None else total + value
        return total

    grad_hidden_m = tp_sum(feed_back(0), feed_back(1))
    feed_gain_part = jnp.sum(grad_hidden_m * normed_m, axis=0)
    grad_middle = norm_back(grad_hidden_m, gain_m, normed_m, scale_m, grad_rows.astype(F32))
    grad_branch = grad_middle.astype(BF16)

    hidden_own, hidden_other = hidden_m[:, :half], hidden_m_land()
    for cut in range(feed_cuts):
        for own, at in ((grad_gate_cuts[cut], gate_at[cut]), (grad_up_cuts[cut], up_at[cut])):
            other = fsdp_lane.get(at)
            for piece in range(2):
                columns = slice(piece * part, (piece + 1) * part)
                reduce_over_ctx(
                    (
                        dot_outer(hidden_own[:, columns], own)
                        + dot_outer(hidden_other[:, columns], other)
                    ).astype(BF16)
                )

    def down_project(which):
        total = None
        for cut in range(feed_cuts):
            act_rows = row_halves(act_cuts[cut])[which]
            columns = slice(cut * feed_part, (cut + 1) * feed_part)
            value = jnp.concatenate(
                [dot_rows(act_rows, down_weight[columns])]
                + [dot_rows(act_rows, piece) for piece in down_pieces[cut]],
                axis=1,
            )
            total = value if total is None else total + value
        return total

    branch_m = tp_sum(down_project(0), down_project(1))
    block_out = from_local((middle + branch_m).astype(BF16)).reshape(seqs, span, width)

    grad_mixed = (
        dot_back(grad_branch[:, :half], out_weight)
        + dot_back(grad_branch[:, half : half + part], out_pieces[0])
        + dot_back(grad_branch[:, half + part :], out_pieces[1])
    ).astype(BF16)
    branch_land = swap_half(other_half(grad_branch))
    mixed_at = fsdp_lane.send(mixed_low)
    hidden_a_land = swap_half(other_half(hidden_a))
    grad_query, grad_keys_values = attend_backward(
        query_low,
        keys_values,
        grad_mixed.reshape(seqs, span, q_width),
        jnp.swapaxes(log_sums, 1, 2)[:, : q_width // HD],
        query_segments,
        key_segments,
        base,
        lead,
        group,
    )
    kv_sum = grad_keys_values[:, blocks_back * span :]
    for back in range(1, blocks_back + 1):
        at = (blocks_back - back) * span
        kv_sum = kv_sum + shift(
            grad_keys_values[:, at : at + span].astype(BF16), "ctx", ctx_count, -back
        ).astype(F32)
    kv_sum = kv_sum.reshape(rows, 2 * kv_width)
    grad_qkv = jnp.concatenate(
        [
            rotate(grad_query.reshape(rows, q_width), cosine, -sine),
            rotate(kv_sum[:, :kv_width], cosine, -sine),
            kv_sum[:, kv_width:],
        ],
        axis=1,
    ).astype(BF16)
    qkv_at = fsdp_lane.send(grad_qkv)
    grad_hidden_a = tp_sum(
        *(back_pieces(value, qkv_own, qkv_pieces) for value in row_halves(grad_qkv))
    )
    attention_gain_part = jnp.sum(grad_hidden_a * normed_a, axis=0)
    input_grad = norm_back(grad_hidden_a, gain_a, normed_a, scale_a, grad_middle)
    input_grad = from_local(input_grad.astype(BF16)).reshape(seqs, span, width)

    reduce_over_ctx(
        (
            dot_outer(mixed_low, grad_branch[:, :half])
            + dot_outer(fsdp_lane.get(mixed_at), branch_land())
        ).astype(BF16)
    )
    own, other = grad_qkv, fsdp_lane.get(qkv_at)
    hidden_own, hidden_other = hidden_a[:, :half], hidden_a_land()

    def qkv_grad(columns, rows_at):
        return (
            dot_outer(hidden_own[:, rows_at], own[:, columns])
            + dot_outer(hidden_other[:, rows_at], other[:, columns])
        ).astype(BF16)

    row_cuts = [slice(0, part), slice(part, half)]
    reduce_over_ctx(
        jnp.concatenate([qkv_grad(slice(0, q_width), cut) for cut in row_cuts], axis=1)
    )
    reduce_over_ctx(
        jnp.concatenate([qkv_grad(slice(q_width, None), cut) for cut in row_cuts], axis=1)
    )

    gain_parts = jnp.stack([attention_gain_part, feed_gain_part])
    gain_other = swap(other_half(gain_parts), "fsdp", shard_count, 1)
    gain_sums = lax.psum(gain_parts[:, :half] + gain_other, "ctx")

    outs = [line_sum.finish() for line_sum in line]
    sums = [outs[at % 2][at // 2] for at in range(len(made))]
    down_grad = jnp.concatenate(sums[:4], axis=0)
    gate_up = []
    for which in range(2):
        gate_up.append(
            jnp.concatenate(
                [
                    jnp.concatenate(sums[at : at + 2], axis=0)
                    for at in (4 + 2 * which, 8 + 2 * which)
                ],
                axis=1,
            )
        )
    out_grad, q_sum, kv_sum = sums[12:]
    query_grad = jnp.concatenate([q_sum[:, :q_width], q_sum[:, q_width:]], axis=0)
    kv_grad = jnp.concatenate([kv_sum[:, : 2 * kv_width], kv_sum[:, 2 * kv_width :]], axis=0)
    return (
        block_out,
        input_grad,
        gain_sums[0],
        query_grad,
        kv_grad[:, :kv_width],
        kv_grad[:, kv_width:],
        out_grad,
        gain_sums[1],
        gate_up[0],
        gate_up[1],
        down_grad,
    )


def solution(mesh):
    sizes = tuple(mesh.shape[name] for name in ("fsdp", "ctx", "tp"))
    in_specs = (
        P("fsdp", "ctx", None),
        P("fsdp", None),
        P("fsdp"),
        P("fsdp", "tp"),
        P("fsdp", "tp"),
        P("fsdp", "tp"),
        P("tp", "fsdp"),
        P("fsdp"),
        P("fsdp", "tp"),
        P("fsdp", "tp"),
        P("tp", "fsdp"),
        P("fsdp", "ctx", None),
    )
    out_specs = (
        P("fsdp", "ctx", None),
        P("fsdp", "ctx", None),
        P("fsdp"),
        P("fsdp", "tp"),
        P("fsdp", "tp"),
        P("fsdp", "tp"),
        P("tp", "fsdp"),
        P("fsdp"),
        P("fsdp", "tp"),
        P("fsdp", "tp"),
        P("tp", "fsdp"),
    )
    return jax.shard_map(
        functools.partial(shards, sizes),
        mesh=mesh,
        in_specs=in_specs,
        out_specs=out_specs,
        check_vma=False,
    )
```

```python
import functools

import jax
import jax.numpy as jnp
from jax import lax
from jax.experimental import pallas as pl
from jax.experimental.pallas import tpu as pltpu
from jax.sharding import PartitionSpec as P

HD = 64
WINDOW = 1024
NORM_EPS = 1e-05
ROPE_BASE = 500000.0
MASK_FILL = -1e30
LANES = 128
F32 = jnp.float32
BF16 = jnp.bfloat16


def dot_rows(matrix, other_side):
    return jnp.dot(matrix, other_side, preferred_element_type=F32)


def dot_back(matrix, other_side):
    return lax.dot_general(matrix, other_side, (((1,), (1,)), ((), ())), preferred_element_type=F32)


def dot_outer(matrix, other_side):
    return lax.dot_general(matrix, other_side, (((0,), (0,)), ((), ())), preferred_element_type=F32)


def tie(*values):
    return lax.optimization_barrier(values)


def take(array, start, size, axis):
    return lax.dynamic_slice_in_dim(array, start, size, axis)


def doc_positions(segments):
    seq_count, seq_length = segments.shape
    index_grid = jnp.broadcast_to(jnp.arange(seq_length, dtype=jnp.int32)[None, :], segments.shape)
    begins = jnp.concatenate(
        [jnp.ones((seq_count, 1), dtype=bool), segments[:, 1:] != segments[:, :-1]], axis=1
    )
    return index_grid - lax.cummax(jnp.where(begins, index_grid, 0), axis=1)


def rope_tables(positions):
    half_size = HD // 2
    frequency = ROPE_BASE ** (-(jnp.arange(half_size, dtype=F32) * 2.0 / HD))
    angles = positions.astype(F32)[:, None] * frequency
    cosine, sine = jnp.cos(angles), jnp.sin(angles)
    return jnp.concatenate([cosine] * 4, axis=1), jnp.concatenate([-sine, sine] * 2, axis=1)


def rotate(vectors, cosine, signed_sine):
    width = vectors.shape[1]
    half = HD // 2
    ahead = jnp.concatenate([vectors[:, half:], vectors[:, :half]], axis=1)
    behind = jnp.concatenate([vectors[:, -half:], vectors[:, :-half]], axis=1)
    first = (jnp.arange(width) % HD < half)[None, :]
    reps = width // LANES
    return vectors * jnp.tile(cosine, (1, reps)) + jnp.where(first, ahead, behind) * jnp.tile(
        signed_sine, (1, reps)
    )


def row_scale_of(values):
    return lax.rsqrt(jnp.mean(values * values, axis=-1, keepdims=True) + NORM_EPS)


def norm_back(grad_hidden, gain, normed, row_scale, residual_grad):
    grad_normed = grad_hidden * gain
    return residual_grad + row_scale * (
        grad_normed - normed * jnp.mean(grad_normed * normed, axis=-1, keepdims=True)
    )


def attend_forward_body(lead, heads, group, q_ref, kv_ref, qseg_ref, kseg_ref, mixed_ref, lse_ref):
    block = q_ref.shape[1]
    reach = kseg_ref.shape[-1]
    start = pl.multiple_of(pl.program_id(1) * block, block)
    window = kv_ref.at[0, pl.ds(start, reach), :]
    distance = (
        lax.broadcasted_iota(jnp.int32, (block, reach), 0)
        + lead
        - lax.broadcasted_iota(jnp.int32, (block, reach), 1)
    )
    allowed = (qseg_ref[0] == kseg_ref[0, 0]) & (distance >= 0) & (distance < WINDOW)
    bias = jnp.where(allowed, 0.0, MASK_FILL)
    lane = lax.broadcasted_iota(jnp.int32, (block, LANES), 1)
    log_sums = jnp.zeros((block, LANES), F32)
    kv_width = heads // group * HD
    outs = []
    for head in range(heads):
        shared = head // group * HD
        keys = window[:, shared : shared + HD]
        values = window[:, kv_width + shared : kv_width + shared + HD]
        scores = dot_back(q_ref[0, :, head * HD : (head + 1) * HD], keys) + bias
        row_max = jnp.max(scores, axis=-1, keepdims=True)
        exponent = jnp.exp(scores - row_max)
        row_total = jnp.sum(exponent, axis=-1, keepdims=True)
        probs = (exponent * (1.0 / row_total)).astype(BF16)
        outs.append(dot_rows(probs, values))
        log_sums = jnp.where(lane == head, row_max + jnp.log(row_total), log_sums)
    mixed_ref[0] = jnp.concatenate(outs, axis=1).astype(BF16)
    lse_ref[0] = log_sums


def attend_backward_body(
    lead, heads, group, q_ref, kv_ref, grad_ref, lse_ref, qseg_ref, kseg_ref, dq_ref, dkv_ref
):
    block = q_ref.shape[1]
    reach = block + lead
    step = pl.program_id(1)
    start = pl.multiple_of(step * block, block)
    window = kv_ref.at[0, pl.ds(start, reach), :]

    @pl.when(step == 0)
    def _():
        dkv_ref[...] = jnp.zeros_like(dkv_ref)

    distance = (
        lax.broadcasted_iota(jnp.int32, (reach, block), 1)
        + lead
        - lax.broadcasted_iota(jnp.int32, (reach, block), 0)
    )
    same = kseg_ref[0, pl.ds(start, reach), :] == qseg_ref[0]
    bias = jnp.where(same & (distance >= 0) & (distance < WINDOW), 0.0, MASK_FILL)
    query_grad, keys_grad = backward_tile(
        heads,
        group,
        lambda head: q_ref[0, :, head * HD : (head + 1) * HD],
        lambda head: grad_ref[0, :, head * HD : (head + 1) * HD],
        lambda head: lse_ref[0, head : head + 1, :],
        lambda at: window[:, at * HD : (at + 1) * HD],
        bias,
    )
    dq_ref[0] = query_grad
    dkv_ref[0, pl.ds(start, reach), :] += keys_grad


def backward_tile(heads, group, query_of, grad_of, log_sum_of, window_of, bias):
    key_grads, value_grads, query_grads = [], [], []
    shared_heads = heads // group
    for shared in range(shared_heads):
        keys, values = window_of(shared), window_of(shared_heads + shared)
        key_sum = value_sum = None
        for member in range(group):
            head = shared * group + member
            query, grad = query_of(head), grad_of(head)
            probs = jnp.exp(dot_back(keys, query) + bias - log_sum_of(head))
            grad_probs = dot_back(values, grad)
            spread = jnp.sum(probs * grad_probs, axis=0, keepdims=True)
            grad_scores = (probs * (grad_probs - spread)).astype(BF16)
            value_part = dot_rows(probs.astype(BF16), grad)
            key_part = dot_rows(grad_scores, query)
            query_grads.append(dot_outer(grad_scores, keys) * HD**-0.5)
            value_sum = value_part if value_sum is None else value_sum + value_part
            key_sum = key_part if key_sum is None else key_sum + key_part
        key_grads.append(key_sum)
        value_grads.append(value_sum)
    return jnp.concatenate(query_grads, axis=1), jnp.concatenate(key_grads + value_grads, axis=1)


def attention_plan(span, window):
    blocks_back = -(-(window - 1) // span)
    base = (blocks_back * span - (window - 1)) // LANES * LANES
    return blocks_back, base, blocks_back * span - base


def key_tiles(key_segments, base, lead, block, span):
    return jnp.stack(
        [
            key_segments[:, base + at : base + at + block + lead]
            for at in range(0, span, block)
        ],
        axis=1,
    )[:, :, None, :]


def attend_forward(query, keys_values, query_segments, key_segments, base, lead, group):
    seqs, span, width = query.shape
    block = min(LANES, span)
    heads = width // HD
    reach = block + lead
    keys_used = keys_values[:, base:]
    return pl.pallas_call(
        functools.partial(attend_forward_body, lead, heads, group),
        grid=(seqs, span // block),
        in_specs=[
            pl.BlockSpec((1, block, width), lambda s, i: (s, i, 0)),
            pl.BlockSpec((1,) + keys_used.shape[1:], lambda s, i: (s, 0, 0)),
            pl.BlockSpec((1, block, 1), lambda s, i: (s, i, 0)),
            pl.BlockSpec((1, 1, 1, reach), lambda s, i: (s, i, 0, 0)),
        ],
        out_specs=[
            pl.BlockSpec((1, block, width), lambda s, i: (s, i, 0)),
            pl.BlockSpec((1, block, LANES), lambda s, i: (s, i, 0)),
        ],
        out_shape=[
            jax.ShapeDtypeStruct(query.shape, BF16),
            jax.ShapeDtypeStruct((seqs, span, LANES), F32),
        ],
        compiler_params=pltpu.CompilerParams(vmem_limit_bytes=40 << 20),
        cost_estimate=pl.CostEstimate(
            flops=70 * seqs * span * reach * width, bytes_accessed=4 << 20, transcendentals=0
        ),
        name="attend_forward",
    )(query, keys_used, query_segments[:, :, None], key_tiles(key_segments, base, lead, block, span))


def attend_backward(
    query, keys_values, grad_mixed, log_sums, query_segments, key_segments, base, lead, group
):
    seqs, span, width = query.shape
    block = min(LANES, span)
    heads = width // HD
    reach = block + lead
    keys_used = keys_values[:, base:]
    whole_keys = pl.BlockSpec((1,) + keys_used.shape[1:], lambda s, i: (s, 0, 0))
    rows = pl.BlockSpec((1, block, width), lambda s, i: (s, i, 0))
    grad_query, grad_keys_values = pl.pallas_call(
        functools.partial(attend_backward_body, lead, heads, group),
        grid=(seqs, span // block),
        in_specs=[
            rows,
            whole_keys,
            rows,
            pl.BlockSpec((1, heads, block), lambda s, i: (s, 0, i)),
            pl.BlockSpec((1, 1, block), lambda s, i: (s, 0, i)),
            pl.BlockSpec((1, keys_used.shape[1], 1), lambda s, i: (s, 0, 0)),
        ],
        out_specs=[rows, whole_keys],
        out_shape=[
            jax.ShapeDtypeStruct(query.shape, F32),
            jax.ShapeDtypeStruct(keys_used.shape, F32),
        ],
        compiler_params=pltpu.CompilerParams(vmem_limit_bytes=40 << 20),
        cost_estimate=pl.CostEstimate(
            flops=85 * seqs * span * reach * width, bytes_accessed=6 << 20, transcendentals=0
        ),
        name="attend_backward",
    )(
        query,
        keys_used,
        grad_mixed,
        log_sums,
        query_segments[:, None, :],
        key_segments[:, base:, None],
    )
    return grad_query, jnp.pad(grad_keys_values, ((0, 0), (base, 0), (0, 0)))


def whole(array):
    return pl.BlockSpec(array.shape, lambda *at: (0,) * array.ndim)


def kernel_cost(flops, moved):
    return pl.CostEstimate(flops=flops, bytes_accessed=moved, transcendentals=0)


def feed_forward_body(sizes, hidden_ref, *refs):
    count = len(sizes)
    gate_refs, up_refs = refs[:count], refs[count : 2 * count]
    gate_ref, up_ref, act_ref = refs[2 * count :]

    def project(pieces):
        total, at = None, 0
        for size, piece in zip(sizes, pieces):
            value = dot_rows(hidden_ref[:, at : at + size], piece[...])
            total = value if total is None else total + value
            at += size
        return total

    gate_value, up_value = project(gate_refs), project(up_refs)
    gate_ref[...] = gate_value
    up_ref[...] = up_value
    act_ref[...] = (gate_value * jax.nn.sigmoid(gate_value) * up_value).astype(BF16)


def feed_forward(hidden, gate_pieces, up_pieces, cut, columns):
    rows = hidden.shape[0]
    tile = min(512, columns)
    steps = columns // tile
    own = lambda w: pl.BlockSpec((w.shape[0], tile), lambda i: (0, cut * steps + i))
    rest = lambda w: pl.BlockSpec((w.shape[0], tile), lambda i: (0, i))
    specs = [own(gate_pieces[0])] + [rest(w) for w in gate_pieces[1:]]
    out = pl.BlockSpec((rows, tile), lambda i: (0, i))
    return pl.pallas_call(
        functools.partial(feed_forward_body, tuple(w.shape[0] for w in gate_pieces)),
        grid=(steps,),
        in_specs=[whole(hidden)] + specs + specs,
        out_specs=[out] * 3,
        out_shape=[
            jax.ShapeDtypeStruct((rows, columns), F32),
            jax.ShapeDtypeStruct((rows, columns), F32),
            jax.ShapeDtypeStruct((rows, columns), BF16),
        ],
        compiler_params=pltpu.CompilerParams(vmem_limit_bytes=40 << 20),
        cost_estimate=kernel_cost(6 * rows * columns * hidden.shape[1], 8 << 20),
        name="feed_forward",
    )(hidden, *gate_pieces, *up_pieces)


def feed_backward_body(sizes, grad_ref, *refs):
    count = len(sizes)
    gate_ref, up_ref, grad_gate_ref, grad_up_ref = refs[count:]
    grad_act, at = None, 0
    for size, piece in zip(sizes, refs[:count]):
        value = dot_back(grad_ref[:, at : at + size], piece[...])
        grad_act = value if grad_act is None else grad_act + value
        at += size
    gate_value = gate_ref[...]
    sigmoid_gate = jax.nn.sigmoid(gate_value)
    grad_up = grad_act * sigmoid_gate
    grad_gate_ref[...] = (
        grad_up * up_ref[...] * (1.0 + gate_value * (1.0 - sigmoid_gate))
    ).astype(BF16)
    grad_up_ref[...] = (grad_up * gate_value).astype(BF16)


def feed_backward(grad, down_pieces, gate_value, up_value, cut):
    rows, columns = gate_value.shape
    tile = min(512, columns)
    steps = columns // tile
    own = lambda w: pl.BlockSpec((tile, w.shape[1]), lambda i: (cut * steps + i, 0))
    rest = lambda w: pl.BlockSpec((tile, w.shape[1]), lambda i: (i, 0))
    out = pl.BlockSpec((rows, tile), lambda i: (0, i))
    return pl.pallas_call(
        functools.partial(feed_backward_body, tuple(w.shape[1] for w in down_pieces)),
        grid=(steps,),
        in_specs=[whole(grad), own(down_pieces[0])]
        + [rest(w) for w in down_pieces[1:]]
        + [out, out],
        out_specs=[out] * 2,
        out_shape=[jax.ShapeDtypeStruct((rows, columns), BF16)] * 2,
        compiler_params=pltpu.CompilerParams(vmem_limit_bytes=40 << 20),
        cost_estimate=kernel_cost(4 * rows * columns * grad.shape[1], 8 << 20),
        name="feed_backward",
    )(grad, *down_pieces, gate_value, up_value)


def project_body(cuts, steps, terms, pieces, transposed, sibling_ref, *refs):
    first_ref, second_ref, total_ref = refs[-3:]
    step = pl.program_id(0)
    lefts = refs[: cuts * terms]
    weights = refs[cuts * terms : -3]

    @pl.when(step == 0)
    def _():
        total_ref[...] = jnp.zeros_like(total_ref)

    for cut in range(cuts):

        @pl.when(step // steps == cut)
        def _():
            at = 0
            for piece in range(pieces):
                value = None
                for term in range(terms):
                    left = lefts[cut * terms + term][...]
                    weight = weights[(cut * terms + term) * pieces + piece][...]
                    part = dot_back(left, weight) if transposed else dot_rows(left, weight)
                    value = part if value is None else value + part
                total_ref[:, at : at + value.shape[1]] += value
                at += value.shape[1]

    @pl.when(step == cuts * steps - 1)
    def _():
        half = total_ref.shape[0] // 2
        mine = pl.multiple_of(sibling_ref[0] * half, half)
        theirs = pl.multiple_of((1 - sibling_ref[0]) * half, half)
        first_ref[...] = total_ref[pl.ds(theirs, half), :].astype(BF16)
        second_ref[...] = total_ref[pl.ds(mine, half), :]


def project(sibling, lefts, weights, width, transposed):
    cuts, terms, pieces = len(lefts), len(lefts[0]), len(weights[0][0])
    rows, columns = lefts[0][0].shape
    tile = min(512, columns)
    steps = columns // tile
    in_specs = [pl.BlockSpec(memory_space=pltpu.SMEM)]
    operands = []

    def clipped(cut):
        return lambda i: jnp.clip(i - cut * steps, 0, steps - 1)

    for cut in range(cuts):
        for left in lefts[cut]:
            in_specs.append(pl.BlockSpec((rows, tile), lambda i, f=clipped(cut): (0, f(i))))
            operands.append(left)
    for cut in range(cuts):
        for term in weights[cut]:
            for piece, weight in enumerate(term):
                offset = cut * steps if piece == 0 else 0
                if transposed:
                    spec = pl.BlockSpec(
                        (weight.shape[0], tile), lambda i, f=clipped(cut), o=offset: (0, o + f(i))
                    )
                else:
                    spec = pl.BlockSpec(
                        (tile, weight.shape[1]), lambda i, f=clipped(cut), o=offset: (o + f(i), 0)
                    )
                in_specs.append(spec)
                operands.append(weight)
    half_rows = jax.ShapeDtypeStruct((rows // 2, width), BF16)
    return pl.pallas_call(
        functools.partial(project_body, cuts, steps, terms, pieces, transposed),
        grid=(cuts * steps,),
        in_specs=in_specs,
        out_specs=[whole(half_rows)] * 2,
        out_shape=[half_rows, jax.ShapeDtypeStruct((rows // 2, width), F32)],
        scratch_shapes=[pltpu.VMEM((rows, width), F32)],
        compiler_params=pltpu.CompilerParams(vmem_limit_bytes=48 << 20),
        cost_estimate=kernel_cost(3 * terms * rows * columns * cuts * width, 16 << 20),
        name="project",
    )(sibling.reshape(1), *operands)


CHUNK_ROWS, CHUNK_COLUMNS = 256, 1024


def outer_sum_body(split, groups, left_ref, left_other_ref, *refs):
    out_ref = refs[-1]
    rights, others = refs[:groups], refs[groups : 2 * groups]
    blocks = left_ref.shape[1] // CHUNK_ROWS
    for group in range(groups):

        def emit():
            for block in range(blocks):
                rows = slice(block * CHUNK_ROWS, (block + 1) * CHUNK_ROWS)
                value = dot_outer(left_ref[:, rows], rights[group][...])
                value += dot_outer(left_other_ref[:, rows], others[group][...])
                width = value.shape[1]
                out_ref[0, :, block * width : (block + 1) * width] = value.astype(BF16)

        if groups == 1:
            emit()
        else:
            pl.when(pl.program_id(0) // split == group)(emit)


def outer_sum(pool, at, count, left, left_other, rights, rights_other):
    groups = len(rights)
    rows = left.shape[0]
    columns = CHUNK_ROWS * CHUNK_COLUMNS // rights[0].shape[1]
    split = left.shape[1] // columns
    left_spec = pl.BlockSpec((rows, columns), lambda i: (0, lax.rem(i, split)))
    operands = (left, left_other, *rights, *rights_other)
    in_specs = [left_spec] * 2 + [whole(value) for value in operands[2:]]
    aliases = {}
    if pool is not None:
        operands += (pool,)
        in_specs.append(pl.BlockSpec(memory_space=pl.ANY))
        aliases = {len(operands) - 1: 0}
    return pl.pallas_call(
        functools.partial(outer_sum_body, split, groups),
        grid=(split * groups,),
        in_specs=in_specs,
        out_specs=pl.BlockSpec((1, CHUNK_ROWS, CHUNK_COLUMNS), lambda i: (at + i, 0, 0)),
        out_shape=jax.ShapeDtypeStruct((count, CHUNK_ROWS, CHUNK_COLUMNS), BF16),
        input_output_aliases=aliases,
        compiler_params=pltpu.CompilerParams(vmem_limit_bytes=48 << 20),
        cost_estimate=kernel_cost(
            4 * split * groups * rows * CHUNK_ROWS * CHUNK_COLUMNS, 4 << 20
        ),
        name="outer_sum",
    )(*operands)


def widen_body(starts, pool_ref, *out_refs):
    step = pl.program_id(0)
    value = pool_ref[0].astype(F32)
    last = len(starts) - 1
    for at, start in enumerate(starts):
        stop = starts[at + 1] if at < last else pl.num_programs(0)

        @pl.when((step >= start) & (step < stop))
        def _():
            if at < last - 1:
                out_refs[at][...] = value
            elif at == last - 1:
                half = CHUNK_COLUMNS // 2
                out_refs[at][:CHUNK_ROWS] = value[:, :half]
                out_refs[at][CHUNK_ROWS:] = value[:, half:]
            else:
                width = out_refs[at].shape[1]
                for block in range(CHUNK_COLUMNS // (2 * width)):
                    rows = slice(block * CHUNK_ROWS, (block + 1) * CHUNK_ROWS)
                    left = 2 * block * width
                    out_refs[at][rows] = value[:, left : left + width]
                    out_refs[at + 1][rows] = value[:, left + width : left + 2 * width]


def widen(pool, starts, shapes):
    specs = []
    for at, shape in enumerate(shapes):
        which = min(at, len(starts) - 1)
        start = starts[which]
        stop = starts[which + 1] if which + 1 < len(starts) else pool.shape[0]
        size = stop - start
        block = (shape[0] * shape[1] // (size * CHUNK_COLUMNS), CHUNK_COLUMNS)
        if which == len(starts) - 1:
            block = shape
        elif which == len(starts) - 2:
            block = (2 * CHUNK_ROWS, shape[1])
        down = shape[0] // block[0]

        def place(i, start=start, size=size, down=down):
            k = jnp.clip(i - start, 0, size - 1)
            return lax.rem(k, down), k // down

        specs.append(pl.BlockSpec(block, place))
    return pl.pallas_call(
        functools.partial(widen_body, starts),
        grid=(pool.shape[0],),
        in_specs=[pl.BlockSpec((1, CHUNK_ROWS, CHUNK_COLUMNS), lambda i: (i, 0, 0))],
        out_specs=specs,
        out_shape=[jax.ShapeDtypeStruct(shape, F32) for shape in shapes],
        compiler_params=pltpu.CompilerParams(vmem_limit_bytes=48 << 20),
        cost_estimate=kernel_cost(1, 45 << 20),
        name="widen",
    )(pool)


def tail_body(plan, *refs):
    heads, group, lead, ready, starts, count = plan
    (
        pool_in, gate_refs, up_refs, hidden_m_ref, hidden_m_send, hidden_a_ref, hidden_a_send,
        branch_ref, branch_send, mixed_ref, out_refs, query_ref, keys_ref, log_ref,
        query_seg_ref, key_seg_ref, cosine_ref, sine_ref, qkv_refs, inputs_ref, scale_ref,
        gain_ref, grad_middle_ref,
        pool_ref, sum_ref, near_ref, across_ref, grad_ref, gain_out_ref,
        gate_land, up_land, hidden_m_land, hidden_a_land, branch_land, mixed_land, qkv_land,
        grad_mixed_ref, dq_ref, dkv_ref, kv_send, kv_land, qkv_grad_ref,
        first_ref, second_ref, core_land, chip_ref, y_land, total_ref, other_ref,
        own_buf, near_buf, part_buf, across_buf, total_buf, piece_buf,
        x_send, x_recv, tp_send, tp_recv, kv_send_sem, kv_recv_sem,
        send_sem, land_sem, cross_send, cross_land, keep_sem, load_sem, piece_sem,
    ) = refs
    rows, width = inputs_ref.shape
    half, part = width // 2, width // 4
    half_rows = rows // 2
    mesh_id = pl.DeviceIdType.MESH
    shard, ctx, tp = (lax.axis_index(name) for name in ("fsdp", "ctx", "tp"))
    sibling = lax.rem(tp, 2)
    core = tp + 1 - 2 * sibling
    across_y = lax.rem(tp + 2, 4)
    partner = 1 - shard
    pair = ctx + 1 - 2 * lax.rem(ctx, 2)
    across = 3 - ctx
    is_end = (ctx == 0) | (ctx == 3)
    is_middle = jnp.logical_not(is_end)

    kv_land[...] = jnp.zeros_like(kv_land)
    dkv_ref[...] = jnp.zeros_like(dkv_ref)

    barrier = pltpu.get_barrier_semaphore()
    others = [{"fsdp": partner}, {"tp": core}, {"tp": across_y}]
    others += [{"ctx": lax.rem(ctx + step, 4)} for step in (1, 2, 3)]
    for other in others:
        pl.semaphore_signal(barrier, inc=1, device_id=other, device_id_type=mesh_id)
    pl.semaphore_wait(barrier, len(others))

    def x_copy(at, source, land):
        return pltpu.make_async_remote_copy(
            src_ref=source, dst_ref=land, send_sem=x_send.at[at], recv_sem=x_recv.at[at],
            device_id={"fsdp": partner}, device_id_type=mesh_id,
        )

    cuts = len(gate_refs)
    gate_copies = [x_copy(i, gate_refs[i], gate_land[i]) for i in range(cuts)]
    up_copies = [x_copy(cuts + i, up_refs[i], up_land[i]) for i in range(cuts)]
    hidden_m_copy = x_copy(2 * cuts, hidden_m_send, hidden_m_land)
    branch_copy = x_copy(2 * cuts + 1, branch_send, branch_land)
    mixed_copy = x_copy(2 * cuts + 2, mixed_ref, mixed_land)
    hidden_a_copy = x_copy(2 * cuts + 3, hidden_a_send, hidden_a_land)
    qkv_copy = x_copy(2 * cuts + 4, qkv_grad_ref, qkv_land)
    queue = gate_copies + [hidden_m_copy] + up_copies
    queue += [branch_copy, mixed_copy, qkv_copy, hidden_a_copy]

    def send_next(first, last):
        for at in range(first, last):
            if at >= 2:
                queue[at - 2].wait_send()
            queue[at].start()

    def to_pair(source, land, k):
        return pltpu.make_async_remote_copy(
            src_ref=source, dst_ref=land.at[k], send_sem=send_sem.at[k],
            recv_sem=land_sem.at[k], device_id={"ctx": pair}, device_id_type=mesh_id,
        )

    def inward_copy(k):
        return to_pair(pool_ref.at[k], near_ref, k)

    def outward_copy(k):
        return to_pair(total_buf.at[lax.rem(k, 2)], sum_ref, k)

    def cross_copy(k):
        return pltpu.make_async_remote_copy(
            src_ref=part_buf.at[lax.rem(k, 4)], dst_ref=across_ref.at[k],
            send_sem=cross_send.at[k], recv_sem=cross_land.at[k],
            device_id={"ctx": across}, device_id_type=mesh_id,
        )

    def keep_copy(k):
        return pltpu.make_async_copy(total_buf.at[lax.rem(k, 2)], sum_ref.at[k], keep_sem.at[k])

    def load(source, buffer, at):
        return pltpu.make_async_copy(source, buffer, load_sem.at[at])

    lag = 2

    def inward(k):
        inward_copy(k).wait_recv()
        loads = [load(pool_ref.at[k], own_buf, 0), load(near_ref.at[k], near_buf, 1)]
        for copy in loads:
            copy.start()
        for copy in loads:
            copy.wait()
        part_buf[lax.rem(k, 4)] = (own_buf[...].astype(F32) + near_buf[...].astype(F32)).astype(
            BF16
        )
        cross_copy(k).start()

    def outward(k, reuse):
        cross_copy(k).wait_recv()
        copy = load(across_ref.at[k], across_buf, 2)
        copy.start()
        if reuse:
            keep_copy(k - 2).wait()
            outward_copy(k - 2).wait_send()
        copy.wait()
        total_buf[lax.rem(k, 2)] = (
            part_buf[lax.rem(k, 4)].astype(F32) + across_buf[...].astype(F32)
        ).astype(BF16)
        cross_copy(k).wait_send()
        outward_copy(k).start()
        keep_copy(k).start()

    ahead = 2

    def send_piece(k, carry):
        inward_copy(k).wait_send()

        @pl.when(k + ahead < count)
        def _():
            inward_copy(k + ahead).start()

        return carry

    def pump(first, last):
        @pl.when(is_end)
        def _():
            lax.fori_loop(min(first, count), min(last, count), send_piece, 0)

        @pl.when(is_middle)
        def _():
            k = first
            while k < min(last, lag + 2):
                inward(jnp.int32(k))
                if k >= lag:
                    outward(jnp.int32(k - lag), False)
                k += 1
            if k < min(last, count):

                def both(at, carry):
                    inward(at)
                    outward(at - lag, True)
                    return carry

                lax.fori_loop(k, min(last, count), both, 0)
            k = max(k, count)
            while k < last:
                outward(jnp.int32(k - lag), True)
                k += 1

    @pl.when(is_end)
    def _():
        for k in range(ahead):
            inward_copy(jnp.int32(k)).start()

    send_next(0, 2)

    grad_mixed = None
    at = 0
    for piece in out_refs:
        value = dot_back(branch_ref[:, at : at + piece.shape[1]], piece[...])
        grad_mixed = value if grad_mixed is None else grad_mixed + value
        at += piece.shape[1]
    grad_mixed_ref[...] = grad_mixed.astype(BF16)

    tile = log_ref.shape[2]
    tiles = rows // tile
    reach = tile + lead

    def attend(step, carry):
        start = pl.multiple_of(step * tile, tile)
        distance = (
            lax.broadcasted_iota(jnp.int32, (reach, tile), 1)
            + lead
            - lax.broadcasted_iota(jnp.int32, (reach, tile), 0)
        )
        same = key_seg_ref[pl.ds(start, reach), :] == query_seg_ref[step]
        bias = jnp.where(same & (distance >= 0) & (distance < WINDOW), 0.0, MASK_FILL)
        query_grad, keys_grad = backward_tile(
            heads,
            group,
            lambda head: query_ref[pl.ds(start, tile), head * HD : (head + 1) * HD],
            lambda head: grad_mixed_ref[pl.ds(start, tile), head * HD : (head + 1) * HD],
            lambda head: log_ref[step, head : head + 1, :],
            lambda at: keys_ref[pl.ds(start, reach), at * HD : (at + 1) * HD],
            bias,
        )
        dq_ref[pl.ds(start, tile), :] = query_grad
        dkv_ref[pl.ds(start, reach), :] += keys_grad
        return carry

    lax.fori_loop(0, tiles, attend, 0)
    pump(0, 2)
    send_next(2, 3)

    for back in (1, 2):
        kv_send[back - 1] = dkv_ref[(2 - back) * rows : (3 - back) * rows, :].astype(BF16)

    def kv_copy(back):
        return pltpu.make_async_remote_copy(
            src_ref=kv_send.at[back - 1], dst_ref=kv_land.at[back - 1],
            send_sem=kv_send_sem.at[back - 1], recv_sem=kv_recv_sem.at[back - 1],
            device_id={"ctx": lax.rem(ctx + 4 - back, 4)}, device_id_type=mesh_id,
        )

    for back in (1, 2):

        @pl.when(ctx >= back)
        def _():
            kv_copy(back).start()

    pump(2, 3)
    for back in (1, 2):

        @pl.when(ctx + back < 4)
        def _():
            kv_copy(back).wait_recv()

    send_next(3, 4)
    kv_width = dkv_ref.shape[1] // 2
    q_width = dq_ref.shape[1]
    cosine, sine = cosine_ref[...], sine_ref[...]
    front = lax.rem(lax.broadcasted_iota(jnp.int32, (rows, LANES), 1), HD) < HD // 2

    def unrotate(value):
        swapped = jnp.where(
            front, pltpu.roll(value, LANES - HD // 2, 1), pltpu.roll(value, HD // 2, 1)
        )
        return (value * cosine - swapped * sine).astype(BF16)

    for at in range(0, q_width, LANES):
        qkv_grad_ref[:, at : at + LANES] = unrotate(dq_ref[:, at : at + LANES])
    kv_sum = dkv_ref[2 * rows :, :]
    for back in range(2):
        kv_sum = kv_sum + kv_land[back].astype(F32)
    for at in range(0, kv_width, LANES):
        qkv_grad_ref[:, q_width + at : q_width + at + LANES] = unrotate(
            kv_sum[:, at : at + LANES]
        )
    qkv_grad_ref[:, q_width + kv_width :] = kv_sum[:, kv_width:].astype(BF16)

    def tp_copy(at, source, land, target):
        return pltpu.make_async_remote_copy(
            src_ref=source, dst_ref=land, send_sem=tp_send.at[at], recv_sem=tp_recv.at[at],
            device_id={"tp": target}, device_id_type=mesh_id,
        )

    first_copy = tp_copy(0, first_ref, core_land, core)
    y_copy = tp_copy(1, chip_ref, y_land, across_y)
    total_copy = tp_copy(2, total_ref, other_ref, core)
    theirs = pl.multiple_of((1 - sibling) * half_rows, half_rows)
    mine = pl.multiple_of(sibling * half_rows, half_rows)

    def back_project(start, store):
        at = 0
        for piece in qkv_refs:
            size = piece.shape[0]
            store(at, size, dot_back(qkv_grad_ref[pl.ds(start, half_rows), :], piece[...]))
            at += size

    def store_first(at, size, value):
        first_ref[:, at : at + size] = value.astype(BF16)

    def store_second(at, size, value):
        second_ref[:, at : at + size] = value

    back_project(theirs, store_first)
    first_copy.start()
    back_project(mine, store_second)
    pump(3, 5)
    first_copy.wait_recv()
    chip_ref[...] = (second_ref[...] + core_land[...].astype(F32)).astype(BF16)
    y_copy.start()
    pump(5, 6)
    send_next(4, 5)

    def piece_copy(slot, k):
        return pltpu.make_async_copy(piece_buf.at[slot], pool_ref.at[k], piece_sem.at[slot])

    def put(first, values):
        for at, make in enumerate(values):
            slot = at % 2
            if at >= 2:
                piece_copy(slot, first + at - 2).wait()
            piece_buf[slot] = make()
            piece_copy(slot, first + at).start()
        for at in range(max(0, len(values) - 2), len(values)):
            piece_copy(at % 2, first + at).wait()

    def outer(left, left_other, right, right_other, block):
        columns = slice(block * CHUNK_ROWS, (block + 1) * CHUNK_ROWS)
        return (
            dot_outer(left[:, columns], right[...]) + dot_outer(left_other[:, columns], right_other[...])
        ).astype(BF16)

    def feed_pieces(rights, rights_other):
        return [
            functools.partial(outer, hidden_m_ref, hidden_m_land, right, right_other, block)
            for right, right_other in zip(rights, rights_other)
            for block in range(half // CHUNK_ROWS)
        ]

    for copy in gate_copies + [hidden_m_copy]:
        copy.wait_recv()
    put(starts[1], feed_pieces(gate_refs, gate_land))
    pump(6, 7)

    y_copy.wait_recv()
    total_ref[...] = (chip_ref[...].astype(F32) + y_land[...].astype(F32)).astype(BF16)
    total_copy.start()
    gain = gain_ref[...]
    near_at = pl.multiple_of((1 - shard) * half + lax.rem(ctx, 2) * part, part)
    far_at = pl.multiple_of((1 - shard) * half + (1 - lax.rem(ctx, 2)) * part, part)
    own_at = pl.multiple_of(shard * half, half)
    step_rows = 64

    def norm_rows(source, base):
        def body(step, total):
            at = pl.multiple_of(step * step_rows, step_rows)
            here = pl.ds(pl.multiple_of(base + at, step_rows), step_rows)
            scale = scale_ref[here, :]
            normed = inputs_ref[here, :].astype(F32) * scale
            hidden = source[pl.ds(at, step_rows), :].astype(F32)
            grad = hidden * gain
            mean = jnp.sum(grad * normed, axis=-1, keepdims=True) * (1.0 / width)
            value = (grad_middle_ref[here, :] + scale * (grad - normed * mean)).astype(BF16)
            grad_ref[here, pl.ds(own_at, half)] = value[:, :half]
            grad_ref[here, pl.ds(near_at, part)] = value[:, half : half + part]
            grad_ref[here, pl.ds(far_at, part)] = value[:, half + part :]
            return total + jnp.sum(hidden * normed, axis=0, keepdims=True)

        return lax.fori_loop(0, half_rows // step_rows, body, jnp.zeros((1, width), F32))

    gain_sum = norm_rows(total_ref, mine)
    pump(7, 8)
    send_next(5, 6)
    total_copy.wait_recv()
    gain_out_ref[...] = gain_sum + norm_rows(other_ref, theirs)
    pump(8, 10)
    send_next(6, 7)
    for copy in up_copies:
        copy.wait_recv()
    put(starts[2], feed_pieces(up_refs, up_land))
    pump(10, 12)
    send_next(7, 8)
    pump(12, 14)
    send_next(8, len(queue))
    branch_copy.wait_recv()
    mixed_copy.wait_recv()
    put(
        starts[3],
        [
            functools.partial(
                outer, mixed_ref, mixed_land, branch_ref.at[:, :half], branch_land, block
            )
            for block in range(q_width // CHUNK_ROWS)
        ],
    )
    pump(14, 17)
    hidden_a_copy.wait_recv()
    qkv_copy.wait_recv()

    def side_by_side(first, number, columns):
        return jnp.concatenate(
            [
                outer(
                    hidden_a_ref, hidden_a_land, qkv_grad_ref.at[:, columns],
                    qkv_land.at[:, columns], block,
                )
                for block in range(first, first + number)
            ],
            axis=1,
        )

    q_blocks = CHUNK_COLUMNS // q_width
    put(
        starts[4],
        [
            functools.partial(side_by_side, first, q_blocks, slice(0, q_width))
            for first in range(0, half // CHUNK_ROWS, q_blocks)
        ]
        + [
            functools.partial(
                side_by_side, 0, half // CHUNK_ROWS, slice(q_width, q_width + 2 * kv_width)
            )
        ],
    )
    pump(17, count + lag)

    for copy in queue[-2:] + [first_copy, y_copy, total_copy]:
        copy.wait_send()
    for back in (1, 2):

        @pl.when(ctx >= back)
        def _():
            kv_copy(back).wait_send()

    @pl.when(is_middle)
    def _():
        for k in (count - 2, count - 1):
            outward_copy(jnp.int32(k)).wait_send()
            keep_copy(jnp.int32(k)).wait()

    @pl.when(is_end)
    def _():
        def close(k, carry):
            to_pair(pool_ref.at[k], sum_ref, k).wait_recv()
            return carry

        lax.fori_loop(0, count, close, 0)


def flat_call(body, groups, **call):
    flat, tree = jax.tree.flatten(groups, is_leaf=lambda x: isinstance(x, tuple) and len(x) == 2 and isinstance(x[1], pl.BlockSpec))
    arrays, specs = [x[0] for x in flat], [x[1] for x in flat]

    def unflatten(*refs):
        body(*jax.tree.unflatten(tree, refs[: len(flat)]), *refs[len(flat) :])

    return pl.pallas_call(unflatten, in_specs=specs, **call)(*arrays)


def tail(plan, pool, v):
    heads, group, lead, ready, starts, count = plan
    rows, width = v["inputs"].shape
    half = width // 2
    q_width, kv_width = v["query"].shape[1], v["keys_values"].shape[1] // 2
    qkv_width = q_width + 2 * kv_width
    piece = (CHUNK_ROWS, CHUNK_COLUMNS)
    cuts, feed_part = len(v["grad_gate"]), v["grad_gate"][0].shape[1]

    def near(value):
        return (value, pl.BlockSpec(memory_space=pltpu.VMEM))

    def far(value):
        return (value, pl.BlockSpec(memory_space=pl.ANY))

    operands = [
        far(pool),
        [near(value) for value in v["grad_gate"]],
        [near(value) for value in v["grad_up"]],
        near(v["hidden_m"]), far(v["hidden_m_send"]),
        near(v["hidden_a"]), far(v["hidden_a_send"]),
        near(v["branch"]), far(v["branch_send"]),
        near(v["mixed"]),
        [near(value) for value in v["out_pieces"]],
        near(v["query"]), near(v["keys_values"]), near(v["log_sums"]),
        near(v["query_segments"]), near(v["key_segments"]),
        near(v["cosine"]), near(v["sine"]),
        [near(value) for value in v["qkv_pieces"]],
        near(v["inputs"]), near(v["scale"]), near(v["gain"]), near(v["grad_middle"]),
    ]
    any_space, vmem_space = pl.BlockSpec(memory_space=pl.ANY), pl.BlockSpec(memory_space=pltpu.VMEM)
    line = jax.ShapeDtypeStruct((count,) + piece, BF16)
    dma = pltpu.SemaphoreType.DMA
    low = lambda *shape: pltpu.VMEM(shape, BF16)
    wide = lambda *shape: pltpu.VMEM(shape, F32)
    scratch = [
        [low(rows, feed_part) for _ in range(cuts)],
        [low(rows, feed_part) for _ in range(cuts)],
        low(rows, half), low(rows, half), low(rows, half),
        low(rows, q_width), low(rows, qkv_width),
        low(rows, q_width), wide(rows, q_width), wide(3 * rows, 2 * kv_width),
        low(2, rows, 2 * kv_width), low(2, rows, 2 * kv_width), low(rows, qkv_width),
        low(rows // 2, width), wide(rows // 2, width), low(rows // 2, width),
        low(rows // 2, width), low(rows // 2, width), low(rows // 2, width),
        low(rows // 2, width),
        low(*piece), low(*piece), low(4, *piece), low(*piece), low(2, *piece), low(2, *piece),
        dma((2 * cuts + 5,)), dma((2 * cuts + 5,)), dma((3,)), dma((3,)), dma((2,)), dma((2,)),
        dma((count,)), dma((count,)), dma((count,)), dma((count,)), dma((count,)),
        dma((3,)), dma((2,)),
    ]
    outs = flat_call(
        functools.partial(tail_body, plan),
        operands,
        out_specs=[any_space, any_space, any_space, any_space, vmem_space, vmem_space],
        out_shape=[
            line, line, line, line,
            jax.ShapeDtypeStruct((rows, width), BF16),
            jax.ShapeDtypeStruct((1, width), F32),
        ],
        scratch_shapes=scratch,
        input_output_aliases={0: 0},
        compiler_params=pltpu.CompilerParams(
            collective_id=0, has_side_effects=True, vmem_limit_bytes=60 << 20
        ),
        cost_estimate=pl.CostEstimate(
            flops=400 << 30, bytes_accessed=30 << 20, transcendentals=0
        ),
        name="tail",
    )
    return outs[1], outs[4], outs[5]


def swap(value, axis, size, bit):
    return lax.ppermute(value, axis, [(i, i ^ bit) for i in range(size)])


def shift(value, axis, size, by):
    if abs(by) >= size:
        return jnp.zeros_like(value)
    return lax.ppermute(
        value, axis, [(i, i + by) for i in range(size) if 0 <= i + by < size]
    )


class Lane:
    def __init__(self, move, depth=2):
        self.move, self.depth, self.done = move, depth, []

    def send(self, value):
        if len(self.done) >= self.depth:
            value, self.done[-self.depth] = tie(value, self.done[-self.depth])
        self.done.append(self.move(value))
        return len(self.done) - 1

    def get(self, at):
        return self.done[at]


def shards(
    sizes,
    block_input,
    segment_ids,
    attention_gain,
    query_weight,
    key_weight,
    value_weight,
    out_weight,
    feed_gain,
    gate_weight,
    up_weight,
    down_weight,
    cotangent,
):
    shard_count, ctx_count, tp_count = sizes
    seqs, span, width = block_input.shape
    rows = seqs * span
    seq_length = segment_ids.shape[1]
    half = width // 2
    part = half // 2
    q_width = query_weight.shape[1]
    kv_width = key_weight.shape[1]
    feed_width = gate_weight.shape[1]
    group = q_width // kv_width
    shard, ctx, tp = (lax.axis_index(name) for name in ("fsdp", "ctx", "tp"))
    odd = ctx % 2
    sibling = tp % 2

    own_at = shard * half
    near_at = (1 - shard) * half + odd * part
    far_at = (1 - shard) * half + (1 - odd) * part

    def to_local(value):
        return jnp.concatenate(
            [
                take(value, own_at, half, 1),
                take(value, near_at, part, 1),
                take(value, far_at, part, 1),
            ],
            axis=1,
        )

    def other_half(value):
        return jnp.concatenate(
            [
                take(value, half + odd * part, part, 1),
                take(value, half + (1 - odd) * part, part, 1),
            ],
            axis=1,
        )

    def from_local(value):
        own, other = value[:, :half], other_half(value)
        return jnp.where(
            shard == 0,
            jnp.concatenate([own, other], axis=1),
            jnp.concatenate([other, own], axis=1),
        )

    fsdp_lane = Lane(lambda value: swap(value, "fsdp", shard_count, 1))

    def over_fsdp(value):
        return swap(value, "fsdp", shard_count, 1)

    def over_ctx(value):
        return swap(value, "ctx", ctx_count, 1)

    def near_part(weight, axis):
        return take(weight, odd * part, part, axis)

    def core_half(value):
        return take(value, sibling * (rows // 2), rows // 2, 0)

    def join_cores(mine):
        other = swap(mine, "tp", tp_count, 1)
        return jnp.where(
            sibling == 0,
            jnp.concatenate([mine, other], axis=0),
            jnp.concatenate([other, mine], axis=0),
        )

    def chip_sum(first, second):
        return (second + swap(first, "tp", tp_count, 1).astype(F32)).astype(BF16)

    def finish_sum(chip):
        total = (chip.astype(F32) + swap(chip, "tp", tp_count, 2).astype(F32)).astype(BF16)
        return join_cores(total).astype(F32)

    def tp_sum(first, second):
        if tp_count != 4:
            whole_rows = jnp.where(
                sibling == 0,
                jnp.concatenate([second, first.astype(F32)], axis=0),
                jnp.concatenate([first.astype(F32), second], axis=0),
            )
            return lax.psum(whole_rows, "tp")
        return finish_sum(chip_sum(first, second))

    gains_own = jnp.stack([attention_gain, feed_gain])
    qkv_own = jnp.concatenate([query_weight, key_weight, value_weight], axis=1)
    feed_cuts = 2
    feed_part = feed_width // feed_cuts
    columns = [slice(cut * feed_part, (cut + 1) * feed_part) for cut in range(feed_cuts)]
    grad_rows = to_local(cotangent.reshape(rows, width))
    send_gate = [near_part(gate_weight[:, cut], 0) for cut in columns]
    send_up = [near_part(up_weight[:, cut], 0) for cut in columns]
    send_down = [near_part(down_weight[cut], 1) for cut in columns]
    send_grad = core_half(other_half(grad_rows))

    gains_other = over_fsdp(gains_own)
    near_qkv = over_fsdp(near_part(qkv_own, 0))
    near_out = over_fsdp(near_part(out_weight, 1))

    span_start = ctx * span
    positions = take(doc_positions(segment_ids), span_start, span, 1).reshape(rows)
    query_segments = take(segment_ids, span_start, span, 1)
    cosine, sine = rope_tables(positions)
    blocks_back, base, lead = attention_plan(span, WINDOW)
    key_segments = take(
        jnp.pad(segment_ids, ((0, 0), (blocks_back * span, 0)), constant_values=-1),
        span_start,
        (blocks_back + 1) * span,
        1,
    )

    inputs = to_local(block_input.reshape(rows, width)).astype(F32)
    scale_a = row_scale_of(inputs)
    normed_a = inputs * scale_a
    gains = jnp.concatenate(
        [gains_own, take(gains_other, odd * part, part, 1), take(gains_other, (1 - odd) * part, part, 1)],
        axis=1,
    ).astype(F32)
    gain_a, gain_m = gains[0:1], gains[1:2]
    hidden_a = (normed_a * gain_a).astype(BF16)

    near_qkv, send_gate[0] = tie(near_qkv, send_gate[0])
    near_gate, near_up, far_gate, far_up = ([None] * feed_cuts for _ in range(4))
    near_gate[0] = over_fsdp(send_gate[0])
    far_qkv = over_ctx(near_qkv)
    near_out, send_up[0] = tie(near_out, send_up[0])
    near_up[0] = over_fsdp(send_up[0])
    far_qkv, near_out = tie(far_qkv, near_out)
    far_out = over_ctx(near_out)

    def dot_pieces(matrix, own, near, far):
        return (
            dot_rows(matrix[:, :half], own)
            + dot_rows(matrix[:, half : half + part], near)
            + dot_rows(matrix[:, half + part :], far)
        )

    def back_pieces(matrix, own, near, far):
        return jnp.concatenate(
            [dot_back(matrix, own), dot_back(matrix, near), dot_back(matrix, far)], axis=1
        )

    qkv = dot_pieces(hidden_a, qkv_own, near_qkv, far_qkv)
    key_low = rotate(qkv[:, q_width : q_width + kv_width], cosine, sine).astype(BF16)
    value_low = qkv[:, q_width + kv_width :].astype(BF16)
    keys_values = jnp.concatenate([key_low, value_low], axis=1).reshape(seqs, span, 2 * kv_width)
    query_low = (rotate(qkv[:, :q_width], cosine, sine).astype(BF16) * HD**-0.5).reshape(
        seqs, span, q_width
    )
    earlier = [shift(keys_values, "ctx", ctx_count, back) for back in range(blocks_back, 0, -1)]
    *earlier, near_gate[0], far_out, query_low, send_gate[1] = tie(
        *earlier, near_gate[0], far_out, query_low, send_gate[1]
    )
    near_gate[1] = over_fsdp(send_gate[1])
    far_gate[0] = over_ctx(near_gate[0])
    keys_values = jnp.concatenate(earlier + [keys_values], axis=1)
    mixed, log_sums = attend_forward(
        query_low, keys_values, query_segments, key_segments, base, lead, group
    )
    mixed_low = mixed.reshape(rows, q_width)
    mixed_low, near_up[0], send_up[1] = tie(mixed_low, near_up[0], send_up[1])
    near_up[1] = over_fsdp(send_up[1])
    far_up[0] = over_ctx(near_up[0])

    def out_project(at):
        matrix = take(mixed_low, at * (rows // 2), rows // 2, 0)
        return jnp.concatenate(
            [dot_rows(matrix, out_weight), dot_rows(matrix, near_out), dot_rows(matrix, far_out)],
            axis=1,
        )

    first, second = out_project(1 - sibling).astype(BF16), out_project(sibling)
    if tp_count == 4:
        chip = chip_sum(first, second)
        chip, near_gate[1], far_gate[0], send_down[0] = tie(
            chip, near_gate[1], far_gate[0], send_down[0]
        )
        near_down = [over_fsdp(send_down[0])]
        far_gate[1] = over_ctx(near_gate[1])
        total = (chip.astype(F32) + swap(chip, "tp", tp_count, 2).astype(F32)).astype(BF16)
        total, near_up[1], far_up[0], send_down[1] = tie(
            total, near_up[1], far_up[0], send_down[1]
        )
        near_down.append(over_fsdp(send_down[1]))
        far_up[1] = over_ctx(near_up[1])
        branch_a = join_cores(total).astype(F32)
    else:
        branch_a = tp_sum(first, second)
        near_down = [over_fsdp(value) for value in send_down]
        far_gate[1] = over_ctx(near_gate[1])
        far_up[1] = over_ctx(near_up[1])
    middle = inputs + branch_a

    scale_m = row_scale_of(middle)
    normed_m = middle * scale_m
    hidden_m = (normed_m * gain_m).astype(BF16)
    gate_cuts, up_cuts, act_cuts = [], [], []
    for cut in range(feed_cuts):
        gate_value, up_value, activated = feed_forward(
            hidden_m,
            (gate_weight, near_gate[cut], far_gate[cut]),
            (up_weight, near_up[cut], far_up[cut]),
            cut,
            feed_part,
        )
        gate_cuts.append(gate_value)
        up_cuts.append(up_value)
        act_cuts.append(activated)
    act_cuts[0], near_down[0], send_grad = tie(act_cuts[0], near_down[0], send_grad)
    other_grad = over_fsdp(send_grad)
    far_down = [over_ctx(near_down[0])]
    act_other = [over_fsdp(act_cuts[0])]
    act_cuts[1], near_down[1] = tie(act_cuts[1], near_down[1])
    act_other.append(over_fsdp(act_cuts[1]))
    far_down.append(over_ctx(near_down[1]))
    grad_own, grad_other = grad_rows[:, :half], join_cores(other_grad)
    fsdp_lane.done = list(act_other)

    pieces = CHUNK_ROWS * CHUNK_COLUMNS
    down_count = feed_width * half // pieces
    starts, pool_size = [], 0
    for size in (feed_width * half,) * 3 + (q_width * half,) * 2 + (2 * kv_width * half,):
        starts.append(pool_size)
        pool_size += size // pieces
    pool = None
    for cut in range(feed_cuts):
        pool = outer_sum(
            pool,
            cut * down_count // feed_cuts,
            pool_size,
            act_cuts[cut],
            act_other[cut],
            [grad_own],
            [grad_other],
        )

    grad_gate_cuts, grad_up_cuts = [], []
    for cut in range(feed_cuts):
        grad_gate, grad_up = feed_backward(
            grad_rows,
            (down_weight, near_down[cut], far_down[cut]),
            gate_cuts[cut],
            up_cuts[cut],
            cut,
        )
        grad_gate_cuts.append(grad_gate)
        grad_up_cuts.append(grad_up)

    grad_hidden_m = tp_sum(
        *project(
            sibling,
            list(zip(grad_gate_cuts, grad_up_cuts)),
            [
                (
                    (gate_weight, near_gate[cut], far_gate[cut]),
                    (up_weight, near_up[cut], far_up[cut]),
                )
                for cut in range(feed_cuts)
            ],
            width,
            True,
        )
    )
    feed_gain_part = jnp.sum(grad_hidden_m * normed_m, axis=0)
    grad_middle = norm_back(grad_hidden_m, gain_m, normed_m, scale_m, grad_rows.astype(F32))
    grad_branch = grad_middle.astype(BF16)

    branch_m = tp_sum(
        *project(
            sibling,
            [(value,) for value in act_cuts],
            [((down_weight, near_down[cut], far_down[cut]),) for cut in range(feed_cuts)],
            width,
            False,
        )
    )
    block_out = from_local((middle + branch_m).astype(BF16)).reshape(seqs, span, width)

    fused = (shard_count, ctx_count, tp_count) == (2, 4, 4)
    fused = fused and seqs == 1 and (blocks_back, base) == (2, 0)
    if fused:
        tile = min(LANES, rows)
        log_rows = jnp.swapaxes(log_sums[0, :, : q_width // HD].reshape(rows // tile, tile, -1), 1, 2)
        pool, input_grad, gain_row = tail(
            (
                q_width // HD,
                group,
                lead,
                starts[1],
                tuple(starts),
                pool_size,
            ),
            pool,
            {
                "grad_gate": grad_gate_cuts,
                "grad_up": grad_up_cuts,
                "hidden_m": hidden_m[:, :half],
                "hidden_m_send": other_half(hidden_m),
                "hidden_a": hidden_a[:, :half],
                "hidden_a_send": other_half(hidden_a),
                "branch": grad_branch,
                "branch_send": other_half(grad_branch),
                "mixed": mixed_low,
                "out_pieces": [out_weight, near_out, far_out],
                "query": query_low[0],
                "keys_values": keys_values[0],
                "log_sums": log_rows,
                "query_segments": query_segments.reshape(rows // tile, 1, tile),
                "key_segments": key_segments.reshape(-1, 1),
                "cosine": cosine,
                "sine": sine,
                "qkv_pieces": [qkv_own, near_qkv, far_qkv],
                "inputs": inputs.astype(BF16),
                "scale": scale_a,
                "gain": gain_a,
                "grad_middle": grad_middle,
            },
        )
        attention_gain_part = gain_row[0]
        input_grad = input_grad.reshape(seqs, span, width)
    else:
        gate_at = [fsdp_lane.send(value) for value in grad_gate_cuts]
        up_at = [fsdp_lane.send(value) for value in grad_up_cuts]
        hidden_m_at = fsdp_lane.send(core_half(other_half(hidden_m)))
        hidden_own, hidden_other = hidden_m[:, :half], join_cores(fsdp_lane.get(hidden_m_at))
        for which, (own, at) in enumerate(((grad_gate_cuts, gate_at), (grad_up_cuts, up_at))):
            pool = outer_sum(
                pool,
                starts[1 + which],
                pool_size,
                hidden_own,
                hidden_other,
                own,
                [fsdp_lane.get(i) for i in at],
            )

        grad_mixed = (
            dot_back(grad_branch[:, :half], out_weight)
            + dot_back(grad_branch[:, half : half + part], near_out)
            + dot_back(grad_branch[:, half + part :], far_out)
        ).astype(BF16)
        branch_at = fsdp_lane.send(core_half(other_half(grad_branch)))
        mixed_at = fsdp_lane.send(mixed_low)
        hidden_a_at = fsdp_lane.send(core_half(other_half(hidden_a)))
        grad_query, grad_keys_values = attend_backward(
            query_low,
            keys_values,
            grad_mixed.reshape(seqs, span, q_width),
            jnp.swapaxes(log_sums, 1, 2)[:, : q_width // HD],
            query_segments,
            key_segments,
            base,
            lead,
            group,
        )
        kv_sum = grad_keys_values[:, blocks_back * span :]
        for back in range(1, blocks_back + 1):
            at = (blocks_back - back) * span
            kv_sum = kv_sum + shift(
                grad_keys_values[:, at : at + span].astype(BF16), "ctx", ctx_count, -back
            ).astype(F32)
        kv_sum = kv_sum.reshape(rows, 2 * kv_width)
        grad_qkv = jnp.concatenate(
            [
                rotate(grad_query.reshape(rows, q_width), cosine, -sine),
                rotate(kv_sum[:, :kv_width], cosine, -sine),
                kv_sum[:, kv_width:],
            ],
            axis=1,
        ).astype(BF16)
        qkv_at = fsdp_lane.send(grad_qkv)
        first, second = (
            back_pieces(take(grad_qkv, at * (rows // 2), rows // 2, 0), qkv_own, near_qkv, far_qkv)
            for at in (1 - sibling, sibling)
        )
        grad_hidden_a = tp_sum(first.astype(BF16), second)
        attention_gain_part = jnp.sum(grad_hidden_a * normed_a, axis=0)
        input_grad = norm_back(grad_hidden_a, gain_a, normed_a, scale_a, grad_middle)
        input_grad = from_local(input_grad.astype(BF16)).reshape(seqs, span, width)

        pool = outer_sum(
            pool,
            starts[3],
            pool_size,
            mixed_low,
            fsdp_lane.get(mixed_at),
            [grad_branch[:, :half]],
            [join_cores(fsdp_lane.get(branch_at))],
        )
        qkv_other = fsdp_lane.get(qkv_at)
        hidden_own, hidden_other = hidden_a[:, :half], join_cores(fsdp_lane.get(hidden_a_at))
        for which, cut in ((4, slice(0, q_width)), (5, slice(q_width, None))):
            pool = outer_sum(
                pool,
                starts[which],
                pool_size,
                hidden_own,
                hidden_other,
                [grad_qkv[:, cut]],
                [qkv_other[:, cut]],
            )
        pool = lax.psum(pool.astype(F32), "ctx")

    gain_parts = jnp.stack([attention_gain_part, feed_gain_part])
    gain_other = over_fsdp(other_half(gain_parts))
    gain_sums = lax.psum(gain_parts[:, :half] + gain_other, "ctx")

    down_grad, gate_grad, up_grad, out_grad, query_grad, key_grad, value_grad = widen(
        pool,
        starts,
        [
            down_weight.shape,
            gate_weight.shape,
            up_weight.shape,
            out_weight.shape,
            query_weight.shape,
            key_weight.shape,
            value_weight.shape,
        ],
    )
    return (
        block_out,
        input_grad,
        gain_sums[0],
        query_grad,
        key_grad,
        value_grad,
        out_grad,
        gain_sums[1],
        gate_grad,
        up_grad,
        down_grad,
    )


def solution(mesh):
    sizes = tuple(mesh.shape[name] for name in ("fsdp", "ctx", "tp"))
    in_specs = (
        P("fsdp", "ctx", None),
        P("fsdp", None),
        P("fsdp"),
        P("fsdp", "tp"),
        P("fsdp", "tp"),
        P("fsdp", "tp"),
        P("tp", "fsdp"),
        P("fsdp"),
        P("fsdp", "tp"),
        P("fsdp", "tp"),
        P("tp", "fsdp"),
        P("fsdp", "ctx", None),
    )
    out_specs = (
        P("fsdp", "ctx", None),
        P("fsdp", "ctx", None),
        P("fsdp"),
        P("fsdp", "tp"),
        P("fsdp", "tp"),
        P("fsdp", "tp"),
        P("tp", "fsdp"),
        P("fsdp"),
        P("fsdp", "tp"),
        P("fsdp", "tp"),
        P("tp", "fsdp"),
    )
    return jax.shard_map(
        functools.partial(shards, sizes),
        mesh=mesh,
        in_specs=in_specs,
        out_specs=out_specs,
        check_vma=False,
    )
```

```python
import functools

import jax
import jax.numpy as jnp
from jax import lax
from jax.experimental import pallas as pl
from jax.experimental.pallas import tpu as pltpu
from jax.sharding import PartitionSpec as P

HD = 64
WINDOW = 1024
NORM_EPS = 1e-05
ROPE_BASE = 500000.0
MASK_FILL = -1e30
LANES = 128
F32 = jnp.float32
BF16 = jnp.bfloat16


def dot_rows(matrix, other_side):
    return jnp.dot(matrix, other_side, preferred_element_type=F32)


def dot_back(matrix, other_side):
    return lax.dot_general(matrix, other_side, (((1,), (1,)), ((), ())), preferred_element_type=F32)


def dot_outer(matrix, other_side):
    return lax.dot_general(matrix, other_side, (((0,), (0,)), ((), ())), preferred_element_type=F32)


def tie(*values):
    return lax.optimization_barrier(values)


def take(array, start, size, axis):
    return lax.dynamic_slice_in_dim(array, start, size, axis)


def doc_positions(segments):
    seq_count, seq_length = segments.shape
    index_grid = jnp.broadcast_to(jnp.arange(seq_length, dtype=jnp.int32)[None, :], segments.shape)
    begins = jnp.concatenate(
        [jnp.ones((seq_count, 1), dtype=bool), segments[:, 1:] != segments[:, :-1]], axis=1
    )
    return index_grid - lax.cummax(jnp.where(begins, index_grid, 0), axis=1)


def rope_tables(positions):
    half_size = HD // 2
    frequency = ROPE_BASE ** (-(jnp.arange(half_size, dtype=F32) * 2.0 / HD))
    angles = positions.astype(F32)[:, None] * frequency
    cosine, sine = jnp.cos(angles), jnp.sin(angles)
    return jnp.concatenate([cosine] * 4, axis=1), jnp.concatenate([-sine, sine] * 2, axis=1)


def rotate(vectors, cosine, signed_sine):
    width = vectors.shape[1]
    half = HD // 2
    ahead = jnp.concatenate([vectors[:, half:], vectors[:, :half]], axis=1)
    behind = jnp.concatenate([vectors[:, -half:], vectors[:, :-half]], axis=1)
    first = (jnp.arange(width) % HD < half)[None, :]
    reps = width // LANES
    return vectors * jnp.tile(cosine, (1, reps)) + jnp.where(first, ahead, behind) * jnp.tile(
        signed_sine, (1, reps)
    )


def row_scale_of(values):
    return lax.rsqrt(jnp.mean(values * values, axis=-1, keepdims=True) + NORM_EPS)


def norm_back(grad_hidden, gain, normed, row_scale, residual_grad):
    grad_normed = grad_hidden * gain
    return residual_grad + row_scale * (
        grad_normed - normed * jnp.mean(grad_normed * normed, axis=-1, keepdims=True)
    )


def attend_forward_body(lead, heads, group, q_ref, kv_ref, qseg_ref, kseg_ref, mixed_ref, lse_ref):
    block = q_ref.shape[1]
    reach = kseg_ref.shape[-1]
    start = pl.multiple_of(pl.program_id(1) * block, block)
    window = kv_ref.at[0, pl.ds(start, reach), :]
    distance = (
        lax.broadcasted_iota(jnp.int32, (block, reach), 0)
        + lead
        - lax.broadcasted_iota(jnp.int32, (block, reach), 1)
    )
    allowed = (qseg_ref[0] == kseg_ref[0, 0]) & (distance >= 0) & (distance < WINDOW)
    bias = jnp.where(allowed, 0.0, MASK_FILL)
    lane = lax.broadcasted_iota(jnp.int32, (block, LANES), 1)
    log_sums = jnp.zeros((block, LANES), F32)
    kv_width = heads // group * HD
    outs = []
    for head in range(heads):
        shared = head // group * HD
        keys = window[:, shared : shared + HD]
        values = window[:, kv_width + shared : kv_width + shared + HD]
        scores = dot_back(q_ref[0, :, head * HD : (head + 1) * HD], keys) + bias
        row_max = jnp.max(scores, axis=-1, keepdims=True)
        exponent = jnp.exp(scores - row_max)
        row_total = jnp.sum(exponent, axis=-1, keepdims=True)
        probs = (exponent * (1.0 / row_total)).astype(BF16)
        outs.append(dot_rows(probs, values))
        log_sums = jnp.where(lane == head, row_max + jnp.log(row_total), log_sums)
    mixed_ref[0] = jnp.concatenate(outs, axis=1).astype(BF16)
    lse_ref[0] = log_sums


def attend_backward_body(
    lead, heads, group, q_ref, kv_ref, grad_ref, lse_ref, qseg_ref, kseg_ref, dq_ref, dkv_ref
):
    block = q_ref.shape[1]
    reach = block + lead
    step = pl.program_id(1)
    start = pl.multiple_of(step * block, block)
    window = kv_ref.at[0, pl.ds(start, reach), :]

    @pl.when(step == 0)
    def _():
        dkv_ref[...] = jnp.zeros_like(dkv_ref)

    distance = (
        lax.broadcasted_iota(jnp.int32, (reach, block), 1)
        + lead
        - lax.broadcasted_iota(jnp.int32, (reach, block), 0)
    )
    same = kseg_ref[0, pl.ds(start, reach), :] == qseg_ref[0]
    bias = jnp.where(same & (distance >= 0) & (distance < WINDOW), 0.0, MASK_FILL)
    query_grad, keys_grad = backward_tile(
        heads,
        group,
        lambda head: q_ref[0, :, head * HD : (head + 1) * HD],
        lambda head: grad_ref[0, :, head * HD : (head + 1) * HD],
        lambda head: lse_ref[0, head : head + 1, :],
        lambda at: window[:, at * HD : (at + 1) * HD],
        bias,
    )
    dq_ref[0] = query_grad
    dkv_ref[0, pl.ds(start, reach), :] += keys_grad


def backward_tile(heads, group, query_of, grad_of, log_sum_of, window_of, bias):
    key_grads, value_grads, query_grads = [], [], []
    shared_heads = heads // group
    for shared in range(shared_heads):
        keys, values = window_of(shared), window_of(shared_heads + shared)
        key_sum = value_sum = None
        for member in range(group):
            head = shared * group + member
            query, grad = query_of(head), grad_of(head)
            probs = jnp.exp(dot_back(keys, query) + bias - log_sum_of(head))
            grad_probs = dot_back(values, grad)
            spread = jnp.sum(probs * grad_probs, axis=0, keepdims=True)
            grad_scores = (probs * (grad_probs - spread)).astype(BF16)
            value_part = dot_rows(probs.astype(BF16), grad)
            key_part = dot_rows(grad_scores, query)
            query_grads.append(dot_outer(grad_scores, keys) * HD**-0.5)
            value_sum = value_part if value_sum is None else value_sum + value_part
            key_sum = key_part if key_sum is None else key_sum + key_part
        key_grads.append(key_sum)
        value_grads.append(value_sum)
    return jnp.concatenate(query_grads, axis=1), jnp.concatenate(key_grads + value_grads, axis=1)


def attention_plan(span, window):
    blocks_back = -(-(window - 1) // span)
    base = (blocks_back * span - (window - 1)) // LANES * LANES
    return blocks_back, base, blocks_back * span - base


def key_tiles(key_segments, base, lead, block, span):
    return jnp.stack(
        [
            key_segments[:, base + at : base + at + block + lead]
            for at in range(0, span, block)
        ],
        axis=1,
    )[:, :, None, :]


def attend_forward(query, keys_values, query_segments, key_segments, base, lead, group):
    seqs, span, width = query.shape
    block = min(LANES, span)
    heads = width // HD
    reach = block + lead
    keys_used = keys_values[:, base:]
    return pl.pallas_call(
        functools.partial(attend_forward_body, lead, heads, group),
        grid=(seqs, span // block),
        in_specs=[
            pl.BlockSpec((1, block, width), lambda s, i: (s, i, 0)),
            pl.BlockSpec((1,) + keys_used.shape[1:], lambda s, i: (s, 0, 0)),
            pl.BlockSpec((1, block, 1), lambda s, i: (s, i, 0)),
            pl.BlockSpec((1, 1, 1, reach), lambda s, i: (s, i, 0, 0)),
        ],
        out_specs=[
            pl.BlockSpec((1, block, width), lambda s, i: (s, i, 0)),
            pl.BlockSpec((1, block, LANES), lambda s, i: (s, i, 0)),
        ],
        out_shape=[
            jax.ShapeDtypeStruct(query.shape, BF16),
            jax.ShapeDtypeStruct((seqs, span, LANES), F32),
        ],
        compiler_params=pltpu.CompilerParams(vmem_limit_bytes=40 << 20),
        cost_estimate=pl.CostEstimate(
            flops=70 * seqs * span * reach * width, bytes_accessed=4 << 20, transcendentals=0
        ),
        name="attend_forward",
    )(query, keys_used, query_segments[:, :, None], key_tiles(key_segments, base, lead, block, span))


def attend_backward(
    query, keys_values, grad_mixed, log_sums, query_segments, key_segments, base, lead, group
):
    seqs, span, width = query.shape
    block = min(LANES, span)
    heads = width // HD
    reach = block + lead
    keys_used = keys_values[:, base:]
    whole_keys = pl.BlockSpec((1,) + keys_used.shape[1:], lambda s, i: (s, 0, 0))
    rows = pl.BlockSpec((1, block, width), lambda s, i: (s, i, 0))
    grad_query, grad_keys_values = pl.pallas_call(
        functools.partial(attend_backward_body, lead, heads, group),
        grid=(seqs, span // block),
        in_specs=[
            rows,
            whole_keys,
            rows,
            pl.BlockSpec((1, heads, block), lambda s, i: (s, 0, i)),
            pl.BlockSpec((1, 1, block), lambda s, i: (s, 0, i)),
            pl.BlockSpec((1, keys_used.shape[1], 1), lambda s, i: (s, 0, 0)),
        ],
        out_specs=[rows, whole_keys],
        out_shape=[
            jax.ShapeDtypeStruct(query.shape, F32),
            jax.ShapeDtypeStruct(keys_used.shape, F32),
        ],
        compiler_params=pltpu.CompilerParams(vmem_limit_bytes=40 << 20),
        cost_estimate=pl.CostEstimate(
            flops=85 * seqs * span * reach * width, bytes_accessed=6 << 20, transcendentals=0
        ),
        name="attend_backward",
    )(
        query,
        keys_used,
        grad_mixed,
        log_sums,
        query_segments[:, None, :],
        key_segments[:, base:, None],
    )
    return grad_query, jnp.pad(grad_keys_values, ((0, 0), (base, 0), (0, 0)))


def whole(array):
    return pl.BlockSpec(array.shape, lambda *at: (0,) * array.ndim)


def kernel_cost(flops, moved):
    return pl.CostEstimate(flops=flops, bytes_accessed=moved, transcendentals=0)


def feed_forward_body(sizes, hidden_ref, *refs):
    count = len(sizes)
    gate_refs, up_refs = refs[:count], refs[count : 2 * count]
    gate_ref, up_ref, act_ref = refs[2 * count :]

    def project(pieces):
        total, at = None, 0
        for size, piece in zip(sizes, pieces):
            value = dot_rows(hidden_ref[:, at : at + size], piece[...])
            total = value if total is None else total + value
            at += size
        return total

    gate_value, up_value = project(gate_refs), project(up_refs)
    gate_ref[...] = gate_value
    up_ref[...] = up_value
    act_ref[...] = (gate_value * jax.nn.sigmoid(gate_value) * up_value).astype(BF16)


def feed_forward(hidden, gate_pieces, up_pieces, cut, columns):
    rows = hidden.shape[0]
    tile = min(512, columns)
    steps = columns // tile
    own = lambda w: pl.BlockSpec((w.shape[0], tile), lambda i: (0, cut * steps + i))
    rest = lambda w: pl.BlockSpec((w.shape[0], tile), lambda i: (0, i))
    specs = [own(gate_pieces[0])] + [rest(w) for w in gate_pieces[1:]]
    out = pl.BlockSpec((rows, tile), lambda i: (0, i))
    return pl.pallas_call(
        functools.partial(feed_forward_body, tuple(w.shape[0] for w in gate_pieces)),
        grid=(steps,),
        in_specs=[whole(hidden)] + specs + specs,
        out_specs=[out] * 3,
        out_shape=[
            jax.ShapeDtypeStruct((rows, columns), F32),
            jax.ShapeDtypeStruct((rows, columns), F32),
            jax.ShapeDtypeStruct((rows, columns), BF16),
        ],
        compiler_params=pltpu.CompilerParams(vmem_limit_bytes=40 << 20),
        cost_estimate=kernel_cost(6 * rows * columns * hidden.shape[1], 8 << 20),
        name="feed_forward",
    )(hidden, *gate_pieces, *up_pieces)


def feed_backward_body(sizes, grad_ref, *refs):
    count = len(sizes)
    gate_ref, up_ref, grad_gate_ref, grad_up_ref = refs[count:]
    grad_act, at = None, 0
    for size, piece in zip(sizes, refs[:count]):
        value = dot_back(grad_ref[:, at : at + size], piece[...])
        grad_act = value if grad_act is None else grad_act + value
        at += size
    gate_value = gate_ref[...]
    sigmoid_gate = jax.nn.sigmoid(gate_value)
    grad_up = grad_act * sigmoid_gate
    grad_gate_ref[...] = (
        grad_up * up_ref[...] * (1.0 + gate_value * (1.0 - sigmoid_gate))
    ).astype(BF16)
    grad_up_ref[...] = (grad_up * gate_value).astype(BF16)


def feed_backward(grad, down_pieces, gate_value, up_value, cut):
    rows, columns = gate_value.shape
    tile = min(512, columns)
    steps = columns // tile
    own = lambda w: pl.BlockSpec((tile, w.shape[1]), lambda i: (cut * steps + i, 0))
    rest = lambda w: pl.BlockSpec((tile, w.shape[1]), lambda i: (i, 0))
    out = pl.BlockSpec((rows, tile), lambda i: (0, i))
    return pl.pallas_call(
        functools.partial(feed_backward_body, tuple(w.shape[1] for w in down_pieces)),
        grid=(steps,),
        in_specs=[whole(grad), own(down_pieces[0])]
        + [rest(w) for w in down_pieces[1:]]
        + [out, out],
        out_specs=[out] * 2,
        out_shape=[jax.ShapeDtypeStruct((rows, columns), BF16)] * 2,
        compiler_params=pltpu.CompilerParams(vmem_limit_bytes=40 << 20),
        cost_estimate=kernel_cost(4 * rows * columns * grad.shape[1], 8 << 20),
        name="feed_backward",
    )(grad, *down_pieces, gate_value, up_value)


def project_body(cuts, steps, terms, pieces, transposed, sibling_ref, *refs):
    first_ref, second_ref, total_ref = refs[-3:]
    step = pl.program_id(0)
    lefts = refs[: cuts * terms]
    weights = refs[cuts * terms : -3]

    @pl.when(step == 0)
    def _():
        total_ref[...] = jnp.zeros_like(total_ref)

    for cut in range(cuts):

        @pl.when(step // steps == cut)
        def _():
            at = 0
            for piece in range(pieces):
                value = None
                for term in range(terms):
                    left = lefts[cut * terms + term][...]
                    weight = weights[(cut * terms + term) * pieces + piece][...]
                    part = dot_back(left, weight) if transposed else dot_rows(left, weight)
                    value = part if value is None else value + part
                total_ref[:, at : at + value.shape[1]] += value
                at += value.shape[1]

    @pl.when(step == cuts * steps - 1)
    def _():
        half = total_ref.shape[0] // 2
        mine = pl.multiple_of(sibling_ref[0] * half, half)
        theirs = pl.multiple_of((1 - sibling_ref[0]) * half, half)
        first_ref[...] = total_ref[pl.ds(theirs, half), :].astype(BF16)
        second_ref[...] = total_ref[pl.ds(mine, half), :]


def project(sibling, lefts, weights, width, transposed):
    cuts, terms, pieces = len(lefts), len(lefts[0]), len(weights[0][0])
    rows, columns = lefts[0][0].shape
    tile = min(512, columns)
    steps = columns // tile
    in_specs = [pl.BlockSpec(memory_space=pltpu.SMEM)]
    operands = []

    def clipped(cut):
        return lambda i: jnp.clip(i - cut * steps, 0, steps - 1)

    for cut in range(cuts):
        for left in lefts[cut]:
            in_specs.append(pl.BlockSpec((rows, tile), lambda i, f=clipped(cut): (0, f(i))))
            operands.append(left)
    for cut in range(cuts):
        for term in weights[cut]:
            for piece, weight in enumerate(term):
                offset = cut * steps if piece == 0 else 0
                if transposed:
                    spec = pl.BlockSpec(
                        (weight.shape[0], tile), lambda i, f=clipped(cut), o=offset: (0, o + f(i))
                    )
                else:
                    spec = pl.BlockSpec(
                        (tile, weight.shape[1]), lambda i, f=clipped(cut), o=offset: (o + f(i), 0)
                    )
                in_specs.append(spec)
                operands.append(weight)
    half_rows = jax.ShapeDtypeStruct((rows // 2, width), BF16)
    return pl.pallas_call(
        functools.partial(project_body, cuts, steps, terms, pieces, transposed),
        grid=(cuts * steps,),
        in_specs=in_specs,
        out_specs=[whole(half_rows)] * 2,
        out_shape=[half_rows, jax.ShapeDtypeStruct((rows // 2, width), F32)],
        scratch_shapes=[pltpu.VMEM((rows, width), F32)],
        compiler_params=pltpu.CompilerParams(vmem_limit_bytes=48 << 20),
        cost_estimate=kernel_cost(3 * terms * rows * columns * cuts * width, 16 << 20),
        name="project",
    )(sibling.reshape(1), *operands)


CHUNK_ROWS, CHUNK_COLUMNS = 256, 1024


def outer_sum_body(split, groups, left_ref, left_other_ref, *refs):
    out_ref = refs[-1]
    rights, others = refs[:groups], refs[groups : 2 * groups]
    blocks = left_ref.shape[1] // CHUNK_ROWS
    for group in range(groups):

        def emit():
            for block in range(blocks):
                rows = slice(block * CHUNK_ROWS, (block + 1) * CHUNK_ROWS)
                value = dot_outer(left_ref[:, rows], rights[group][...])
                value += dot_outer(left_other_ref[:, rows], others[group][...])
                width = value.shape[1]
                out_ref[0, :, block * width : (block + 1) * width] = value.astype(BF16)

        if groups == 1:
            emit()
        else:
            pl.when(pl.program_id(0) // split == group)(emit)


def outer_sum(pool, at, count, left, left_other, rights, rights_other):
    groups = len(rights)
    rows = left.shape[0]
    columns = CHUNK_ROWS * CHUNK_COLUMNS // rights[0].shape[1]
    split = left.shape[1] // columns
    left_spec = pl.BlockSpec((rows, columns), lambda i: (0, lax.rem(i, split)))
    operands = (left, left_other, *rights, *rights_other)
    in_specs = [left_spec] * 2 + [whole(value) for value in operands[2:]]
    aliases = {}
    if pool is not None:
        operands += (pool,)
        in_specs.append(pl.BlockSpec(memory_space=pl.ANY))
        aliases = {len(operands) - 1: 0}
    return pl.pallas_call(
        functools.partial(outer_sum_body, split, groups),
        grid=(split * groups,),
        in_specs=in_specs,
        out_specs=pl.BlockSpec((1, CHUNK_ROWS, CHUNK_COLUMNS), lambda i: (at + i, 0, 0)),
        out_shape=jax.ShapeDtypeStruct((count, CHUNK_ROWS, CHUNK_COLUMNS), BF16),
        input_output_aliases=aliases,
        compiler_params=pltpu.CompilerParams(vmem_limit_bytes=48 << 20),
        cost_estimate=kernel_cost(
            4 * split * groups * rows * CHUNK_ROWS * CHUNK_COLUMNS, 4 << 20
        ),
        name="outer_sum",
    )(*operands)


def widen_body(starts, pool_ref, *out_refs):
    step = pl.program_id(0)
    value = pool_ref[0].astype(F32)
    last = len(starts) - 1
    for at, start in enumerate(starts):
        stop = starts[at + 1] if at < last else pl.num_programs(0)

        @pl.when((step >= start) & (step < stop))
        def _():
            if at < last - 1:
                out_refs[at][...] = value
            elif at == last - 1:
                half = CHUNK_COLUMNS // 2
                out_refs[at][:CHUNK_ROWS] = value[:, :half]
                out_refs[at][CHUNK_ROWS:] = value[:, half:]
            else:
                width = out_refs[at].shape[1]
                for block in range(CHUNK_COLUMNS // (2 * width)):
                    rows = slice(block * CHUNK_ROWS, (block + 1) * CHUNK_ROWS)
                    left = 2 * block * width
                    out_refs[at][rows] = value[:, left : left + width]
                    out_refs[at + 1][rows] = value[:, left + width : left + 2 * width]


def widen(pool, starts, shapes):
    specs = []
    for at, shape in enumerate(shapes):
        which = min(at, len(starts) - 1)
        start = starts[which]
        stop = starts[which + 1] if which + 1 < len(starts) else pool.shape[0]
        size = stop - start
        block = (shape[0] * shape[1] // (size * CHUNK_COLUMNS), CHUNK_COLUMNS)
        if which == len(starts) - 1:
            block = shape
        elif which == len(starts) - 2:
            block = (2 * CHUNK_ROWS, shape[1])
        down = shape[0] // block[0]

        def place(i, start=start, size=size, down=down):
            k = jnp.clip(i - start, 0, size - 1)
            return lax.rem(k, down), k // down

        specs.append(pl.BlockSpec(block, place))
    return pl.pallas_call(
        functools.partial(widen_body, starts),
        grid=(pool.shape[0],),
        in_specs=[pl.BlockSpec((1, CHUNK_ROWS, CHUNK_COLUMNS), lambda i: (i, 0, 0))],
        out_specs=specs,
        out_shape=[jax.ShapeDtypeStruct(shape, F32) for shape in shapes],
        compiler_params=pltpu.CompilerParams(vmem_limit_bytes=48 << 20),
        cost_estimate=kernel_cost(1, 45 << 20),
        name="widen",
    )(pool)


def tail_body(plan, *refs):
    heads, group, lead, starts, count = plan
    (
        pool_in, hidden_m_send, hidden_a_send, branch_send, stored,
        pool_ref, sum_ref, near_ref, across_ref, grad_ref, gain_out_ref,
        gate_land, up_land, hidden_m_land, hidden_a_land, branch_land, mixed_land, qkv_land,
        grad_mixed_ref, dq_ref, dkv_ref, kv_send, kv_land, qkv_grad_ref,
        first_ref, second_ref, core_land, chip_ref, y_land, total_ref, other_ref,
        own_buf, near_buf, part_buf, across_buf, total_buf, piece_buf,
        x_send, x_recv, tp_send, tp_recv, kv_send_sem, kv_recv_sem,
        send_sem, land_sem, cross_send, cross_land, keep_sem, load_sem, piece_sem,
        loaded, loaded_sem,
    ) = refs
    (
        gate_refs, up_refs, hidden_m_ref, hidden_a_ref, branch_ref, mixed_ref, out_refs,
        query_ref, keys_ref, log_ref, query_seg_ref, key_seg_ref, cosine_ref, sine_ref,
        qkv_refs, inputs_ref, scale_ref, gain_ref, grad_middle_ref,
    ) = loaded
    stored_gate, stored_up, stored_mixed = stored[0], stored[1], stored[5]
    rows, width = inputs_ref.shape
    half, part = width // 2, width // 4
    half_rows = rows // 2
    mesh_id = pl.DeviceIdType.MESH
    shard, ctx, tp = (lax.axis_index(name) for name in ("fsdp", "ctx", "tp"))
    sibling = lax.rem(tp, 2)
    core = tp + 1 - 2 * sibling
    across_y = lax.rem(tp + 2, 4)
    partner = 1 - shard
    pair = ctx + 1 - 2 * lax.rem(ctx, 2)
    across = 3 - ctx
    is_end = (ctx == 0) | (ctx == 3)
    is_middle = jnp.logical_not(is_end)

    kv_land[...] = jnp.zeros_like(kv_land)
    dkv_ref[...] = jnp.zeros_like(dkv_ref)

    barrier = pltpu.get_barrier_semaphore()
    others = [{"fsdp": partner}, {"tp": core}, {"tp": across_y}]
    others += [{"ctx": lax.rem(ctx + step, 4)} for step in (1, 2, 3)]
    for other in others:
        pl.semaphore_signal(barrier, inc=1, device_id=other, device_id_type=mesh_id)
    pl.semaphore_wait(barrier, len(others))

    def x_copy(at, source, land):
        return pltpu.make_async_remote_copy(
            src_ref=source, dst_ref=land, send_sem=x_send.at[at], recv_sem=x_recv.at[at],
            device_id={"fsdp": partner}, device_id_type=mesh_id,
        )

    cuts = len(gate_refs)
    gate_copies = [x_copy(i, stored_gate[i], gate_land[i]) for i in range(cuts)]
    up_copies = [x_copy(cuts + i, stored_up[i], up_land[i]) for i in range(cuts)]
    hidden_m_copy = x_copy(2 * cuts, hidden_m_send, hidden_m_land)
    branch_copy = x_copy(2 * cuts + 1, branch_send, branch_land)
    mixed_copy = x_copy(2 * cuts + 2, stored_mixed, mixed_land)
    hidden_a_copy = x_copy(2 * cuts + 3, hidden_a_send, hidden_a_land)
    qkv_copy = x_copy(2 * cuts + 4, qkv_grad_ref, qkv_land)
    queue = gate_copies + [hidden_m_copy] + up_copies
    queue += [branch_copy, mixed_copy, qkv_copy, hidden_a_copy]

    def send_next(first, last):
        for at in range(first, last):
            if at >= 2:
                queue[at - 2].wait_send()
            queue[at].start()

    split = CHUNK_ROWS // own_buf.shape[0]
    count = count * split

    def share(ref, k):
        size = CHUNK_ROWS // split
        return ref.at[k // split, pl.ds(pl.multiple_of(lax.rem(k, split) * size, size), size), :]

    def to_pair(source, land, k):
        return pltpu.make_async_remote_copy(
            src_ref=source, dst_ref=share(land, k), send_sem=send_sem.at[k],
            recv_sem=land_sem.at[k], device_id={"ctx": pair}, device_id_type=mesh_id,
        )

    def inward_copy(k):
        return to_pair(share(pool_ref, k), near_ref, k)

    def outward_copy(k):
        return to_pair(total_buf.at[lax.rem(k, 2)], sum_ref, k)

    def cross_copy(k):
        return pltpu.make_async_remote_copy(
            src_ref=part_buf.at[lax.rem(k, 4)], dst_ref=share(across_ref, k),
            send_sem=cross_send.at[k], recv_sem=cross_land.at[k],
            device_id={"ctx": across}, device_id_type=mesh_id,
        )

    def keep_copy(k):
        return pltpu.make_async_copy(
            total_buf.at[lax.rem(k, 2)], share(sum_ref, k), keep_sem.at[k]
        )

    def load(source, buffer, at):
        return pltpu.make_async_copy(source, buffer, load_sem.at[at])

    lag = 2

    def inward(k):
        inward_copy(k).wait_recv()
        loads = [load(share(pool_ref, k), own_buf, 0), load(share(near_ref, k), near_buf, 1)]
        for copy in loads:
            copy.start()
        for copy in loads:
            copy.wait()
        part_buf[lax.rem(k, 4)] = (own_buf[...].astype(F32) + near_buf[...].astype(F32)).astype(
            BF16
        )
        cross_copy(k).start()

    def outward(k, reuse):
        cross_copy(k).wait_recv()
        copy = load(share(across_ref, k), across_buf, 2)
        copy.start()
        if reuse:
            keep_copy(k - 2).wait()
            outward_copy(k - 2).wait_send()
        copy.wait()
        total_buf[lax.rem(k, 2)] = (
            part_buf[lax.rem(k, 4)].astype(F32) + across_buf[...].astype(F32)
        ).astype(BF16)
        cross_copy(k).wait_send()
        outward_copy(k).start()
        keep_copy(k).start()

    ahead = 2 * split

    def send_piece(k, carry):
        inward_copy(k).wait_send()

        @pl.when(k + ahead < count)
        def _():
            inward_copy(k + ahead).start()

        return carry

    def pump(first, last):
        first, last = first * split, last * split

        @pl.when(is_end)
        def _():
            lax.fori_loop(min(first, count), min(last, count), send_piece, 0)

        @pl.when(is_middle)
        def _():
            k = first
            while k < min(last, lag + 2):
                inward(jnp.int32(k))
                if k >= lag:
                    outward(jnp.int32(k - lag), False)
                k += 1
            if k < min(last, count):

                def both(at, carry):
                    inward(at)
                    outward(at - lag, True)
                    return carry

                lax.fori_loop(k, min(last, count), both, 0)
            k = max(k, count)
            while k < min(last, count + lag):
                outward(jnp.int32(k - lag), True)
                k += 1

    @pl.when(is_end)
    def _():
        for k in range(ahead):
            inward_copy(jnp.int32(k)).start()

    send_next(0, 2)
    fills = [
        pltpu.make_async_copy(source, buffer, loaded_sem.at[at])
        for at, (source, buffer) in enumerate(
            zip(jax.tree.leaves(stored), jax.tree.leaves(loaded))
        )
    ]
    for fill in fills:
        fill.start()
    for fill in fills:
        fill.wait()

    grad_mixed = None
    at = 0
    for piece in out_refs:
        value = dot_back(branch_ref[:, at : at + piece.shape[1]], piece[...])
        grad_mixed = value if grad_mixed is None else grad_mixed + value
        at += piece.shape[1]
    grad_mixed_ref[...] = grad_mixed.astype(BF16)

    tile = log_ref.shape[2]
    tiles = rows // tile
    reach = tile + lead

    def attend(step, carry):
        start = pl.multiple_of(step * tile, tile)
        distance = (
            lax.broadcasted_iota(jnp.int32, (reach, tile), 1)
            + lead
            - lax.broadcasted_iota(jnp.int32, (reach, tile), 0)
        )
        same = key_seg_ref[pl.ds(start, reach), :] == query_seg_ref[step]
        bias = jnp.where(same & (distance >= 0) & (distance < WINDOW), 0.0, MASK_FILL)
        query_grad, keys_grad = backward_tile(
            heads,
            group,
            lambda head: query_ref[pl.ds(start, tile), head * HD : (head + 1) * HD],
            lambda head: grad_mixed_ref[pl.ds(start, tile), head * HD : (head + 1) * HD],
            lambda head: log_ref[step, head : head + 1, :],
            lambda at: keys_ref[pl.ds(start, reach), at * HD : (at + 1) * HD],
            bias,
        )
        dq_ref[pl.ds(start, tile), :] = query_grad
        dkv_ref[pl.ds(start, reach), :] += keys_grad
        return carry

    lax.fori_loop(0, tiles, attend, 0)
    pump(0, 2)
    send_next(2, 3)

    for back in (1, 2):
        kv_send[back - 1] = dkv_ref[(2 - back) * rows : (3 - back) * rows, :].astype(BF16)

    def kv_copy(back):
        return pltpu.make_async_remote_copy(
            src_ref=kv_send.at[back - 1], dst_ref=kv_land.at[back - 1],
            send_sem=kv_send_sem.at[back - 1], recv_sem=kv_recv_sem.at[back - 1],
            device_id={"ctx": lax.rem(ctx + 4 - back, 4)}, device_id_type=mesh_id,
        )

    for back in (1, 2):

        @pl.when(ctx >= back)
        def _():
            kv_copy(back).start()

    pump(2, 3)
    for back in (1, 2):

        @pl.when(ctx + back < 4)
        def _():
            kv_copy(back).wait_recv()

    send_next(3, 4)
    kv_width = dkv_ref.shape[1] // 2
    q_width = dq_ref.shape[1]
    cosine, sine = cosine_ref[...], sine_ref[...]
    front = lax.rem(lax.broadcasted_iota(jnp.int32, (rows, LANES), 1), HD) < HD // 2

    def unrotate(value):
        swapped = jnp.where(
            front, pltpu.roll(value, LANES - HD // 2, 1), pltpu.roll(value, HD // 2, 1)
        )
        return (value * cosine - swapped * sine).astype(BF16)

    for at in range(0, q_width, LANES):
        qkv_grad_ref[:, at : at + LANES] = unrotate(dq_ref[:, at : at + LANES])
    kv_sum = dkv_ref[2 * rows :, :]
    for back in range(2):
        kv_sum = kv_sum + kv_land[back].astype(F32)
    for at in range(0, kv_width, LANES):
        qkv_grad_ref[:, q_width + at : q_width + at + LANES] = unrotate(
            kv_sum[:, at : at + LANES]
        )
    qkv_grad_ref[:, q_width + kv_width :] = kv_sum[:, kv_width:].astype(BF16)

    def tp_copy(at, source, land, target):
        return pltpu.make_async_remote_copy(
            src_ref=source, dst_ref=land, send_sem=tp_send.at[at], recv_sem=tp_recv.at[at],
            device_id={"tp": target}, device_id_type=mesh_id,
        )

    first_copy = tp_copy(0, first_ref, core_land, core)
    y_copy = tp_copy(1, chip_ref, y_land, across_y)
    total_copy = tp_copy(2, total_ref, other_ref, core)
    theirs = pl.multiple_of((1 - sibling) * half_rows, half_rows)
    mine = pl.multiple_of(sibling * half_rows, half_rows)

    def back_project(start, store):
        at = 0
        for piece in qkv_refs:
            size = piece.shape[0]
            store(at, size, dot_back(qkv_grad_ref[pl.ds(start, half_rows), :], piece[...]))
            at += size

    def store_first(at, size, value):
        first_ref[:, at : at + size] = value.astype(BF16)

    def store_second(at, size, value):
        second_ref[:, at : at + size] = value

    back_project(theirs, store_first)
    first_copy.start()
    back_project(mine, store_second)
    pump(3, 5)
    first_copy.wait_recv()
    chip_ref[...] = (second_ref[...] + core_land[...].astype(F32)).astype(BF16)
    y_copy.start()
    pump(5, 6)
    send_next(4, 5)

    def piece_copy(slot, k):
        return pltpu.make_async_copy(piece_buf.at[slot], pool_ref.at[k], piece_sem.at[slot])

    def put(first, values):
        for at, make in enumerate(values):
            slot = at % 2
            if at >= 2:
                piece_copy(slot, first + at - 2).wait()
            piece_buf[slot] = make()
            piece_copy(slot, first + at).start()
        for at in range(max(0, len(values) - 2), len(values)):
            piece_copy(at % 2, first + at).wait()

    def outer(left, left_other, right, right_other, block):
        columns = slice(block * CHUNK_ROWS, (block + 1) * CHUNK_ROWS)
        return (
            dot_outer(left[:, columns], right[...]) + dot_outer(left_other[:, columns], right_other[...])
        ).astype(BF16)

    def feed_pieces(rights, rights_other):
        return [
            functools.partial(outer, hidden_m_ref, hidden_m_land, right, right_other, block)
            for right, right_other in zip(rights, rights_other)
            for block in range(half // CHUNK_ROWS)
        ]

    for copy in gate_copies + [hidden_m_copy]:
        copy.wait_recv()
    put(starts[1], feed_pieces(gate_refs, gate_land))
    pump(6, 7)

    y_copy.wait_recv()
    total_ref[...] = (chip_ref[...].astype(F32) + y_land[...].astype(F32)).astype(BF16)
    total_copy.start()
    gain = gain_ref[...]
    near_at = pl.multiple_of((1 - shard) * half + lax.rem(ctx, 2) * part, part)
    far_at = pl.multiple_of((1 - shard) * half + (1 - lax.rem(ctx, 2)) * part, part)
    own_at = pl.multiple_of(shard * half, half)
    step_rows = 64

    def norm_rows(source, base):
        def body(step, total):
            at = pl.multiple_of(step * step_rows, step_rows)
            here = pl.ds(pl.multiple_of(base + at, step_rows), step_rows)
            scale = scale_ref[here, :]
            normed = inputs_ref[here, :].astype(F32) * scale
            hidden = source[pl.ds(at, step_rows), :].astype(F32)
            grad = hidden * gain
            mean = jnp.sum(grad * normed, axis=-1, keepdims=True) * (1.0 / width)
            value = (grad_middle_ref[here, :] + scale * (grad - normed * mean)).astype(BF16)
            grad_ref[here, pl.ds(own_at, half)] = value[:, :half]
            grad_ref[here, pl.ds(near_at, part)] = value[:, half : half + part]
            grad_ref[here, pl.ds(far_at, part)] = value[:, half + part :]
            return total + jnp.sum(hidden * normed, axis=0, keepdims=True)

        return lax.fori_loop(0, half_rows // step_rows, body, jnp.zeros((1, width), F32))

    gain_sum = norm_rows(total_ref, mine)
    pump(7, 8)
    send_next(5, 6)
    total_copy.wait_recv()
    gain_out_ref[...] = gain_sum + norm_rows(other_ref, theirs)
    pump(8, 10)
    send_next(6, 7)
    for copy in up_copies:
        copy.wait_recv()
    put(starts[2], feed_pieces(up_refs, up_land))
    pump(10, 12)
    send_next(7, 8)
    pump(12, 14)
    send_next(8, len(queue))
    branch_copy.wait_recv()
    mixed_copy.wait_recv()
    put(
        starts[3],
        [
            functools.partial(
                outer, mixed_ref, mixed_land, branch_ref.at[:, :half], branch_land, block
            )
            for block in range(q_width // CHUNK_ROWS)
        ],
    )
    pump(14, 17)
    hidden_a_copy.wait_recv()
    qkv_copy.wait_recv()

    def side_by_side(first, number, columns):
        return jnp.concatenate(
            [
                outer(
                    hidden_a_ref, hidden_a_land, qkv_grad_ref.at[:, columns],
                    qkv_land.at[:, columns], block,
                )
                for block in range(first, first + number)
            ],
            axis=1,
        )

    q_blocks = CHUNK_COLUMNS // q_width
    put(
        starts[4],
        [
            functools.partial(side_by_side, first, q_blocks, slice(0, q_width))
            for first in range(0, half // CHUNK_ROWS, q_blocks)
        ]
        + [
            functools.partial(
                side_by_side, 0, half // CHUNK_ROWS, slice(q_width, q_width + 2 * kv_width)
            )
        ],
    )
    pump(17, count // split + lag)

    for copy in queue[-2:] + [first_copy, y_copy, total_copy]:
        copy.wait_send()
    for back in (1, 2):

        @pl.when(ctx >= back)
        def _():
            kv_copy(back).wait_send()

    @pl.when(is_middle)
    def _():
        for k in (count - 2, count - 1):
            outward_copy(jnp.int32(k)).wait_send()
            keep_copy(jnp.int32(k)).wait()

    @pl.when(is_end)
    def _():
        def close(k, carry):
            to_pair(share(pool_ref, k), sum_ref, k).wait_recv()
            return carry

        lax.fori_loop(0, count, close, 0)


def flat_call(body, operands, **call):
    flat, tree = jax.tree.flatten(operands)

    def unflatten(*refs):
        body(*jax.tree.unflatten(tree, refs[: len(flat)]), *refs[len(flat) :])

    in_specs = [pl.BlockSpec(memory_space=pl.ANY)] * len(flat)
    return pl.pallas_call(unflatten, in_specs=in_specs, **call)(*flat)


def tail(plan, pool, v):
    heads, group, lead, starts, count = plan
    rows, width = v["inputs"].shape
    half = width // 2
    q_width, kv_width = v["query"].shape[1], v["keys_values"].shape[1] // 2
    qkv_width = q_width + 2 * kv_width
    piece = (CHUNK_ROWS, CHUNK_COLUMNS)
    split = 2
    step, steps = (CHUNK_ROWS // split, CHUNK_COLUMNS), count * split
    cuts, feed_part = len(v["grad_gate"]), v["grad_gate"][0].shape[1]

    stored = [
        v["grad_gate"], v["grad_up"], v["hidden_m"], v["hidden_a"], v["branch"], v["mixed"],
        v["out_pieces"], v["query"], v["keys_values"], v["log_sums"], v["query_segments"],
        v["key_segments"], v["cosine"], v["sine"], v["qkv_pieces"], v["inputs"], v["scale"],
        v["gain"], v["grad_middle"],
    ]
    operands = [pool, v["hidden_m_send"], v["hidden_a_send"], v["branch_send"], stored]
    loaded = jax.tree.map(lambda value: pltpu.VMEM(value.shape, value.dtype), stored)
    any_space, vmem_space = pl.BlockSpec(memory_space=pl.ANY), pl.BlockSpec(memory_space=pltpu.VMEM)
    line = jax.ShapeDtypeStruct((count,) + piece, BF16)
    dma = pltpu.SemaphoreType.DMA
    low = lambda *shape: pltpu.VMEM(shape, BF16)
    wide = lambda *shape: pltpu.VMEM(shape, F32)
    scratch = [
        [low(rows, feed_part) for _ in range(cuts)],
        [low(rows, feed_part) for _ in range(cuts)],
        low(rows, half), low(rows, half), low(rows, half),
        low(rows, q_width), low(rows, qkv_width),
        low(rows, q_width), wide(rows, q_width), wide(3 * rows, 2 * kv_width),
        low(2, rows, 2 * kv_width), low(2, rows, 2 * kv_width), low(rows, qkv_width),
        low(rows // 2, width), wide(rows // 2, width), low(rows // 2, width),
        low(rows // 2, width), low(rows // 2, width), low(rows // 2, width),
        low(rows // 2, width),
        low(*step), low(*step), low(4, *step), low(*step), low(2, *step), low(2, *piece),
        dma((2 * cuts + 5,)), dma((2 * cuts + 5,)), dma((3,)), dma((3,)), dma((2,)), dma((2,)),
        dma((steps,)), dma((steps,)), dma((steps,)), dma((steps,)), dma((steps,)),
        dma((3,)), dma((2,)),
        loaded, dma((len(jax.tree.leaves(stored)),)),
    ]
    outs = flat_call(
        functools.partial(tail_body, plan),
        operands,
        out_specs=[any_space, any_space, any_space, any_space, vmem_space, vmem_space],
        out_shape=[
            line, line, line, line,
            jax.ShapeDtypeStruct((rows, width), BF16),
            jax.ShapeDtypeStruct((1, width), F32),
        ],
        scratch_shapes=scratch,
        input_output_aliases={0: 0},
        compiler_params=pltpu.CompilerParams(
            collective_id=0, has_side_effects=True, vmem_limit_bytes=60 << 20
        ),
        cost_estimate=pl.CostEstimate(
            flops=400 << 30, bytes_accessed=30 << 20, transcendentals=0
        ),
        name="tail",
    )
    return outs[1], outs[4], outs[5]


def swap(value, axis, size, bit):
    return lax.ppermute(value, axis, [(i, i ^ bit) for i in range(size)])


def shift(value, axis, size, by):
    if abs(by) >= size:
        return jnp.zeros_like(value)
    return lax.ppermute(
        value, axis, [(i, i + by) for i in range(size) if 0 <= i + by < size]
    )


class Lane:
    def __init__(self, move, depth=2):
        self.move, self.depth, self.done = move, depth, []

    def send(self, value):
        if len(self.done) >= self.depth:
            value, self.done[-self.depth] = tie(value, self.done[-self.depth])
        self.done.append(self.move(value))
        return len(self.done) - 1

    def get(self, at):
        return self.done[at]


def shards(
    sizes,
    block_input,
    segment_ids,
    attention_gain,
    query_weight,
    key_weight,
    value_weight,
    out_weight,
    feed_gain,
    gate_weight,
    up_weight,
    down_weight,
    cotangent,
):
    shard_count, ctx_count, tp_count = sizes
    seqs, span, width = block_input.shape
    rows = seqs * span
    seq_length = segment_ids.shape[1]
    half = width // 2
    part = half // 2
    q_width = query_weight.shape[1]
    kv_width = key_weight.shape[1]
    feed_width = gate_weight.shape[1]
    group = q_width // kv_width
    shard, ctx, tp = (lax.axis_index(name) for name in ("fsdp", "ctx", "tp"))
    odd = ctx % 2
    sibling = tp % 2

    own_at = shard * half
    near_at = (1 - shard) * half + odd * part
    far_at = (1 - shard) * half + (1 - odd) * part

    def to_local(value):
        return jnp.concatenate(
            [
                take(value, own_at, half, 1),
                take(value, near_at, part, 1),
                take(value, far_at, part, 1),
            ],
            axis=1,
        )

    def other_half(value):
        return jnp.concatenate(
            [
                take(value, half + odd * part, part, 1),
                take(value, half + (1 - odd) * part, part, 1),
            ],
            axis=1,
        )

    def from_local(value):
        own, other = value[:, :half], other_half(value)
        return jnp.where(
            shard == 0,
            jnp.concatenate([own, other], axis=1),
            jnp.concatenate([other, own], axis=1),
        )

    fsdp_lane = Lane(lambda value: swap(value, "fsdp", shard_count, 1))

    def over_fsdp(value):
        return swap(value, "fsdp", shard_count, 1)

    def over_ctx(value):
        return swap(value, "ctx", ctx_count, 1)

    def near_part(weight, axis):
        return take(weight, odd * part, part, axis)

    def core_half(value):
        return take(value, sibling * (rows // 2), rows // 2, 0)

    def join_cores(mine):
        other = swap(mine, "tp", tp_count, 1)
        return jnp.where(
            sibling == 0,
            jnp.concatenate([mine, other], axis=0),
            jnp.concatenate([other, mine], axis=0),
        )

    def chip_sum(first, second):
        return (second + swap(first, "tp", tp_count, 1).astype(F32)).astype(BF16)

    def finish_sum(chip):
        total = (chip.astype(F32) + swap(chip, "tp", tp_count, 2).astype(F32)).astype(BF16)
        return join_cores(total).astype(F32)

    def tp_sum(first, second):
        if tp_count != 4:
            whole_rows = jnp.where(
                sibling == 0,
                jnp.concatenate([second, first.astype(F32)], axis=0),
                jnp.concatenate([first.astype(F32), second], axis=0),
            )
            return lax.psum(whole_rows, "tp")
        return finish_sum(chip_sum(first, second))

    gains_own = jnp.stack([attention_gain, feed_gain])
    qkv_own = jnp.concatenate([query_weight, key_weight, value_weight], axis=1)
    feed_cuts = 2
    feed_part = feed_width // feed_cuts
    columns = [slice(cut * feed_part, (cut + 1) * feed_part) for cut in range(feed_cuts)]
    grad_rows = to_local(cotangent.reshape(rows, width))
    send_gate = [near_part(gate_weight[:, cut], 0) for cut in columns]
    send_up = [near_part(up_weight[:, cut], 0) for cut in columns]
    send_down = [near_part(down_weight[cut], 1) for cut in columns]
    send_grad = core_half(other_half(grad_rows))

    gains_other = over_fsdp(gains_own)
    near_qkv = over_fsdp(near_part(qkv_own, 0))
    gains_other, send_out = tie(gains_other, near_part(out_weight, 1))
    near_out = over_fsdp(send_out)

    span_start = ctx * span
    positions = take(doc_positions(segment_ids), span_start, span, 1).reshape(rows)
    query_segments = take(segment_ids, span_start, span, 1)
    cosine, sine = rope_tables(positions)
    blocks_back, base, lead = attention_plan(span, WINDOW)
    key_segments = take(
        jnp.pad(segment_ids, ((0, 0), (blocks_back * span, 0)), constant_values=-1),
        span_start,
        (blocks_back + 1) * span,
        1,
    )

    inputs = to_local(block_input.reshape(rows, width)).astype(F32)
    scale_a = row_scale_of(inputs)
    normed_a = inputs * scale_a
    gains = jnp.concatenate(
        [gains_own, take(gains_other, odd * part, part, 1), take(gains_other, (1 - odd) * part, part, 1)],
        axis=1,
    ).astype(F32)
    gain_a, gain_m = gains[0:1], gains[1:2]
    hidden_a = (normed_a * gain_a).astype(BF16)

    near_qkv, send_gate[0] = tie(near_qkv, send_gate[0])
    near_gate, near_up, far_gate, far_up = ([None] * feed_cuts for _ in range(4))
    near_gate[0] = over_fsdp(send_gate[0])
    far_qkv = over_ctx(near_qkv)
    near_out, send_up[0] = tie(near_out, send_up[0])
    near_up[0] = over_fsdp(send_up[0])
    far_qkv, near_out = tie(far_qkv, near_out)
    far_out = over_ctx(near_out)

    def dot_pieces(matrix, own, near, far):
        return (
            dot_rows(matrix[:, :half], own)
            + dot_rows(matrix[:, half : half + part], near)
            + dot_rows(matrix[:, half + part :], far)
        )

    def back_pieces(matrix, own, near, far):
        return jnp.concatenate(
            [dot_back(matrix, own), dot_back(matrix, near), dot_back(matrix, far)], axis=1
        )

    qkv = dot_pieces(hidden_a, qkv_own, near_qkv, far_qkv)
    key_low = rotate(qkv[:, q_width : q_width + kv_width], cosine, sine).astype(BF16)
    value_low = qkv[:, q_width + kv_width :].astype(BF16)
    keys_values = jnp.concatenate([key_low, value_low], axis=1).reshape(seqs, span, 2 * kv_width)
    query_low = (rotate(qkv[:, :q_width], cosine, sine).astype(BF16) * HD**-0.5).reshape(
        seqs, span, q_width
    )
    earlier = [shift(keys_values, "ctx", ctx_count, back) for back in range(blocks_back, 0, -1)]
    *earlier, query_low = tie(*earlier, query_low)
    keys_values = jnp.concatenate(earlier + [keys_values], axis=1)
    mixed, log_sums = attend_forward(
        query_low, keys_values, query_segments, key_segments, base, lead, group
    )
    mixed_low = mixed.reshape(rows, q_width)
    mixed_low, far_out, near_gate[0], near_up[0], send_gate[1], send_up[1] = tie(
        mixed_low, far_out, near_gate[0], near_up[0], send_gate[1], send_up[1]
    )
    near_gate[1] = over_fsdp(send_gate[1])
    far_gate[0] = over_ctx(near_gate[0])
    near_up[1] = over_fsdp(send_up[1])
    far_up[0] = over_ctx(near_up[0])

    def out_project(at):
        matrix = take(mixed_low, at * (rows // 2), rows // 2, 0)
        return jnp.concatenate(
            [dot_rows(matrix, out_weight), dot_rows(matrix, near_out), dot_rows(matrix, far_out)],
            axis=1,
        )

    first, second = out_project(1 - sibling).astype(BF16), out_project(sibling)
    if tp_count == 4:
        chip = chip_sum(first, second)
        total = (chip.astype(F32) + swap(chip, "tp", tp_count, 2).astype(F32)).astype(BF16)
        total, near_gate[1], far_gate[0] = tie(total, near_gate[1], far_gate[0])
        branch_a = join_cores(total).astype(F32)
    else:
        branch_a = tp_sum(first, second)
    far_gate[1] = over_ctx(near_gate[1])
    middle = inputs + branch_a

    scale_m = row_scale_of(middle)
    normed_m = middle * scale_m
    hidden_m = (normed_m * gain_m).astype(BF16)
    hidden_m, near_up[1], far_up[0], send_down[0] = tie(
        hidden_m, near_up[1], far_up[0], send_down[0]
    )
    near_down = [over_fsdp(send_down[0])]
    far_up[1] = over_ctx(near_up[1])
    gate_cuts, up_cuts, act_cuts = [], [], []

    def feed(cut):
        gate_value, up_value, activated = feed_forward(
            hidden_m,
            (gate_weight, near_gate[cut], far_gate[cut]),
            (up_weight, near_up[cut], far_up[cut]),
            cut,
            feed_part,
        )
        gate_cuts.append(gate_value)
        up_cuts.append(up_value)
        act_cuts.append(activated)

    feed(0)
    act_cuts[0], near_down[0], far_gate[1], send_down[1] = tie(
        act_cuts[0], near_down[0], far_gate[1], send_down[1]
    )
    near_down.append(over_fsdp(send_down[1]))
    far_down = [over_ctx(near_down[0])]
    feed(1)
    act_cuts[1], near_down[1], send_grad, act_cuts[0] = tie(
        act_cuts[1], near_down[1], send_grad, act_cuts[0]
    )
    other_grad = over_fsdp(send_grad)
    act_other = [over_fsdp(act_cuts[0]), over_fsdp(act_cuts[1])]
    far_down.append(over_ctx(near_down[1]))

    pieces = CHUNK_ROWS * CHUNK_COLUMNS
    down_count = feed_width * half // pieces
    starts, pool_size = [], 0
    for size in (feed_width * half,) * 3 + (q_width * half,) * 2 + (2 * kv_width * half,):
        starts.append(pool_size)
        pool_size += size // pieces
    grad_gate_cuts, grad_up_cuts = [], []
    for cut in range(feed_cuts):
        grad_gate, grad_up = feed_backward(
            grad_rows,
            (down_weight, near_down[cut], far_down[cut]),
            gate_cuts[cut],
            up_cuts[cut],
            cut,
        )
        grad_gate_cuts.append(grad_gate)
        grad_up_cuts.append(grad_up)

    grad_gate_cuts[1], act_other[0], other_grad = tie(
        grad_gate_cuts[1], act_other[0], other_grad
    )
    grad_own, grad_other = grad_rows[:, :half], join_cores(other_grad)
    first, second = project(
        sibling,
        list(zip(grad_gate_cuts, grad_up_cuts)),
        [
            (
                (gate_weight, near_gate[cut], far_gate[cut]),
                (up_weight, near_up[cut], far_up[cut]),
            )
            for cut in range(feed_cuts)
        ],
        width,
        True,
    )
    first, second, act_other[1], *act_cuts = tie(first, second, act_other[1], *act_cuts)
    if tp_count == 4:
        chip = chip_sum(first, second)
        total = (chip.astype(F32) + swap(chip, "tp", tp_count, 2).astype(F32)).astype(BF16)
        grad_hidden_m = join_cores(total).astype(F32)
    else:
        total = None
        grad_hidden_m = tp_sum(first, second)
    fsdp_lane.done = list(act_other)
    pool = None
    for cut in range(feed_cuts):
        pool = outer_sum(
            pool,
            cut * down_count // feed_cuts,
            pool_size,
            act_cuts[cut],
            act_other[cut],
            [grad_own],
            [grad_other],
        )

    feed_gain_part = jnp.sum(grad_hidden_m * normed_m, axis=0)
    grad_middle = norm_back(grad_hidden_m, gain_m, normed_m, scale_m, grad_rows.astype(F32))
    grad_branch = grad_middle.astype(BF16)

    first, second = project(
        sibling,
        [(value,) for value in act_cuts],
        [((down_weight, near_down[cut], far_down[cut]),) for cut in range(feed_cuts)],
        width,
        False,
    )
    if tp_count == 4:
        chip = chip_sum(first, second)
        across = swap(chip, "tp", tp_count, 2)
    else:
        chip = across = None
        branch_m = tp_sum(first, second)

    fused = (shard_count, ctx_count, tp_count) == (2, 4, 4)
    fused = fused and seqs == 1 and (blocks_back, base) == (2, 0)
    if fused:
        tile = min(LANES, rows)
        log_rows = jnp.swapaxes(log_sums[0, :, : q_width // HD].reshape(rows // tile, tile, -1), 1, 2)
        pool, input_grad, gain_row = tail(
            (
                q_width // HD,
                group,
                lead,
                tuple(starts),
                pool_size,
            ),
            pool,
            {
                "grad_gate": grad_gate_cuts,
                "grad_up": grad_up_cuts,
                "hidden_m": hidden_m[:, :half],
                "hidden_m_send": other_half(hidden_m),
                "hidden_a": hidden_a[:, :half],
                "hidden_a_send": other_half(hidden_a),
                "branch": grad_branch,
                "branch_send": other_half(grad_branch),
                "mixed": mixed_low,
                "out_pieces": [out_weight, near_out, far_out],
                "query": query_low[0],
                "keys_values": keys_values[0],
                "log_sums": log_rows,
                "query_segments": query_segments.reshape(rows // tile, 1, tile),
                "key_segments": key_segments.reshape(-1, 1),
                "cosine": cosine,
                "sine": sine,
                "qkv_pieces": [qkv_own, near_qkv, far_qkv],
                "inputs": inputs.astype(BF16),
                "scale": scale_a,
                "gain": gain_a,
                "grad_middle": grad_middle,
            },
        )
        attention_gain_part = gain_row[0]
        input_grad = input_grad.reshape(seqs, span, width)
        across, pool = tie(across, pool)
    else:
        gate_at = [fsdp_lane.send(value) for value in grad_gate_cuts]
        up_at = [fsdp_lane.send(value) for value in grad_up_cuts]
        hidden_m_at = fsdp_lane.send(core_half(other_half(hidden_m)))
        hidden_own, hidden_other = hidden_m[:, :half], join_cores(fsdp_lane.get(hidden_m_at))
        for which, (own, at) in enumerate(((grad_gate_cuts, gate_at), (grad_up_cuts, up_at))):
            pool = outer_sum(
                pool,
                starts[1 + which],
                pool_size,
                hidden_own,
                hidden_other,
                own,
                [fsdp_lane.get(i) for i in at],
            )

        grad_mixed = (
            dot_back(grad_branch[:, :half], out_weight)
            + dot_back(grad_branch[:, half : half + part], near_out)
            + dot_back(grad_branch[:, half + part :], far_out)
        ).astype(BF16)
        branch_at = fsdp_lane.send(core_half(other_half(grad_branch)))
        mixed_at = fsdp_lane.send(mixed_low)
        hidden_a_at = fsdp_lane.send(core_half(other_half(hidden_a)))
        grad_query, grad_keys_values = attend_backward(
            query_low,
            keys_values,
            grad_mixed.reshape(seqs, span, q_width),
            jnp.swapaxes(log_sums, 1, 2)[:, : q_width // HD],
            query_segments,
            key_segments,
            base,
            lead,
            group,
        )
        kv_sum = grad_keys_values[:, blocks_back * span :]
        for back in range(1, blocks_back + 1):
            at = (blocks_back - back) * span
            kv_sum = kv_sum + shift(
                grad_keys_values[:, at : at + span].astype(BF16), "ctx", ctx_count, -back
            ).astype(F32)
        kv_sum = kv_sum.reshape(rows, 2 * kv_width)
        grad_qkv = jnp.concatenate(
            [
                rotate(grad_query.reshape(rows, q_width), cosine, -sine),
                rotate(kv_sum[:, :kv_width], cosine, -sine),
                kv_sum[:, kv_width:],
            ],
            axis=1,
        ).astype(BF16)
        qkv_at = fsdp_lane.send(grad_qkv)
        first, second = (
            back_pieces(take(grad_qkv, at * (rows // 2), rows // 2, 0), qkv_own, near_qkv, far_qkv)
            for at in (1 - sibling, sibling)
        )
        grad_hidden_a = tp_sum(first.astype(BF16), second)
        attention_gain_part = jnp.sum(grad_hidden_a * normed_a, axis=0)
        input_grad = norm_back(grad_hidden_a, gain_a, normed_a, scale_a, grad_middle)
        input_grad = from_local(input_grad.astype(BF16)).reshape(seqs, span, width)

        pool = outer_sum(
            pool,
            starts[3],
            pool_size,
            mixed_low,
            fsdp_lane.get(mixed_at),
            [grad_branch[:, :half]],
            [join_cores(fsdp_lane.get(branch_at))],
        )
        qkv_other = fsdp_lane.get(qkv_at)
        hidden_own, hidden_other = hidden_a[:, :half], join_cores(fsdp_lane.get(hidden_a_at))
        for which, cut in ((4, slice(0, q_width)), (5, slice(q_width, None))):
            pool = outer_sum(
                pool,
                starts[which],
                pool_size,
                hidden_own,
                hidden_other,
                [grad_qkv[:, cut]],
                [qkv_other[:, cut]],
            )
        pool = lax.psum(pool.astype(F32), "ctx")

    if tp_count == 4:
        total = (chip.astype(F32) + across.astype(F32)).astype(BF16)
        branch_m = join_cores(total).astype(F32)
    block_out = from_local((middle + branch_m).astype(BF16)).reshape(seqs, span, width)

    gain_parts = jnp.stack([attention_gain_part, feed_gain_part])
    gain_other = over_fsdp(other_half(gain_parts))
    gain_sums = lax.psum(gain_parts[:, :half] + gain_other, "ctx")

    down_grad, gate_grad, up_grad, out_grad, query_grad, key_grad, value_grad = widen(
        pool,
        starts,
        [
            down_weight.shape,
            gate_weight.shape,
            up_weight.shape,
            out_weight.shape,
            query_weight.shape,
            key_weight.shape,
            value_weight.shape,
        ],
    )
    return (
        block_out,
        input_grad,
        gain_sums[0],
        query_grad,
        key_grad,
        value_grad,
        out_grad,
        gain_sums[1],
        gate_grad,
        up_grad,
        down_grad,
    )


def solution(mesh):
    sizes = tuple(mesh.shape[name] for name in ("fsdp", "ctx", "tp"))
    in_specs = (
        P("fsdp", "ctx", None),
        P("fsdp", None),
        P("fsdp"),
        P("fsdp", "tp"),
        P("fsdp", "tp"),
        P("fsdp", "tp"),
        P("tp", "fsdp"),
        P("fsdp"),
        P("fsdp", "tp"),
        P("fsdp", "tp"),
        P("tp", "fsdp"),
        P("fsdp", "ctx", None),
    )
    out_specs = (
        P("fsdp", "ctx", None),
        P("fsdp", "ctx", None),
        P("fsdp"),
        P("fsdp", "tp"),
        P("fsdp", "tp"),
        P("fsdp", "tp"),
        P("tp", "fsdp"),
        P("fsdp"),
        P("fsdp", "tp"),
        P("fsdp", "tp"),
        P("tp", "fsdp"),
    )
    return jax.shard_map(
        functools.partial(shards, sizes),
        mesh=mesh,
        in_specs=in_specs,
        out_specs=out_specs,
        check_vma=False,
    )
```

```python
import functools

import jax
import jax.numpy as jnp
from jax import lax
from jax.experimental import pallas as pl
from jax.experimental.pallas import tpu as pltpu
from jax.sharding import PartitionSpec as P

HD = 64
WINDOW = 1024
NORM_EPS = 1e-05
ROPE_BASE = 500000.0
MASK_FILL = -1e30
LANES = 128
F32 = jnp.float32
BF16 = jnp.bfloat16


def dot_rows(matrix, other_side):
    return jnp.dot(matrix, other_side, preferred_element_type=F32)


def dot_back(matrix, other_side):
    return lax.dot_general(matrix, other_side, (((1,), (1,)), ((), ())), preferred_element_type=F32)


def dot_outer(matrix, other_side):
    return lax.dot_general(matrix, other_side, (((0,), (0,)), ((), ())), preferred_element_type=F32)


def tie(*values):
    return lax.optimization_barrier(values)


def take(array, start, size, axis):
    return lax.dynamic_slice_in_dim(array, start, size, axis)


def doc_positions(segments):
    seq_count, seq_length = segments.shape
    index_grid = jnp.broadcast_to(jnp.arange(seq_length, dtype=jnp.int32)[None, :], segments.shape)
    begins = jnp.concatenate(
        [jnp.ones((seq_count, 1), dtype=bool), segments[:, 1:] != segments[:, :-1]], axis=1
    )
    return index_grid - lax.cummax(jnp.where(begins, index_grid, 0), axis=1)


def rope_tables(positions):
    half_size = HD // 2
    frequency = ROPE_BASE ** (-(jnp.arange(half_size, dtype=F32) * 2.0 / HD))
    angles = positions.astype(F32)[:, None] * frequency
    cosine, sine = jnp.cos(angles), jnp.sin(angles)
    return jnp.concatenate([cosine] * 4, axis=1), jnp.concatenate([-sine, sine] * 2, axis=1)


def rotate(vectors, cosine, signed_sine):
    width = vectors.shape[1]
    half = HD // 2
    ahead = jnp.concatenate([vectors[:, half:], vectors[:, :half]], axis=1)
    behind = jnp.concatenate([vectors[:, -half:], vectors[:, :-half]], axis=1)
    first = (jnp.arange(width) % HD < half)[None, :]
    reps = width // LANES
    return vectors * jnp.tile(cosine, (1, reps)) + jnp.where(first, ahead, behind) * jnp.tile(
        signed_sine, (1, reps)
    )


def row_scale_of(values):
    return lax.rsqrt(jnp.mean(values * values, axis=-1, keepdims=True) + NORM_EPS)


def norm_back(grad_hidden, gain, normed, row_scale, residual_grad):
    grad_normed = grad_hidden * gain
    return residual_grad + row_scale * (
        grad_normed - normed * jnp.mean(grad_normed * normed, axis=-1, keepdims=True)
    )


def attend_forward_body(lead, heads, group, q_ref, kv_ref, qseg_ref, kseg_ref, mixed_ref, lse_ref):
    block = q_ref.shape[1]
    reach = kseg_ref.shape[-1]
    start = pl.multiple_of(pl.program_id(1) * block, block)
    window = kv_ref.at[0, pl.ds(start, reach), :]
    distance = (
        lax.broadcasted_iota(jnp.int32, (block, reach), 0)
        + lead
        - lax.broadcasted_iota(jnp.int32, (block, reach), 1)
    )
    allowed = (qseg_ref[0] == kseg_ref[0, 0]) & (distance >= 0) & (distance < WINDOW)
    bias = jnp.where(allowed, 0.0, MASK_FILL)
    lane = lax.broadcasted_iota(jnp.int32, (block, LANES), 1)
    log_sums = jnp.zeros((block, LANES), F32)
    kv_width = heads // group * HD
    outs = []
    for head in range(heads):
        shared = head // group * HD
        keys = window[:, shared : shared + HD]
        values = window[:, kv_width + shared : kv_width + shared + HD]
        scores = dot_back(q_ref[0, :, head * HD : (head + 1) * HD], keys) + bias
        row_max = jnp.max(scores, axis=-1, keepdims=True)
        exponent = jnp.exp(scores - row_max)
        row_total = jnp.sum(exponent, axis=-1, keepdims=True)
        probs = (exponent * (1.0 / row_total)).astype(BF16)
        outs.append(dot_rows(probs, values))
        log_sums = jnp.where(lane == head, row_max + jnp.log(row_total), log_sums)
    mixed_ref[0] = jnp.concatenate(outs, axis=1).astype(BF16)
    lse_ref[0] = log_sums


def attend_backward_body(
    lead, heads, group, q_ref, kv_ref, grad_ref, lse_ref, qseg_ref, kseg_ref, dq_ref, dkv_ref
):
    block = q_ref.shape[1]
    reach = block + lead
    step = pl.program_id(1)
    start = pl.multiple_of(step * block, block)
    window = kv_ref.at[0, pl.ds(start, reach), :]

    @pl.when(step == 0)
    def _():
        dkv_ref[...] = jnp.zeros_like(dkv_ref)

    distance = (
        lax.broadcasted_iota(jnp.int32, (reach, block), 1)
        + lead
        - lax.broadcasted_iota(jnp.int32, (reach, block), 0)
    )
    same = kseg_ref[0, pl.ds(start, reach), :] == qseg_ref[0]
    bias = jnp.where(same & (distance >= 0) & (distance < WINDOW), 0.0, MASK_FILL)
    query_grad, keys_grad = backward_tile(
        heads,
        group,
        lambda head: q_ref[0, :, head * HD : (head + 1) * HD],
        lambda head: grad_ref[0, :, head * HD : (head + 1) * HD],
        lambda head: lse_ref[0, head : head + 1, :],
        lambda at: window[:, at * HD : (at + 1) * HD],
        bias,
    )
    dq_ref[0] = query_grad
    dkv_ref[0, pl.ds(start, reach), :] += keys_grad


def backward_tile(heads, group, query_of, grad_of, log_sum_of, window_of, bias):
    key_grads, value_grads, query_grads = [], [], []
    shared_heads = heads // group
    for shared in range(shared_heads):
        keys, values = window_of(shared), window_of(shared_heads + shared)
        key_sum = value_sum = None
        for member in range(group):
            head = shared * group + member
            query, grad = query_of(head), grad_of(head)
            probs = jnp.exp(dot_back(keys, query) + bias - log_sum_of(head))
            grad_probs = dot_back(values, grad)
            spread = jnp.sum(probs * grad_probs, axis=0, keepdims=True)
            grad_scores = (probs * (grad_probs - spread)).astype(BF16)
            value_part = dot_rows(probs.astype(BF16), grad)
            key_part = dot_rows(grad_scores, query)
            query_grads.append(dot_outer(grad_scores, keys) * HD**-0.5)
            value_sum = value_part if value_sum is None else value_sum + value_part
            key_sum = key_part if key_sum is None else key_sum + key_part
        key_grads.append(key_sum)
        value_grads.append(value_sum)
    return jnp.concatenate(query_grads, axis=1), jnp.concatenate(key_grads + value_grads, axis=1)


def attention_plan(span, window):
    blocks_back = -(-(window - 1) // span)
    base = (blocks_back * span - (window - 1)) // LANES * LANES
    return blocks_back, base, blocks_back * span - base


def key_tiles(key_segments, base, lead, block, span):
    return jnp.stack(
        [
            key_segments[:, base + at : base + at + block + lead]
            for at in range(0, span, block)
        ],
        axis=1,
    )[:, :, None, :]


def attend_forward(query, keys_values, query_segments, key_segments, base, lead, group):
    seqs, span, width = query.shape
    block = min(LANES, span)
    heads = width // HD
    reach = block + lead
    keys_used = keys_values[:, base:]
    return pl.pallas_call(
        functools.partial(attend_forward_body, lead, heads, group),
        grid=(seqs, span // block),
        in_specs=[
            pl.BlockSpec((1, block, width), lambda s, i: (s, i, 0)),
            pl.BlockSpec((1,) + keys_used.shape[1:], lambda s, i: (s, 0, 0)),
            pl.BlockSpec((1, block, 1), lambda s, i: (s, i, 0)),
            pl.BlockSpec((1, 1, 1, reach), lambda s, i: (s, i, 0, 0)),
        ],
        out_specs=[
            pl.BlockSpec((1, block, width), lambda s, i: (s, i, 0)),
            pl.BlockSpec((1, block, LANES), lambda s, i: (s, i, 0)),
        ],
        out_shape=[
            jax.ShapeDtypeStruct(query.shape, BF16),
            jax.ShapeDtypeStruct((seqs, span, LANES), F32),
        ],
        compiler_params=pltpu.CompilerParams(vmem_limit_bytes=40 << 20),
        cost_estimate=pl.CostEstimate(
            flops=70 * seqs * span * reach * width, bytes_accessed=4 << 20, transcendentals=0
        ),
        name="attend_forward",
    )(query, keys_used, query_segments[:, :, None], key_tiles(key_segments, base, lead, block, span))


def attend_backward(
    query, keys_values, grad_mixed, log_sums, query_segments, key_segments, base, lead, group
):
    seqs, span, width = query.shape
    block = min(LANES, span)
    heads = width // HD
    reach = block + lead
    keys_used = keys_values[:, base:]
    whole_keys = pl.BlockSpec((1,) + keys_used.shape[1:], lambda s, i: (s, 0, 0))
    rows = pl.BlockSpec((1, block, width), lambda s, i: (s, i, 0))
    grad_query, grad_keys_values = pl.pallas_call(
        functools.partial(attend_backward_body, lead, heads, group),
        grid=(seqs, span // block),
        in_specs=[
            rows,
            whole_keys,
            rows,
            pl.BlockSpec((1, heads, block), lambda s, i: (s, 0, i)),
            pl.BlockSpec((1, 1, block), lambda s, i: (s, 0, i)),
            pl.BlockSpec((1, keys_used.shape[1], 1), lambda s, i: (s, 0, 0)),
        ],
        out_specs=[rows, whole_keys],
        out_shape=[
            jax.ShapeDtypeStruct(query.shape, F32),
            jax.ShapeDtypeStruct(keys_used.shape, F32),
        ],
        compiler_params=pltpu.CompilerParams(vmem_limit_bytes=40 << 20),
        cost_estimate=pl.CostEstimate(
            flops=85 * seqs * span * reach * width, bytes_accessed=6 << 20, transcendentals=0
        ),
        name="attend_backward",
    )(
        query,
        keys_used,
        grad_mixed,
        log_sums,
        query_segments[:, None, :],
        key_segments[:, base:, None],
    )
    return grad_query, jnp.pad(grad_keys_values, ((0, 0), (base, 0), (0, 0)))


def whole(array):
    return pl.BlockSpec(array.shape, lambda *at: (0,) * array.ndim)


def kernel_cost(flops, moved):
    return pl.CostEstimate(flops=flops, bytes_accessed=moved, transcendentals=0)


def feed_forward_body(sizes, hidden_ref, *refs):
    count = len(sizes)
    gate_refs, up_refs = refs[:count], refs[count : 2 * count]
    gate_ref, up_ref, act_ref = refs[2 * count :]

    def project(pieces):
        total, at = None, 0
        for size, piece in zip(sizes, pieces):
            value = dot_rows(hidden_ref[:, at : at + size], piece[...])
            total = value if total is None else total + value
            at += size
        return total

    gate_value, up_value = project(gate_refs), project(up_refs)
    gate_ref[...] = gate_value
    up_ref[...] = up_value
    act_ref[...] = (gate_value * jax.nn.sigmoid(gate_value) * up_value).astype(BF16)


def feed_forward(hidden, gate_pieces, up_pieces, cut, columns):
    rows = hidden.shape[0]
    tile = min(512, columns)
    steps = columns // tile
    own = lambda w: pl.BlockSpec((w.shape[0], tile), lambda i: (0, cut * steps + i))
    rest = lambda w: pl.BlockSpec((w.shape[0], tile), lambda i: (0, i))
    specs = [own(gate_pieces[0])] + [rest(w) for w in gate_pieces[1:]]
    out = pl.BlockSpec((rows, tile), lambda i: (0, i))
    return pl.pallas_call(
        functools.partial(feed_forward_body, tuple(w.shape[0] for w in gate_pieces)),
        grid=(steps,),
        in_specs=[whole(hidden)] + specs + specs,
        out_specs=[out] * 3,
        out_shape=[
            jax.ShapeDtypeStruct((rows, columns), F32),
            jax.ShapeDtypeStruct((rows, columns), F32),
            jax.ShapeDtypeStruct((rows, columns), BF16),
        ],
        compiler_params=pltpu.CompilerParams(vmem_limit_bytes=40 << 20),
        cost_estimate=kernel_cost(6 * rows * columns * hidden.shape[1], 8 << 20),
        name="feed_forward",
    )(hidden, *gate_pieces, *up_pieces)


def feed_backward_body(sizes, grad_ref, *refs):
    count = len(sizes)
    gate_ref, up_ref, grad_gate_ref, grad_up_ref = refs[count:]
    grad_act, at = None, 0
    for size, piece in zip(sizes, refs[:count]):
        value = dot_back(grad_ref[:, at : at + size], piece[...])
        grad_act = value if grad_act is None else grad_act + value
        at += size
    gate_value = gate_ref[...]
    sigmoid_gate = jax.nn.sigmoid(gate_value)
    grad_up = grad_act * sigmoid_gate
    grad_gate_ref[...] = (
        grad_up * up_ref[...] * (1.0 + gate_value * (1.0 - sigmoid_gate))
    ).astype(BF16)
    grad_up_ref[...] = (grad_up * gate_value).astype(BF16)


def feed_backward(grad, down_pieces, gate_value, up_value, cut):
    rows, columns = gate_value.shape
    tile = min(512, columns)
    steps = columns // tile
    own = lambda w: pl.BlockSpec((tile, w.shape[1]), lambda i: (cut * steps + i, 0))
    rest = lambda w: pl.BlockSpec((tile, w.shape[1]), lambda i: (i, 0))
    out = pl.BlockSpec((rows, tile), lambda i: (0, i))
    return pl.pallas_call(
        functools.partial(feed_backward_body, tuple(w.shape[1] for w in down_pieces)),
        grid=(steps,),
        in_specs=[whole(grad), own(down_pieces[0])]
        + [rest(w) for w in down_pieces[1:]]
        + [out, out],
        out_specs=[out] * 2,
        out_shape=[jax.ShapeDtypeStruct((rows, columns), BF16)] * 2,
        compiler_params=pltpu.CompilerParams(vmem_limit_bytes=40 << 20),
        cost_estimate=kernel_cost(4 * rows * columns * grad.shape[1], 8 << 20),
        name="feed_backward",
    )(grad, *down_pieces, gate_value, up_value)


def project_body(cuts, steps, terms, pieces, transposed, sibling_ref, *refs):
    first_ref, second_ref, total_ref = refs[-3:]
    step = pl.program_id(0)
    lefts = refs[: cuts * terms]
    weights = refs[cuts * terms : -3]

    @pl.when(step == 0)
    def _():
        total_ref[...] = jnp.zeros_like(total_ref)

    for cut in range(cuts):

        @pl.when(step // steps == cut)
        def _():
            at = 0
            for piece in range(pieces):
                value = None
                for term in range(terms):
                    left = lefts[cut * terms + term][...]
                    weight = weights[(cut * terms + term) * pieces + piece][...]
                    part = dot_back(left, weight) if transposed else dot_rows(left, weight)
                    value = part if value is None else value + part
                total_ref[:, at : at + value.shape[1]] += value
                at += value.shape[1]

    @pl.when(step == cuts * steps - 1)
    def _():
        half = total_ref.shape[0] // 2
        mine = pl.multiple_of(sibling_ref[0] * half, half)
        theirs = pl.multiple_of((1 - sibling_ref[0]) * half, half)
        first_ref[...] = total_ref[pl.ds(theirs, half), :].astype(BF16)
        second_ref[...] = total_ref[pl.ds(mine, half), :]


def project(sibling, lefts, weights, width, transposed):
    cuts, terms, pieces = len(lefts), len(lefts[0]), len(weights[0][0])
    rows, columns = lefts[0][0].shape
    tile = min(512, columns)
    steps = columns // tile
    in_specs = [pl.BlockSpec(memory_space=pltpu.SMEM)]
    operands = []

    def clipped(cut):
        return lambda i: jnp.clip(i - cut * steps, 0, steps - 1)

    for cut in range(cuts):
        for left in lefts[cut]:
            in_specs.append(pl.BlockSpec((rows, tile), lambda i, f=clipped(cut): (0, f(i))))
            operands.append(left)
    for cut in range(cuts):
        for term in weights[cut]:
            for piece, weight in enumerate(term):
                offset = cut * steps if piece == 0 else 0
                if transposed:
                    spec = pl.BlockSpec(
                        (weight.shape[0], tile), lambda i, f=clipped(cut), o=offset: (0, o + f(i))
                    )
                else:
                    spec = pl.BlockSpec(
                        (tile, weight.shape[1]), lambda i, f=clipped(cut), o=offset: (o + f(i), 0)
                    )
                in_specs.append(spec)
                operands.append(weight)
    half_rows = jax.ShapeDtypeStruct((rows // 2, width), BF16)
    return pl.pallas_call(
        functools.partial(project_body, cuts, steps, terms, pieces, transposed),
        grid=(cuts * steps,),
        in_specs=in_specs,
        out_specs=[whole(half_rows)] * 2,
        out_shape=[half_rows, jax.ShapeDtypeStruct((rows // 2, width), F32)],
        scratch_shapes=[pltpu.VMEM((rows, width), F32)],
        compiler_params=pltpu.CompilerParams(vmem_limit_bytes=48 << 20),
        cost_estimate=kernel_cost(3 * terms * rows * columns * cuts * width, 16 << 20),
        name="project",
    )(sibling.reshape(1), *operands)


CHUNK_ROWS, CHUNK_COLUMNS = 256, 1024


def outer_sum_body(split, groups, left_ref, left_other_ref, *refs):
    out_ref = refs[-1]
    rights, others = refs[:groups], refs[groups : 2 * groups]
    blocks = left_ref.shape[1] // CHUNK_ROWS
    for group in range(groups):

        def emit():
            for block in range(blocks):
                rows = slice(block * CHUNK_ROWS, (block + 1) * CHUNK_ROWS)
                value = dot_outer(left_ref[:, rows], rights[group][...])
                value += dot_outer(left_other_ref[:, rows], others[group][...])
                width = value.shape[1]
                out_ref[0, :, block * width : (block + 1) * width] = value.astype(BF16)

        if groups == 1:
            emit()
        else:
            pl.when(pl.program_id(0) // split == group)(emit)


def outer_sum(pool, at, count, left, left_other, rights, rights_other):
    groups = len(rights)
    rows = left.shape[0]
    columns = CHUNK_ROWS * CHUNK_COLUMNS // rights[0].shape[1]
    split = left.shape[1] // columns
    left_spec = pl.BlockSpec((rows, columns), lambda i: (0, lax.rem(i, split)))
    operands = (left, left_other, *rights, *rights_other)
    in_specs = [left_spec] * 2 + [whole(value) for value in operands[2:]]
    aliases = {}
    if pool is not None:
        operands += (pool,)
        in_specs.append(pl.BlockSpec(memory_space=pl.ANY))
        aliases = {len(operands) - 1: 0}
    return pl.pallas_call(
        functools.partial(outer_sum_body, split, groups),
        grid=(split * groups,),
        in_specs=in_specs,
        out_specs=pl.BlockSpec((1, CHUNK_ROWS, CHUNK_COLUMNS), lambda i: (at + i, 0, 0)),
        out_shape=jax.ShapeDtypeStruct((count, CHUNK_ROWS, CHUNK_COLUMNS), BF16),
        input_output_aliases=aliases,
        compiler_params=pltpu.CompilerParams(vmem_limit_bytes=48 << 20),
        cost_estimate=kernel_cost(
            4 * split * groups * rows * CHUNK_ROWS * CHUNK_COLUMNS, 4 << 20
        ),
        name="outer_sum",
    )(*operands)


def widen_body(starts, pool_ref, *out_refs):
    step = pl.program_id(0)
    value = pool_ref[0].astype(F32)
    last = len(starts) - 1
    for at, start in enumerate(starts):
        stop = starts[at + 1] if at < last else pl.num_programs(0)

        @pl.when((step >= start) & (step < stop))
        def _():
            if at < last - 1:
                out_refs[at][...] = value
            elif at == last - 1:
                half = CHUNK_COLUMNS // 2
                out_refs[at][:CHUNK_ROWS] = value[:, :half]
                out_refs[at][CHUNK_ROWS:] = value[:, half:]
            else:
                width = out_refs[at].shape[1]
                for block in range(CHUNK_COLUMNS // (2 * width)):
                    rows = slice(block * CHUNK_ROWS, (block + 1) * CHUNK_ROWS)
                    left = 2 * block * width
                    out_refs[at][rows] = value[:, left : left + width]
                    out_refs[at + 1][rows] = value[:, left + width : left + 2 * width]


def widen(pool, starts, shapes):
    specs = []
    for at, shape in enumerate(shapes):
        which = min(at, len(starts) - 1)
        start = starts[which]
        stop = starts[which + 1] if which + 1 < len(starts) else pool.shape[0]
        size = stop - start
        block = (shape[0] * shape[1] // (size * CHUNK_COLUMNS), CHUNK_COLUMNS)
        if which == len(starts) - 1:
            block = shape
        elif which == len(starts) - 2:
            block = (2 * CHUNK_ROWS, shape[1])
        down = shape[0] // block[0]

        def place(i, start=start, size=size, down=down):
            k = jnp.clip(i - start, 0, size - 1)
            return lax.rem(k, down), k // down

        specs.append(pl.BlockSpec(block, place))
    return pl.pallas_call(
        functools.partial(widen_body, starts),
        grid=(pool.shape[0],),
        in_specs=[pl.BlockSpec((1, CHUNK_ROWS, CHUNK_COLUMNS), lambda i: (i, 0, 0))],
        out_specs=specs,
        out_shape=[jax.ShapeDtypeStruct(shape, F32) for shape in shapes],
        compiler_params=pltpu.CompilerParams(vmem_limit_bytes=48 << 20),
        cost_estimate=kernel_cost(1, 45 << 20),
        name="widen",
    )(pool)


def tail_body(plan, *refs):
    heads, group, lead, starts, count = plan
    (
        pool_in, hidden_m_send, hidden_a_send, feed_chip, stored,
        pool_ref, sum_ref, near_ref, across_ref, feed_land, grad_ref, gain_out_ref,
        gate_land, up_land, hidden_m_land, hidden_a_land, branch_land, mixed_land, qkv_land,
        grad_mixed_ref, dq_ref, dkv_ref, kv_send, kv_land, qkv_grad_ref,
        first_ref, second_ref, core_land, chip_ref, y_land, total_ref, other_ref,
        middle_y, middle_total, middle_other, branch_ref, branch_send,
        own_buf, near_buf, part_buf, across_buf, total_buf, piece_buf,
        x_send, x_recv, tp_send, tp_recv, kv_send_sem, kv_recv_sem,
        send_sem, land_sem, cross_send, cross_land, keep_sem, load_sem, piece_sem,
        loaded, loaded_sem,
    ) = refs
    (
        gate_refs, up_refs, hidden_m_ref, hidden_a_ref, mixed_ref, out_refs,
        query_ref, keys_ref, log_ref, query_seg_ref, key_seg_ref, cosine_ref, sine_ref,
        qkv_refs, inputs_ref, scale_ref, gain_ref, grad_middle_ref,
        middle_chip, cotangent_ref, middle_scale, middle_gain,
    ) = loaded
    stored_gate, stored_up, stored_mixed = stored[0], stored[1], stored[4]
    rows, width = inputs_ref.shape
    half, part = width // 2, width // 4
    half_rows = rows // 2
    mesh_id = pl.DeviceIdType.MESH
    shard, ctx, tp = (lax.axis_index(name) for name in ("fsdp", "ctx", "tp"))
    sibling = lax.rem(tp, 2)
    core = tp + 1 - 2 * sibling
    across_y = lax.rem(tp + 2, 4)
    partner = 1 - shard
    pair = ctx + 1 - 2 * lax.rem(ctx, 2)
    across = 3 - ctx
    is_end = (ctx == 0) | (ctx == 3)
    is_middle = jnp.logical_not(is_end)

    kv_land[...] = jnp.zeros_like(kv_land)
    dkv_ref[...] = jnp.zeros_like(dkv_ref)

    barrier = pltpu.get_barrier_semaphore()
    others = [{"fsdp": partner}, {"tp": core}, {"tp": across_y}]
    others += [{"ctx": lax.rem(ctx + step, 4)} for step in (1, 2, 3)]
    for other in others:
        pl.semaphore_signal(barrier, inc=1, device_id=other, device_id_type=mesh_id)
    pl.semaphore_wait(barrier, len(others))

    def x_copy(at, source, land):
        return pltpu.make_async_remote_copy(
            src_ref=source, dst_ref=land, send_sem=x_send.at[at], recv_sem=x_recv.at[at],
            device_id={"fsdp": partner}, device_id_type=mesh_id,
        )

    cuts = len(gate_refs)
    gate_copies = [x_copy(i, stored_gate[i], gate_land[i]) for i in range(cuts)]
    up_copies = [x_copy(cuts + i, stored_up[i], up_land[i]) for i in range(cuts)]
    hidden_m_copy = x_copy(2 * cuts, hidden_m_send, hidden_m_land)
    branch_copy = x_copy(2 * cuts + 1, branch_send, branch_land)
    mixed_copy = x_copy(2 * cuts + 2, stored_mixed, mixed_land)
    hidden_a_copy = x_copy(2 * cuts + 3, hidden_a_send, hidden_a_land)
    qkv_copy = x_copy(2 * cuts + 4, qkv_grad_ref, qkv_land)
    queue = gate_copies + [hidden_m_copy] + up_copies
    queue += [branch_copy, mixed_copy, qkv_copy, hidden_a_copy]

    def send_next(first, last):
        for at in range(first, last):
            if at >= 2:
                queue[at - 2].wait_send()
            queue[at].start()

    def tp_copy(at, source, land, target):
        return pltpu.make_async_remote_copy(
            src_ref=source, dst_ref=land, send_sem=tp_send.at[at], recv_sem=tp_recv.at[at],
            device_id={"tp": target}, device_id_type=mesh_id,
        )

    split = CHUNK_ROWS // own_buf.shape[0]
    count = count * split

    def share(ref, k):
        size = CHUNK_ROWS // split
        return ref.at[k // split, pl.ds(pl.multiple_of(lax.rem(k, split) * size, size), size), :]

    def to_pair(source, land, k):
        return pltpu.make_async_remote_copy(
            src_ref=source, dst_ref=share(land, k), send_sem=send_sem.at[k],
            recv_sem=land_sem.at[k], device_id={"ctx": pair}, device_id_type=mesh_id,
        )

    def inward_copy(k):
        return to_pair(share(pool_ref, k), near_ref, k)

    def outward_copy(k):
        return to_pair(total_buf.at[lax.rem(k, 2)], sum_ref, k)

    def cross_copy(k):
        return pltpu.make_async_remote_copy(
            src_ref=part_buf.at[lax.rem(k, 4)], dst_ref=share(across_ref, k),
            send_sem=cross_send.at[k], recv_sem=cross_land.at[k],
            device_id={"ctx": across}, device_id_type=mesh_id,
        )

    def keep_copy(k):
        return pltpu.make_async_copy(
            total_buf.at[lax.rem(k, 2)], share(sum_ref, k), keep_sem.at[k]
        )

    def load(source, buffer, at):
        return pltpu.make_async_copy(source, buffer, load_sem.at[at])

    lag = 2

    def inward(k):
        inward_copy(k).wait_recv()
        loads = [load(share(pool_ref, k), own_buf, 0), load(share(near_ref, k), near_buf, 1)]
        for copy in loads:
            copy.start()
        for copy in loads:
            copy.wait()
        part_buf[lax.rem(k, 4)] = (own_buf[...].astype(F32) + near_buf[...].astype(F32)).astype(
            BF16
        )
        cross_copy(k).start()

    def outward(k, reuse):
        cross_copy(k).wait_recv()
        copy = load(share(across_ref, k), across_buf, 2)
        copy.start()
        if reuse:
            keep_copy(k - 2).wait()
            outward_copy(k - 2).wait_send()
        copy.wait()
        total_buf[lax.rem(k, 2)] = (
            part_buf[lax.rem(k, 4)].astype(F32) + across_buf[...].astype(F32)
        ).astype(BF16)
        cross_copy(k).wait_send()
        outward_copy(k).start()
        keep_copy(k).start()

    ahead = 2 * split

    def send_piece(k, carry):
        inward_copy(k).wait_send()

        @pl.when(k + ahead < count)
        def _():
            inward_copy(k + ahead).start()

        return carry

    def pump(first, last):
        pump_steps(first * split, last * split)

    def pump_steps(first, last):

        @pl.when(is_end)
        def _():
            lax.fori_loop(min(first, count), min(last, count), send_piece, 0)

        @pl.when(is_middle)
        def _():
            k = first
            while k < min(last, lag + 2):
                inward(jnp.int32(k))
                if k >= lag:
                    outward(jnp.int32(k - lag), False)
                k += 1
            if k < min(last, count):

                def both(at, carry):
                    inward(at)
                    outward(at - lag, True)
                    return carry

                lax.fori_loop(k, min(last, count), both, 0)
            k = max(k, count)
            while k < min(last, count + lag):
                outward(jnp.int32(k - lag), True)
                k += 1

    @pl.when(is_end)
    def _():
        for k in range(ahead):
            inward_copy(jnp.int32(k)).start()

    send_next(0, 2)
    middle_y_copy = tp_copy(3, stored[-4], middle_y, across_y)
    middle_core_copy = tp_copy(4, middle_total, middle_other, core)
    feed_copy = tp_copy(5, feed_chip, feed_land, across_y)
    middle_y_copy.start()
    fills = [
        pltpu.make_async_copy(source, buffer, loaded_sem.at[at])
        for at, (source, buffer) in enumerate(
            zip(jax.tree.leaves(stored), jax.tree.leaves(loaded))
        )
    ]
    for fill in fills:
        fill.start()
    for fill in fills:
        fill.wait()
    pump_steps(0, 3)

    theirs = pl.multiple_of((1 - sibling) * half_rows, half_rows)
    mine = pl.multiple_of(sibling * half_rows, half_rows)
    step_rows = 64
    odd = lax.rem(ctx, 2)
    near_send = pl.multiple_of(odd * part, part)
    far_send = pl.multiple_of((1 - odd) * part, part)

    def middle_rows(source, base):
        def body(step, total):
            at = pl.multiple_of(step * step_rows, step_rows)
            here = pl.ds(pl.multiple_of(base + at, step_rows), step_rows)
            normed = grad_middle_ref[here, :]
            hidden = source[pl.ds(at, step_rows), :].astype(F32)
            grad = hidden * middle_gain[...]
            mean = jnp.sum(grad * normed, axis=-1, keepdims=True) * (1.0 / width)
            value = cotangent_ref[here, :].astype(F32) + middle_scale[here, :] * (
                grad - normed * mean
            )
            grad_middle_ref[here, :] = value
            low = value.astype(BF16)
            branch_ref[here, :] = low
            branch_send[here, pl.ds(near_send, part)] = low[:, half : half + part]
            branch_send[here, pl.ds(far_send, part)] = low[:, half + part :]
            return total + jnp.sum(hidden * normed, axis=0, keepdims=True)

        return lax.fori_loop(0, half_rows // step_rows, body, jnp.zeros((1, width), F32))

    middle_y_copy.wait_recv()
    middle_total[...] = (middle_chip[...].astype(F32) + middle_y[...].astype(F32)).astype(BF16)
    middle_core_copy.start()
    feed_gain = middle_rows(middle_total, mine)
    pump_steps(3, 4)
    middle_core_copy.wait_recv()
    gain_out_ref[1:2, :] = feed_gain + middle_rows(middle_other, theirs)
    send_next(2, 3)

    grad_mixed = None
    at = 0
    for piece in out_refs:
        value = dot_back(branch_ref[:, at : at + piece.shape[1]], piece[...])
        grad_mixed = value if grad_mixed is None else grad_mixed + value
        at += piece.shape[1]
    grad_mixed_ref[...] = grad_mixed.astype(BF16)

    tile = log_ref.shape[2]
    tiles = rows // tile
    reach = tile + lead

    def attend(step, carry):
        @pl.when(is_end)
        def _():
            send_piece(step + lag + 2, 0)

        @pl.when(is_middle)
        def _():
            inward(step + lag + 2)
            outward(step + 2, True)

        start = pl.multiple_of(step * tile, tile)
        distance = (
            lax.broadcasted_iota(jnp.int32, (reach, tile), 1)
            + lead
            - lax.broadcasted_iota(jnp.int32, (reach, tile), 0)
        )
        same = key_seg_ref[pl.ds(start, reach), :] == query_seg_ref[step]
        bias = jnp.where(same & (distance >= 0) & (distance < WINDOW), 0.0, MASK_FILL)
        query_grad, keys_grad = backward_tile(
            heads,
            group,
            lambda head: query_ref[pl.ds(start, tile), head * HD : (head + 1) * HD],
            lambda head: grad_mixed_ref[pl.ds(start, tile), head * HD : (head + 1) * HD],
            lambda head: log_ref[step, head : head + 1, :],
            lambda at: keys_ref[pl.ds(start, reach), at * HD : (at + 1) * HD],
            bias,
        )
        dq_ref[pl.ds(start, tile), :] = query_grad
        dkv_ref[pl.ds(start, reach), :] += keys_grad
        return carry

    lax.fori_loop(0, tiles, attend, 0)
    send_next(3, 4)

    for back in (1, 2):
        kv_send[back - 1] = dkv_ref[(2 - back) * rows : (3 - back) * rows, :].astype(BF16)

    def kv_copy(back):
        return pltpu.make_async_remote_copy(
            src_ref=kv_send.at[back - 1], dst_ref=kv_land.at[back - 1],
            send_sem=kv_send_sem.at[back - 1], recv_sem=kv_recv_sem.at[back - 1],
            device_id={"ctx": lax.rem(ctx + 4 - back, 4)}, device_id_type=mesh_id,
        )

    for back in (1, 2):

        @pl.when(ctx >= back)
        def _():
            kv_copy(back).start()

    def piece_copy(slot, k):
        return pltpu.make_async_copy(piece_buf.at[slot], pool_ref.at[k], piece_sem.at[slot])

    def put(first, values):
        for at, make in enumerate(values):
            slot = at % 2
            if at >= 2:
                piece_copy(slot, first + at - 2).wait()
            piece_buf[slot] = make()
            piece_copy(slot, first + at).start()
        for at in range(max(0, len(values) - 2), len(values)):
            piece_copy(at % 2, first + at).wait()

    def outer(left, left_other, right, right_other, block):
        columns = slice(block * CHUNK_ROWS, (block + 1) * CHUNK_ROWS)
        return (
            dot_outer(left[:, columns], right[...]) + dot_outer(left_other[:, columns], right_other[...])
        ).astype(BF16)

    def feed_pieces(rights, rights_other):
        return [
            functools.partial(outer, hidden_m_ref, hidden_m_land, right, right_other, block)
            for right, right_other in zip(rights, rights_other)
            for block in range(half // CHUNK_ROWS)
        ]

    pump(4, 5)
    for copy in gate_copies + [hidden_m_copy]:
        copy.wait_recv()
    put(starts[1], feed_pieces(gate_refs, gate_land))
    send_next(4, 5)
    pump(5, 6)

    for back in (1, 2):

        @pl.when(ctx + back < 4)
        def _():
            kv_copy(back).wait_recv()

    kv_width = dkv_ref.shape[1] // 2
    q_width = dq_ref.shape[1]
    cosine, sine = cosine_ref[...], sine_ref[...]
    front = lax.rem(lax.broadcasted_iota(jnp.int32, (rows, LANES), 1), HD) < HD // 2

    def unrotate(value):
        swapped = jnp.where(
            front, pltpu.roll(value, LANES - HD // 2, 1), pltpu.roll(value, HD // 2, 1)
        )
        return (value * cosine - swapped * sine).astype(BF16)

    for at in range(0, q_width, LANES):
        qkv_grad_ref[:, at : at + LANES] = unrotate(dq_ref[:, at : at + LANES])
    kv_sum = dkv_ref[2 * rows :, :]
    for back in range(2):
        kv_sum = kv_sum + kv_land[back].astype(F32)
    for at in range(0, kv_width, LANES):
        qkv_grad_ref[:, q_width + at : q_width + at + LANES] = unrotate(
            kv_sum[:, at : at + LANES]
        )
    qkv_grad_ref[:, q_width + kv_width :] = kv_sum[:, kv_width:].astype(BF16)

    first_copy = tp_copy(0, first_ref, core_land, core)
    y_copy = tp_copy(1, chip_ref, y_land, across_y)
    total_copy = tp_copy(2, total_ref, other_ref, core)

    def back_project(start, store):
        at = 0
        for piece in qkv_refs:
            size = piece.shape[0]
            store(at, size, dot_back(qkv_grad_ref[pl.ds(start, half_rows), :], piece[...]))
            at += size

    def store_first(at, size, value):
        first_ref[:, at : at + size] = value.astype(BF16)

    def store_second(at, size, value):
        second_ref[:, at : at + size] = value

    back_project(theirs, store_first)
    first_copy.start()
    back_project(mine, store_second)
    pump(6, 8)
    first_copy.wait_recv()
    chip_ref[...] = (second_ref[...] + core_land[...].astype(F32)).astype(BF16)
    y_copy.start()
    send_next(5, 6)
    pump(8, 10)


    y_copy.wait_recv()
    total_ref[...] = (chip_ref[...].astype(F32) + y_land[...].astype(F32)).astype(BF16)
    total_copy.start()
    feed_copy.start()
    gain = gain_ref[...]
    near_at = pl.multiple_of((1 - shard) * half + lax.rem(ctx, 2) * part, part)
    far_at = pl.multiple_of((1 - shard) * half + (1 - lax.rem(ctx, 2)) * part, part)
    own_at = pl.multiple_of(shard * half, half)

    def norm_rows(source, base):
        def body(step, total):
            at = pl.multiple_of(step * step_rows, step_rows)
            here = pl.ds(pl.multiple_of(base + at, step_rows), step_rows)
            scale = scale_ref[here, :]
            normed = inputs_ref[here, :].astype(F32) * scale
            hidden = source[pl.ds(at, step_rows), :].astype(F32)
            grad = hidden * gain
            mean = jnp.sum(grad * normed, axis=-1, keepdims=True) * (1.0 / width)
            value = (grad_middle_ref[here, :] + scale * (grad - normed * mean)).astype(BF16)
            grad_ref[here, pl.ds(own_at, half)] = value[:, :half]
            grad_ref[here, pl.ds(near_at, part)] = value[:, half : half + part]
            grad_ref[here, pl.ds(far_at, part)] = value[:, half + part :]
            return total + jnp.sum(hidden * normed, axis=0, keepdims=True)

        return lax.fori_loop(0, half_rows // step_rows, body, jnp.zeros((1, width), F32))

    gain_sum = norm_rows(total_ref, mine)
    pump(10, 11)
    send_next(6, 7)
    total_copy.wait_recv()
    gain_out_ref[0:1, :] = gain_sum + norm_rows(other_ref, theirs)
    pump(11, 12)
    for copy in up_copies:
        copy.wait_recv()
    put(starts[2], feed_pieces(up_refs, up_land))
    send_next(7, 8)
    pump(12, 14)
    send_next(8, len(queue))
    branch_copy.wait_recv()
    mixed_copy.wait_recv()
    put(
        starts[3],
        [
            functools.partial(
                outer, mixed_ref, mixed_land, branch_ref.at[:, :half], branch_land, block
            )
            for block in range(q_width // CHUNK_ROWS)
        ],
    )
    pump(14, 17)
    hidden_a_copy.wait_recv()
    qkv_copy.wait_recv()

    def side_by_side(first, number, columns):
        return jnp.concatenate(
            [
                outer(
                    hidden_a_ref, hidden_a_land, qkv_grad_ref.at[:, columns],
                    qkv_land.at[:, columns], block,
                )
                for block in range(first, first + number)
            ],
            axis=1,
        )

    q_blocks = CHUNK_COLUMNS // q_width
    put(
        starts[4],
        [
            functools.partial(side_by_side, first, q_blocks, slice(0, q_width))
            for first in range(0, half // CHUNK_ROWS, q_blocks)
        ]
        + [
            functools.partial(
                side_by_side, 0, half // CHUNK_ROWS, slice(q_width, q_width + 2 * kv_width)
            )
        ],
    )
    pump(17, count // split + lag)

    feed_copy.wait_recv()
    for copy in queue[-2:] + [first_copy, y_copy, total_copy]:
        copy.wait_send()
    for copy in (middle_y_copy, middle_core_copy, feed_copy):
        copy.wait_send()
    for back in (1, 2):

        @pl.when(ctx >= back)
        def _():
            kv_copy(back).wait_send()

    @pl.when(is_middle)
    def _():
        for k in (count - 2, count - 1):
            outward_copy(jnp.int32(k)).wait_send()
            keep_copy(jnp.int32(k)).wait()

    @pl.when(is_end)
    def _():
        def close(k, carry):
            to_pair(share(pool_ref, k), sum_ref, k).wait_recv()
            return carry

        lax.fori_loop(0, count, close, 0)


def flat_call(body, operands, **call):
    flat, tree = jax.tree.flatten(operands)

    def unflatten(*refs):
        body(*jax.tree.unflatten(tree, refs[: len(flat)]), *refs[len(flat) :])

    in_specs = [pl.BlockSpec(memory_space=pl.ANY)] * len(flat)
    return pl.pallas_call(unflatten, in_specs=in_specs, **call)(*flat)


def tail(plan, pool, v):
    heads, group, lead, starts, count = plan
    rows, width = v["inputs"].shape
    half = width // 2
    q_width, kv_width = v["query"].shape[1], v["keys_values"].shape[1] // 2
    qkv_width = q_width + 2 * kv_width
    piece = (CHUNK_ROWS, CHUNK_COLUMNS)
    split = 2
    step, steps = (CHUNK_ROWS // split, CHUNK_COLUMNS), count * split
    cuts, feed_part = len(v["grad_gate"]), v["grad_gate"][0].shape[1]

    stored = [
        v["grad_gate"], v["grad_up"], v["hidden_m"], v["hidden_a"], v["mixed"],
        v["out_pieces"], v["query"], v["keys_values"], v["log_sums"], v["query_segments"],
        v["key_segments"], v["cosine"], v["sine"], v["qkv_pieces"], v["inputs"], v["scale"],
        v["gain"], v["normed_m"], v["middle_chip"], v["cotangent"], v["middle_scale"],
        v["middle_gain"],
    ]
    operands = [pool, v["hidden_m_send"], v["hidden_a_send"], v["feed_chip"], stored]
    loaded = jax.tree.map(lambda value: pltpu.VMEM(value.shape, value.dtype), stored)
    any_space, vmem_space = pl.BlockSpec(memory_space=pl.ANY), pl.BlockSpec(memory_space=pltpu.VMEM)
    line = jax.ShapeDtypeStruct((count,) + piece, BF16)
    dma = pltpu.SemaphoreType.DMA
    low = lambda *shape: pltpu.VMEM(shape, BF16)
    wide = lambda *shape: pltpu.VMEM(shape, F32)
    scratch = [
        [low(rows, feed_part) for _ in range(cuts)],
        [low(rows, feed_part) for _ in range(cuts)],
        low(rows, half), low(rows, half), low(rows, half),
        low(rows, q_width), low(rows, qkv_width),
        low(rows, q_width), wide(rows, q_width), wide(3 * rows, 2 * kv_width),
        low(2, rows, 2 * kv_width), low(2, rows, 2 * kv_width), low(rows, qkv_width),
        low(rows // 2, width), wide(rows // 2, width), low(rows // 2, width),
        low(rows // 2, width), low(rows // 2, width), low(rows // 2, width),
        low(rows // 2, width),
        low(rows // 2, width), low(rows // 2, width), low(rows // 2, width),
        low(rows, width), low(rows, half),
        low(*step), low(*step), low(4, *step), low(*step), low(2, *step), low(2, *piece),
        dma((2 * cuts + 5,)), dma((2 * cuts + 5,)), dma((6,)), dma((6,)), dma((2,)), dma((2,)),
        dma((steps,)), dma((steps,)), dma((steps,)), dma((steps,)), dma((steps,)),
        dma((3,)), dma((2,)),
        loaded, dma((len(jax.tree.leaves(stored)),)),
    ]
    outs = flat_call(
        functools.partial(tail_body, plan),
        operands,
        out_specs=[any_space] * 5 + [vmem_space, vmem_space],
        out_shape=[
            line, line, line, line,
            jax.ShapeDtypeStruct((rows // 2, width), BF16),
            jax.ShapeDtypeStruct((rows, width), BF16),
            jax.ShapeDtypeStruct((2, width), F32),
        ],
        scratch_shapes=scratch,
        input_output_aliases={0: 0},
        compiler_params=pltpu.CompilerParams(
            collective_id=0, has_side_effects=True, vmem_limit_bytes=62 << 20
        ),
        cost_estimate=pl.CostEstimate(
            flops=400 << 30, bytes_accessed=30 << 20, transcendentals=0
        ),
        name="tail",
    )
    return outs[1], outs[4], outs[5], outs[6]


def swap(value, axis, size, bit):
    return lax.ppermute(value, axis, [(i, i ^ bit) for i in range(size)])


def shift(value, axis, size, by):
    if abs(by) >= size:
        return jnp.zeros_like(value)
    return lax.ppermute(
        value, axis, [(i, i + by) for i in range(size) if 0 <= i + by < size]
    )


class Lane:
    def __init__(self, move, depth=2):
        self.move, self.depth, self.done = move, depth, []

    def send(self, value):
        if len(self.done) >= self.depth:
            value, self.done[-self.depth] = tie(value, self.done[-self.depth])
        self.done.append(self.move(value))
        return len(self.done) - 1

    def get(self, at):
        return self.done[at]


def shards(
    sizes,
    block_input,
    segment_ids,
    attention_gain,
    query_weight,
    key_weight,
    value_weight,
    out_weight,
    feed_gain,
    gate_weight,
    up_weight,
    down_weight,
    cotangent,
):
    shard_count, ctx_count, tp_count = sizes
    seqs, span, width = block_input.shape
    rows = seqs * span
    seq_length = segment_ids.shape[1]
    half = width // 2
    part = half // 2
    q_width = query_weight.shape[1]
    kv_width = key_weight.shape[1]
    feed_width = gate_weight.shape[1]
    group = q_width // kv_width
    shard, ctx, tp = (lax.axis_index(name) for name in ("fsdp", "ctx", "tp"))
    odd = ctx % 2
    sibling = tp % 2

    own_at = shard * half
    near_at = (1 - shard) * half + odd * part
    far_at = (1 - shard) * half + (1 - odd) * part

    def to_local(value):
        return jnp.concatenate(
            [
                take(value, own_at, half, 1),
                take(value, near_at, part, 1),
                take(value, far_at, part, 1),
            ],
            axis=1,
        )

    def other_half(value):
        return jnp.concatenate(
            [
                take(value, half + odd * part, part, 1),
                take(value, half + (1 - odd) * part, part, 1),
            ],
            axis=1,
        )

    def from_local(value):
        own, other = value[:, :half], other_half(value)
        return jnp.where(
            shard == 0,
            jnp.concatenate([own, other], axis=1),
            jnp.concatenate([other, own], axis=1),
        )

    fsdp_lane = Lane(lambda value: swap(value, "fsdp", shard_count, 1))

    def over_fsdp(value):
        return swap(value, "fsdp", shard_count, 1)

    def over_ctx(value):
        return swap(value, "ctx", ctx_count, 1)

    def near_part(weight, axis):
        return take(weight, odd * part, part, axis)

    def core_half(value):
        return take(value, sibling * (rows // 2), rows // 2, 0)

    def join_cores(mine):
        other = swap(mine, "tp", tp_count, 1)
        return jnp.where(
            sibling == 0,
            jnp.concatenate([mine, other], axis=0),
            jnp.concatenate([other, mine], axis=0),
        )

    def chip_sum(first, second):
        return (second + swap(first, "tp", tp_count, 1).astype(F32)).astype(BF16)

    def finish_sum(chip):
        total = (chip.astype(F32) + swap(chip, "tp", tp_count, 2).astype(F32)).astype(BF16)
        return join_cores(total).astype(F32)

    def tp_sum(first, second):
        if tp_count != 4:
            whole_rows = jnp.where(
                sibling == 0,
                jnp.concatenate([second, first.astype(F32)], axis=0),
                jnp.concatenate([first.astype(F32), second], axis=0),
            )
            return lax.psum(whole_rows, "tp")
        return finish_sum(chip_sum(first, second))

    gains_own = jnp.stack([attention_gain, feed_gain])
    qkv_own = jnp.concatenate([query_weight, key_weight, value_weight], axis=1)
    feed_cuts = 2
    feed_part = feed_width // feed_cuts
    columns = [slice(cut * feed_part, (cut + 1) * feed_part) for cut in range(feed_cuts)]
    grad_rows = to_local(cotangent.reshape(rows, width))
    send_gate = [near_part(gate_weight[:, cut], 0) for cut in columns]
    send_up = [near_part(up_weight[:, cut], 0) for cut in columns]
    send_down = [near_part(down_weight[cut], 1) for cut in columns]
    send_grad = core_half(other_half(grad_rows))

    gains_other = over_fsdp(gains_own)
    near_qkv = over_fsdp(near_part(qkv_own, 0))
    gains_other, send_out = tie(gains_other, near_part(out_weight, 1))
    near_out = over_fsdp(send_out)

    span_start = ctx * span
    positions = take(doc_positions(segment_ids), span_start, span, 1).reshape(rows)
    query_segments = take(segment_ids, span_start, span, 1)
    cosine, sine = rope_tables(positions)
    blocks_back, base, lead = attention_plan(span, WINDOW)
    key_segments = take(
        jnp.pad(segment_ids, ((0, 0), (blocks_back * span, 0)), constant_values=-1),
        span_start,
        (blocks_back + 1) * span,
        1,
    )

    inputs = to_local(block_input.reshape(rows, width)).astype(F32)
    scale_a = row_scale_of(inputs)
    normed_a = inputs * scale_a
    gains = jnp.concatenate(
        [gains_own, take(gains_other, odd * part, part, 1), take(gains_other, (1 - odd) * part, part, 1)],
        axis=1,
    ).astype(F32)
    gain_a, gain_m = gains[0:1], gains[1:2]
    hidden_a = (normed_a * gain_a).astype(BF16)

    near_qkv, send_gate[0] = tie(near_qkv, send_gate[0])
    near_gate, near_up, far_gate, far_up = ([None] * feed_cuts for _ in range(4))
    near_gate[0] = over_fsdp(send_gate[0])
    far_qkv = over_ctx(near_qkv)
    near_out, send_up[0] = tie(near_out, send_up[0])
    near_up[0] = over_fsdp(send_up[0])
    far_qkv, near_out = tie(far_qkv, near_out)
    far_out = over_ctx(near_out)

    def dot_pieces(matrix, own, near, far):
        return (
            dot_rows(matrix[:, :half], own)
            + dot_rows(matrix[:, half : half + part], near)
            + dot_rows(matrix[:, half + part :], far)
        )

    def back_pieces(matrix, own, near, far):
        return jnp.concatenate(
            [dot_back(matrix, own), dot_back(matrix, near), dot_back(matrix, far)], axis=1
        )

    qkv = dot_pieces(hidden_a, qkv_own, near_qkv, far_qkv)
    key_low = rotate(qkv[:, q_width : q_width + kv_width], cosine, sine).astype(BF16)
    value_low = qkv[:, q_width + kv_width :].astype(BF16)
    keys_values = jnp.concatenate([key_low, value_low], axis=1).reshape(seqs, span, 2 * kv_width)
    query_low = (rotate(qkv[:, :q_width], cosine, sine).astype(BF16) * HD**-0.5).reshape(
        seqs, span, q_width
    )
    earlier = [shift(keys_values, "ctx", ctx_count, back) for back in range(blocks_back, 0, -1)]
    *earlier, query_low = tie(*earlier, query_low)
    keys_values = jnp.concatenate(earlier + [keys_values], axis=1)
    mixed, log_sums = attend_forward(
        query_low, keys_values, query_segments, key_segments, base, lead, group
    )
    mixed_low = mixed.reshape(rows, q_width)
    mixed_low, far_out, near_gate[0], near_up[0], send_gate[1], send_up[1] = tie(
        mixed_low, far_out, near_gate[0], near_up[0], send_gate[1], send_up[1]
    )
    near_gate[1] = over_fsdp(send_gate[1])
    far_gate[0] = over_ctx(near_gate[0])
    near_up[1] = over_fsdp(send_up[1])
    far_up[0] = over_ctx(near_up[0])

    def out_project(at):
        matrix = take(mixed_low, at * (rows // 2), rows // 2, 0)
        return jnp.concatenate(
            [dot_rows(matrix, out_weight), dot_rows(matrix, near_out), dot_rows(matrix, far_out)],
            axis=1,
        )

    first, second = out_project(1 - sibling).astype(BF16), out_project(sibling)
    if tp_count == 4:
        chip = chip_sum(first, second)
        total = (chip.astype(F32) + swap(chip, "tp", tp_count, 2).astype(F32)).astype(BF16)
        total, near_gate[1], far_gate[0] = tie(total, near_gate[1], far_gate[0])
        branch_a = join_cores(total).astype(F32)
    else:
        branch_a = tp_sum(first, second)
    far_gate[1] = over_ctx(near_gate[1])
    middle = inputs + branch_a

    scale_m = row_scale_of(middle)
    normed_m = middle * scale_m
    hidden_m = (normed_m * gain_m).astype(BF16)
    hidden_m, near_up[1], far_up[0], send_down[0] = tie(
        hidden_m, near_up[1], far_up[0], send_down[0]
    )
    near_down = [over_fsdp(send_down[0])]
    far_up[1] = over_ctx(near_up[1])
    gate_cuts, up_cuts, act_cuts = [], [], []

    def feed(cut):
        gate_value, up_value, activated = feed_forward(
            hidden_m,
            (gate_weight, near_gate[cut], far_gate[cut]),
            (up_weight, near_up[cut], far_up[cut]),
            cut,
            feed_part,
        )
        gate_cuts.append(gate_value)
        up_cuts.append(up_value)
        act_cuts.append(activated)

    feed(0)
    act_cuts[0], near_down[0], far_gate[1], send_down[1] = tie(
        act_cuts[0], near_down[0], far_gate[1], send_down[1]
    )
    near_down.append(over_fsdp(send_down[1]))
    far_down = [over_ctx(near_down[0])]
    feed(1)
    act_cuts[1], near_down[1], send_grad, act_cuts[0] = tie(
        act_cuts[1], near_down[1], send_grad, act_cuts[0]
    )
    other_grad = over_fsdp(send_grad)
    act_other = [over_fsdp(act_cuts[0]), over_fsdp(act_cuts[1])]
    far_down.append(over_ctx(near_down[1]))

    pieces = CHUNK_ROWS * CHUNK_COLUMNS
    down_count = feed_width * half // pieces
    starts, pool_size = [], 0
    for size in (feed_width * half,) * 3 + (q_width * half,) * 2 + (2 * kv_width * half,):
        starts.append(pool_size)
        pool_size += size // pieces
    grad_gate_cuts, grad_up_cuts = [], []
    for cut in range(feed_cuts):
        grad_gate, grad_up = feed_backward(
            grad_rows,
            (down_weight, near_down[cut], far_down[cut]),
            gate_cuts[cut],
            up_cuts[cut],
            cut,
        )
        grad_gate_cuts.append(grad_gate)
        grad_up_cuts.append(grad_up)

    grad_gate_cuts[1], act_other[0], other_grad = tie(
        grad_gate_cuts[1], act_other[0], other_grad
    )
    grad_own, grad_other = grad_rows[:, :half], join_cores(other_grad)
    first, second = project(
        sibling,
        list(zip(grad_gate_cuts, grad_up_cuts)),
        [
            (
                (gate_weight, near_gate[cut], far_gate[cut]),
                (up_weight, near_up[cut], far_up[cut]),
            )
            for cut in range(feed_cuts)
        ],
        width,
        True,
    )
    first, second, act_other[1], *act_cuts = tie(first, second, act_other[1], *act_cuts)
    fused = (shard_count, ctx_count, tp_count) == (2, 4, 4)
    fused = fused and seqs == 1 and (blocks_back, base, span) == (2, 0, 4 * LANES)
    if fused:
        middle_chip = chip_sum(first, second)
    else:
        grad_hidden_m = tp_sum(first, second)
    fsdp_lane.done = list(act_other)
    pool = None
    for cut in range(feed_cuts):
        pool = outer_sum(
            pool,
            cut * down_count // feed_cuts,
            pool_size,
            act_cuts[cut],
            act_other[cut],
            [grad_own],
            [grad_other],
        )

    first, second = project(
        sibling,
        [(value,) for value in act_cuts],
        [((down_weight, near_down[cut], far_down[cut]),) for cut in range(feed_cuts)],
        width,
        False,
    )
    if fused:
        feed_chip = chip_sum(first, second)
    else:
        branch_m = tp_sum(first, second)

    if fused:
        tile = min(LANES, rows)
        log_rows = jnp.swapaxes(log_sums[0, :, : q_width // HD].reshape(rows // tile, tile, -1), 1, 2)
        pool, across, input_grad, gain_rows = tail(
            (
                q_width // HD,
                group,
                lead,
                tuple(starts),
                pool_size,
            ),
            pool,
            {
                "grad_gate": grad_gate_cuts,
                "grad_up": grad_up_cuts,
                "hidden_m": hidden_m[:, :half],
                "hidden_m_send": other_half(hidden_m),
                "hidden_a": hidden_a[:, :half],
                "hidden_a_send": other_half(hidden_a),
                "mixed": mixed_low,
                "out_pieces": [out_weight, near_out, far_out],
                "query": query_low[0],
                "keys_values": keys_values[0],
                "log_sums": log_rows,
                "query_segments": query_segments.reshape(rows // tile, 1, tile),
                "key_segments": key_segments.reshape(-1, 1),
                "cosine": cosine,
                "sine": sine,
                "qkv_pieces": [qkv_own, near_qkv, far_qkv],
                "inputs": inputs.astype(BF16),
                "scale": scale_a,
                "gain": gain_a,
                "normed_m": normed_m,
                "middle_chip": middle_chip,
                "cotangent": grad_rows,
                "middle_scale": scale_m,
                "middle_gain": gain_m,
                "feed_chip": feed_chip,
            },
        )
        attention_gain_part, feed_gain_part = gain_rows[0], gain_rows[1]
        input_grad = input_grad.reshape(seqs, span, width)
        total = (feed_chip.astype(F32) + across.astype(F32)).astype(BF16)
        branch_m = join_cores(total).astype(F32)
    else:
        feed_gain_part = jnp.sum(grad_hidden_m * normed_m, axis=0)
        grad_middle = norm_back(grad_hidden_m, gain_m, normed_m, scale_m, grad_rows.astype(F32))
        grad_branch = grad_middle.astype(BF16)
        gate_at = [fsdp_lane.send(value) for value in grad_gate_cuts]
        up_at = [fsdp_lane.send(value) for value in grad_up_cuts]
        hidden_m_at = fsdp_lane.send(core_half(other_half(hidden_m)))
        hidden_own, hidden_other = hidden_m[:, :half], join_cores(fsdp_lane.get(hidden_m_at))
        for which, (own, at) in enumerate(((grad_gate_cuts, gate_at), (grad_up_cuts, up_at))):
            pool = outer_sum(
                pool,
                starts[1 + which],
                pool_size,
                hidden_own,
                hidden_other,
                own,
                [fsdp_lane.get(i) for i in at],
            )

        grad_mixed = (
            dot_back(grad_branch[:, :half], out_weight)
            + dot_back(grad_branch[:, half : half + part], near_out)
            + dot_back(grad_branch[:, half + part :], far_out)
        ).astype(BF16)
        branch_at = fsdp_lane.send(core_half(other_half(grad_branch)))
        mixed_at = fsdp_lane.send(mixed_low)
        hidden_a_at = fsdp_lane.send(core_half(other_half(hidden_a)))
        grad_query, grad_keys_values = attend_backward(
            query_low,
            keys_values,
            grad_mixed.reshape(seqs, span, q_width),
            jnp.swapaxes(log_sums, 1, 2)[:, : q_width // HD],
            query_segments,
            key_segments,
            base,
            lead,
            group,
        )
        kv_sum = grad_keys_values[:, blocks_back * span :]
        for back in range(1, blocks_back + 1):
            at = (blocks_back - back) * span
            kv_sum = kv_sum + shift(
                grad_keys_values[:, at : at + span].astype(BF16), "ctx", ctx_count, -back
            ).astype(F32)
        kv_sum = kv_sum.reshape(rows, 2 * kv_width)
        grad_qkv = jnp.concatenate(
            [
                rotate(grad_query.reshape(rows, q_width), cosine, -sine),
                rotate(kv_sum[:, :kv_width], cosine, -sine),
                kv_sum[:, kv_width:],
            ],
            axis=1,
        ).astype(BF16)
        qkv_at = fsdp_lane.send(grad_qkv)
        first, second = (
            back_pieces(take(grad_qkv, at * (rows // 2), rows // 2, 0), qkv_own, near_qkv, far_qkv)
            for at in (1 - sibling, sibling)
        )
        grad_hidden_a = tp_sum(first.astype(BF16), second)
        attention_gain_part = jnp.sum(grad_hidden_a * normed_a, axis=0)
        input_grad = norm_back(grad_hidden_a, gain_a, normed_a, scale_a, grad_middle)
        input_grad = from_local(input_grad.astype(BF16)).reshape(seqs, span, width)

        pool = outer_sum(
            pool,
            starts[3],
            pool_size,
            mixed_low,
            fsdp_lane.get(mixed_at),
            [grad_branch[:, :half]],
            [join_cores(fsdp_lane.get(branch_at))],
        )
        qkv_other = fsdp_lane.get(qkv_at)
        hidden_own, hidden_other = hidden_a[:, :half], join_cores(fsdp_lane.get(hidden_a_at))
        for which, cut in ((4, slice(0, q_width)), (5, slice(q_width, None))):
            pool = outer_sum(
                pool,
                starts[which],
                pool_size,
                hidden_own,
                hidden_other,
                [grad_qkv[:, cut]],
                [qkv_other[:, cut]],
            )
        pool = lax.psum(pool.astype(F32), "ctx")

    block_out = from_local((middle + branch_m).astype(BF16)).reshape(seqs, span, width)

    gain_parts = jnp.stack([attention_gain_part, feed_gain_part])
    gain_other = over_fsdp(other_half(gain_parts))
    gain_sums = lax.psum(gain_parts[:, :half] + gain_other, "ctx")

    down_grad, gate_grad, up_grad, out_grad, query_grad, key_grad, value_grad = widen(
        pool,
        starts,
        [
            down_weight.shape,
            gate_weight.shape,
            up_weight.shape,
            out_weight.shape,
            query_weight.shape,
            key_weight.shape,
            value_weight.shape,
        ],
    )
    return (
        block_out,
        input_grad,
        gain_sums[0],
        query_grad,
        key_grad,
        value_grad,
        out_grad,
        gain_sums[1],
        gate_grad,
        up_grad,
        down_grad,
    )


def solution(mesh):
    sizes = tuple(mesh.shape[name] for name in ("fsdp", "ctx", "tp"))
    in_specs = (
        P("fsdp", "ctx", None),
        P("fsdp", None),
        P("fsdp"),
        P("fsdp", "tp"),
        P("fsdp", "tp"),
        P("fsdp", "tp"),
        P("tp", "fsdp"),
        P("fsdp"),
        P("fsdp", "tp"),
        P("fsdp", "tp"),
        P("tp", "fsdp"),
        P("fsdp", "ctx", None),
    )
    out_specs = (
        P("fsdp", "ctx", None),
        P("fsdp", "ctx", None),
        P("fsdp"),
        P("fsdp", "tp"),
        P("fsdp", "tp"),
        P("fsdp", "tp"),
        P("tp", "fsdp"),
        P("fsdp"),
        P("fsdp", "tp"),
        P("fsdp", "tp"),
        P("tp", "fsdp"),
    )
    return jax.shard_map(
        functools.partial(shards, sizes),
        mesh=mesh,
        in_specs=in_specs,
        out_specs=out_specs,
        check_vma=False,
    )
```

```python
import functools

import jax
import jax.numpy as jnp
from jax import lax
from jax.experimental import pallas as pl
from jax.experimental.pallas import tpu as pltpu
from jax.sharding import PartitionSpec as P

HD = 64
WINDOW = 1024
NORM_EPS = 1e-05
ROPE_BASE = 500000.0
MASK_FILL = -1e30
LANES = 128
F32 = jnp.float32
BF16 = jnp.bfloat16


def dot_rows(matrix, other_side):
    return jnp.dot(matrix, other_side, preferred_element_type=F32)


def dot_back(matrix, other_side):
    return lax.dot_general(matrix, other_side, (((1,), (1,)), ((), ())), preferred_element_type=F32)


def dot_outer(matrix, other_side):
    return lax.dot_general(matrix, other_side, (((0,), (0,)), ((), ())), preferred_element_type=F32)


def tie(*values):
    return lax.optimization_barrier(values)


def take(array, start, size, axis):
    return lax.dynamic_slice_in_dim(array, start, size, axis)


def doc_positions(segments):
    seq_count, seq_length = segments.shape
    index_grid = jnp.broadcast_to(jnp.arange(seq_length, dtype=jnp.int32)[None, :], segments.shape)
    begins = jnp.concatenate(
        [jnp.ones((seq_count, 1), dtype=bool), segments[:, 1:] != segments[:, :-1]], axis=1
    )
    return index_grid - lax.cummax(jnp.where(begins, index_grid, 0), axis=1)


def rope_tables(positions):
    half_size = HD // 2
    frequency = ROPE_BASE ** (-(jnp.arange(half_size, dtype=F32) * 2.0 / HD))
    angles = positions.astype(F32)[:, None] * frequency
    cosine, sine = jnp.cos(angles), jnp.sin(angles)
    return jnp.concatenate([cosine] * 4, axis=1), jnp.concatenate([-sine, sine] * 2, axis=1)


def rotate(vectors, cosine, signed_sine):
    width = vectors.shape[1]
    half = HD // 2
    ahead = jnp.concatenate([vectors[:, half:], vectors[:, :half]], axis=1)
    behind = jnp.concatenate([vectors[:, -half:], vectors[:, :-half]], axis=1)
    first = (jnp.arange(width) % HD < half)[None, :]
    reps = width // LANES
    return vectors * jnp.tile(cosine, (1, reps)) + jnp.where(first, ahead, behind) * jnp.tile(
        signed_sine, (1, reps)
    )


def row_scale_of(values):
    return lax.rsqrt(jnp.mean(values * values, axis=-1, keepdims=True) + NORM_EPS)


def norm_back(grad_hidden, gain, normed, row_scale, residual_grad):
    grad_normed = grad_hidden * gain
    return residual_grad + row_scale * (
        grad_normed - normed * jnp.mean(grad_normed * normed, axis=-1, keepdims=True)
    )


def attend_forward_body(lead, heads, group, q_ref, kv_ref, qseg_ref, kseg_ref, mixed_ref, lse_ref):
    block = q_ref.shape[1]
    reach = kseg_ref.shape[-1]
    start = pl.multiple_of(pl.program_id(1) * block, block)
    window = kv_ref.at[0, pl.ds(start, reach), :]
    distance = (
        lax.broadcasted_iota(jnp.int32, (block, reach), 0)
        + lead
        - lax.broadcasted_iota(jnp.int32, (block, reach), 1)
    )
    allowed = (qseg_ref[0] == kseg_ref[0, 0]) & (distance >= 0) & (distance < WINDOW)
    bias = jnp.where(allowed, 0.0, MASK_FILL)
    lane = lax.broadcasted_iota(jnp.int32, (block, LANES), 1)
    log_sums = jnp.zeros((block, LANES), F32)
    kv_width = heads // group * HD
    outs = []
    for head in range(heads):
        shared = head // group * HD
        keys = window[:, shared : shared + HD]
        values = window[:, kv_width + shared : kv_width + shared + HD]
        scores = dot_back(q_ref[0, :, head * HD : (head + 1) * HD], keys) + bias
        row_max = jnp.max(scores, axis=-1, keepdims=True)
        exponent = jnp.exp(scores - row_max)
        row_total = jnp.sum(exponent, axis=-1, keepdims=True)
        probs = (exponent * (1.0 / row_total)).astype(BF16)
        outs.append(dot_rows(probs, values))
        log_sums = jnp.where(lane == head, row_max + jnp.log(row_total), log_sums)
    mixed_ref[0] = jnp.concatenate(outs, axis=1).astype(BF16)
    lse_ref[0] = log_sums


def attend_backward_body(
    lead, heads, group, q_ref, kv_ref, grad_ref, lse_ref, qseg_ref, kseg_ref, dq_ref, dkv_ref
):
    block = q_ref.shape[1]
    reach = block + lead
    step = pl.program_id(1)
    start = pl.multiple_of(step * block, block)
    window = kv_ref.at[0, pl.ds(start, reach), :]

    @pl.when(step == 0)
    def _():
        dkv_ref[...] = jnp.zeros_like(dkv_ref)

    distance = (
        lax.broadcasted_iota(jnp.int32, (reach, block), 1)
        + lead
        - lax.broadcasted_iota(jnp.int32, (reach, block), 0)
    )
    same = kseg_ref[0, pl.ds(start, reach), :] == qseg_ref[0]
    bias = jnp.where(same & (distance >= 0) & (distance < WINDOW), 0.0, MASK_FILL)
    query_grad, keys_grad = backward_tile(
        heads,
        group,
        lambda head: q_ref[0, :, head * HD : (head + 1) * HD],
        lambda head: grad_ref[0, :, head * HD : (head + 1) * HD],
        lambda head: lse_ref[0, head : head + 1, :],
        lambda at: window[:, at * HD : (at + 1) * HD],
        bias,
    )
    dq_ref[0] = query_grad
    dkv_ref[0, pl.ds(start, reach), :] += keys_grad


def backward_tile(heads, group, query_of, grad_of, log_sum_of, window_of, bias):
    key_grads, value_grads, query_grads = [], [], []
    shared_heads = heads // group
    for shared in range(shared_heads):
        keys, values = window_of(shared), window_of(shared_heads + shared)
        key_sum = value_sum = None
        for member in range(group):
            head = shared * group + member
            query, grad = query_of(head), grad_of(head)
            probs = jnp.exp(dot_back(keys, query) + bias - log_sum_of(head))
            grad_probs = dot_back(values, grad)
            spread = jnp.sum(probs * grad_probs, axis=0, keepdims=True)
            grad_scores = (probs * (grad_probs - spread)).astype(BF16)
            value_part = dot_rows(probs.astype(BF16), grad)
            key_part = dot_rows(grad_scores, query)
            query_grads.append(dot_outer(grad_scores, keys) * HD**-0.5)
            value_sum = value_part if value_sum is None else value_sum + value_part
            key_sum = key_part if key_sum is None else key_sum + key_part
        key_grads.append(key_sum)
        value_grads.append(value_sum)
    return jnp.concatenate(query_grads, axis=1), jnp.concatenate(key_grads + value_grads, axis=1)


def attention_plan(span, window):
    blocks_back = -(-(window - 1) // span)
    base = (blocks_back * span - (window - 1)) // LANES * LANES
    return blocks_back, base, blocks_back * span - base


def key_tiles(key_segments, base, lead, block, span):
    return jnp.stack(
        [
            key_segments[:, base + at : base + at + block + lead]
            for at in range(0, span, block)
        ],
        axis=1,
    )[:, :, None, :]


def attend_forward(query, keys_values, query_segments, key_segments, base, lead, group):
    seqs, span, width = query.shape
    block = min(LANES, span)
    heads = width // HD
    reach = block + lead
    keys_used = keys_values[:, base:]
    return pl.pallas_call(
        functools.partial(attend_forward_body, lead, heads, group),
        grid=(seqs, span // block),
        in_specs=[
            pl.BlockSpec((1, block, width), lambda s, i: (s, i, 0)),
            pl.BlockSpec((1,) + keys_used.shape[1:], lambda s, i: (s, 0, 0)),
            pl.BlockSpec((1, block, 1), lambda s, i: (s, i, 0)),
            pl.BlockSpec((1, 1, 1, reach), lambda s, i: (s, i, 0, 0)),
        ],
        out_specs=[
            pl.BlockSpec((1, block, width), lambda s, i: (s, i, 0)),
            pl.BlockSpec((1, block, LANES), lambda s, i: (s, i, 0)),
        ],
        out_shape=[
            jax.ShapeDtypeStruct(query.shape, BF16),
            jax.ShapeDtypeStruct((seqs, span, LANES), F32),
        ],
        compiler_params=pltpu.CompilerParams(vmem_limit_bytes=40 << 20),
        cost_estimate=pl.CostEstimate(
            flops=70 * seqs * span * reach * width, bytes_accessed=4 << 20, transcendentals=0
        ),
        name="attend_forward",
    )(query, keys_used, query_segments[:, :, None], key_tiles(key_segments, base, lead, block, span))


def attend_backward(
    query, keys_values, grad_mixed, log_sums, query_segments, key_segments, base, lead, group
):
    seqs, span, width = query.shape
    block = min(LANES, span)
    heads = width // HD
    reach = block + lead
    keys_used = keys_values[:, base:]
    whole_keys = pl.BlockSpec((1,) + keys_used.shape[1:], lambda s, i: (s, 0, 0))
    rows = pl.BlockSpec((1, block, width), lambda s, i: (s, i, 0))
    grad_query, grad_keys_values = pl.pallas_call(
        functools.partial(attend_backward_body, lead, heads, group),
        grid=(seqs, span // block),
        in_specs=[
            rows,
            whole_keys,
            rows,
            pl.BlockSpec((1, heads, block), lambda s, i: (s, 0, i)),
            pl.BlockSpec((1, 1, block), lambda s, i: (s, 0, i)),
            pl.BlockSpec((1, keys_used.shape[1], 1), lambda s, i: (s, 0, 0)),
        ],
        out_specs=[rows, whole_keys],
        out_shape=[
            jax.ShapeDtypeStruct(query.shape, F32),
            jax.ShapeDtypeStruct(keys_used.shape, F32),
        ],
        compiler_params=pltpu.CompilerParams(vmem_limit_bytes=40 << 20),
        cost_estimate=pl.CostEstimate(
            flops=85 * seqs * span * reach * width, bytes_accessed=6 << 20, transcendentals=0
        ),
        name="attend_backward",
    )(
        query,
        keys_used,
        grad_mixed,
        log_sums,
        query_segments[:, None, :],
        key_segments[:, base:, None],
    )
    return grad_query, jnp.pad(grad_keys_values, ((0, 0), (base, 0), (0, 0)))


def whole(array):
    return pl.BlockSpec(array.shape, lambda *at: (0,) * array.ndim)


def kernel_cost(flops, moved):
    return pl.CostEstimate(flops=flops, bytes_accessed=moved, transcendentals=0)


def feed_forward_body(sizes, hidden_ref, *refs):
    count = len(sizes)
    gate_refs, up_refs = refs[:count], refs[count : 2 * count]
    gate_ref, up_ref, act_ref = refs[2 * count :]

    def project(pieces):
        total, at = None, 0
        for size, piece in zip(sizes, pieces):
            value = dot_rows(hidden_ref[:, at : at + size], piece[...])
            total = value if total is None else total + value
            at += size
        return total

    gate_value, up_value = project(gate_refs), project(up_refs)
    gate_ref[...] = gate_value
    up_ref[...] = up_value
    act_ref[...] = (gate_value * jax.nn.sigmoid(gate_value) * up_value).astype(BF16)


def feed_forward(hidden, gate_pieces, up_pieces, cut, columns):
    rows = hidden.shape[0]
    tile = min(512, columns)
    steps = columns // tile
    own = lambda w: pl.BlockSpec((w.shape[0], tile), lambda i: (0, cut * steps + i))
    rest = lambda w: pl.BlockSpec((w.shape[0], tile), lambda i: (0, i))
    specs = [own(gate_pieces[0])] + [rest(w) for w in gate_pieces[1:]]
    out = pl.BlockSpec((rows, tile), lambda i: (0, i))
    return pl.pallas_call(
        functools.partial(feed_forward_body, tuple(w.shape[0] for w in gate_pieces)),
        grid=(steps,),
        in_specs=[whole(hidden)] + specs + specs,
        out_specs=[out] * 3,
        out_shape=[
            jax.ShapeDtypeStruct((rows, columns), F32),
            jax.ShapeDtypeStruct((rows, columns), F32),
            jax.ShapeDtypeStruct((rows, columns), BF16),
        ],
        compiler_params=pltpu.CompilerParams(vmem_limit_bytes=40 << 20),
        cost_estimate=kernel_cost(6 * rows * columns * hidden.shape[1], 8 << 20),
        name="feed_forward",
    )(hidden, *gate_pieces, *up_pieces)


def feed_backward_body(sizes, grad_ref, *refs):
    count = len(sizes)
    gate_ref, up_ref, grad_gate_ref, grad_up_ref = refs[count:]
    grad_act, at = None, 0
    for size, piece in zip(sizes, refs[:count]):
        value = dot_back(grad_ref[:, at : at + size], piece[...])
        grad_act = value if grad_act is None else grad_act + value
        at += size
    gate_value = gate_ref[...]
    sigmoid_gate = jax.nn.sigmoid(gate_value)
    grad_up = grad_act * sigmoid_gate
    grad_gate_ref[...] = (
        grad_up * up_ref[...] * (1.0 + gate_value * (1.0 - sigmoid_gate))
    ).astype(BF16)
    grad_up_ref[...] = (grad_up * gate_value).astype(BF16)


def feed_backward(grad, down_pieces, gate_value, up_value, cut):
    rows, columns = gate_value.shape
    tile = min(512, columns)
    steps = columns // tile
    own = lambda w: pl.BlockSpec((tile, w.shape[1]), lambda i: (cut * steps + i, 0))
    rest = lambda w: pl.BlockSpec((tile, w.shape[1]), lambda i: (i, 0))
    out = pl.BlockSpec((rows, tile), lambda i: (0, i))
    return pl.pallas_call(
        functools.partial(feed_backward_body, tuple(w.shape[1] for w in down_pieces)),
        grid=(steps,),
        in_specs=[whole(grad), own(down_pieces[0])]
        + [rest(w) for w in down_pieces[1:]]
        + [out, out],
        out_specs=[out] * 2,
        out_shape=[jax.ShapeDtypeStruct((rows, columns), BF16)] * 2,
        compiler_params=pltpu.CompilerParams(vmem_limit_bytes=40 << 20),
        cost_estimate=kernel_cost(4 * rows * columns * grad.shape[1], 8 << 20),
        name="feed_backward",
    )(grad, *down_pieces, gate_value, up_value)


def project_body(cuts, steps, terms, pieces, transposed, sibling_ref, *refs):
    first_ref, second_ref, total_ref = refs[-3:]
    step = pl.program_id(0)
    lefts = refs[: cuts * terms]
    weights = refs[cuts * terms : -3]

    @pl.when(step == 0)
    def _():
        total_ref[...] = jnp.zeros_like(total_ref)

    for cut in range(cuts):

        @pl.when(step // steps == cut)
        def _():
            at = 0
            for piece in range(pieces):
                value = None
                for term in range(terms):
                    left = lefts[cut * terms + term][...]
                    weight = weights[(cut * terms + term) * pieces + piece][...]
                    part = dot_back(left, weight) if transposed else dot_rows(left, weight)
                    value = part if value is None else value + part
                total_ref[:, at : at + value.shape[1]] += value
                at += value.shape[1]

    @pl.when(step == cuts * steps - 1)
    def _():
        half = total_ref.shape[0] // 2
        mine = pl.multiple_of(sibling_ref[0] * half, half)
        theirs = pl.multiple_of((1 - sibling_ref[0]) * half, half)
        first_ref[...] = total_ref[pl.ds(theirs, half), :].astype(BF16)
        second_ref[...] = total_ref[pl.ds(mine, half), :]


def project(sibling, lefts, weights, width, transposed):
    cuts, terms, pieces = len(lefts), len(lefts[0]), len(weights[0][0])
    rows, columns = lefts[0][0].shape
    tile = min(512, columns)
    steps = columns // tile
    in_specs = [pl.BlockSpec(memory_space=pltpu.SMEM)]
    operands = []

    def clipped(cut):
        return lambda i: jnp.clip(i - cut * steps, 0, steps - 1)

    for cut in range(cuts):
        for left in lefts[cut]:
            in_specs.append(pl.BlockSpec((rows, tile), lambda i, f=clipped(cut): (0, f(i))))
            operands.append(left)
    for cut in range(cuts):
        for term in weights[cut]:
            for piece, weight in enumerate(term):
                offset = cut * steps if piece == 0 else 0
                if transposed:
                    spec = pl.BlockSpec(
                        (weight.shape[0], tile), lambda i, f=clipped(cut), o=offset: (0, o + f(i))
                    )
                else:
                    spec = pl.BlockSpec(
                        (tile, weight.shape[1]), lambda i, f=clipped(cut), o=offset: (o + f(i), 0)
                    )
                in_specs.append(spec)
                operands.append(weight)
    half_rows = jax.ShapeDtypeStruct((rows // 2, width), BF16)
    return pl.pallas_call(
        functools.partial(project_body, cuts, steps, terms, pieces, transposed),
        grid=(cuts * steps,),
        in_specs=in_specs,
        out_specs=[whole(half_rows)] * 2,
        out_shape=[half_rows, jax.ShapeDtypeStruct((rows // 2, width), F32)],
        scratch_shapes=[pltpu.VMEM((rows, width), F32)],
        compiler_params=pltpu.CompilerParams(vmem_limit_bytes=48 << 20),
        cost_estimate=kernel_cost(3 * terms * rows * columns * cuts * width, 16 << 20),
        name="project",
    )(sibling.reshape(1), *operands)


CHUNK_ROWS, CHUNK_COLUMNS = 256, 1024


def outer_sum_body(split, groups, left_ref, left_other_ref, *refs):
    out_ref = refs[-1]
    rights, others = refs[:groups], refs[groups : 2 * groups]
    blocks = left_ref.shape[1] // CHUNK_ROWS
    for group in range(groups):

        def emit():
            for block in range(blocks):
                rows = slice(block * CHUNK_ROWS, (block + 1) * CHUNK_ROWS)
                value = dot_outer(left_ref[:, rows], rights[group][...])
                value += dot_outer(left_other_ref[:, rows], others[group][...])
                width = value.shape[1]
                out_ref[0, :, block * width : (block + 1) * width] = value.astype(BF16)

        if groups == 1:
            emit()
        else:
            pl.when(pl.program_id(0) // split == group)(emit)


def outer_sum(pool, at, count, left, left_other, rights, rights_other):
    groups = len(rights)
    rows = left.shape[0]
    columns = CHUNK_ROWS * CHUNK_COLUMNS // rights[0].shape[1]
    split = left.shape[1] // columns
    left_spec = pl.BlockSpec((rows, columns), lambda i: (0, lax.rem(i, split)))
    operands = (left, left_other, *rights, *rights_other)
    in_specs = [left_spec] * 2 + [whole(value) for value in operands[2:]]
    aliases = {}
    if pool is not None:
        operands += (pool,)
        in_specs.append(pl.BlockSpec(memory_space=pl.ANY))
        aliases = {len(operands) - 1: 0}
    return pl.pallas_call(
        functools.partial(outer_sum_body, split, groups),
        grid=(split * groups,),
        in_specs=in_specs,
        out_specs=pl.BlockSpec((1, CHUNK_ROWS, CHUNK_COLUMNS), lambda i: (at + i, 0, 0)),
        out_shape=jax.ShapeDtypeStruct((count, CHUNK_ROWS, CHUNK_COLUMNS), BF16),
        input_output_aliases=aliases,
        compiler_params=pltpu.CompilerParams(vmem_limit_bytes=48 << 20),
        cost_estimate=kernel_cost(
            4 * split * groups * rows * CHUNK_ROWS * CHUNK_COLUMNS, 4 << 20
        ),
        name="outer_sum",
    )(*operands)


def widen_body(starts, pool_ref, *out_refs):
    step = pl.program_id(0)
    value = pool_ref[0].astype(F32)
    last = len(starts) - 1
    for at, start in enumerate(starts):
        stop = starts[at + 1] if at < last else pl.num_programs(0)

        @pl.when((step >= start) & (step < stop))
        def _():
            if at < last - 1:
                out_refs[at][...] = value
            elif at == last - 1:
                half = CHUNK_COLUMNS // 2
                out_refs[at][:CHUNK_ROWS] = value[:, :half]
                out_refs[at][CHUNK_ROWS:] = value[:, half:]
            else:
                width = out_refs[at].shape[1]
                for block in range(CHUNK_COLUMNS // (2 * width)):
                    rows = slice(block * CHUNK_ROWS, (block + 1) * CHUNK_ROWS)
                    left = 2 * block * width
                    out_refs[at][rows] = value[:, left : left + width]
                    out_refs[at + 1][rows] = value[:, left + width : left + 2 * width]


def widen(pool, starts, shapes):
    specs = []
    for at, shape in enumerate(shapes):
        which = min(at, len(starts) - 1)
        start = starts[which]
        stop = starts[which + 1] if which + 1 < len(starts) else pool.shape[0]
        size = stop - start
        block = (shape[0] * shape[1] // (size * CHUNK_COLUMNS), CHUNK_COLUMNS)
        if which == len(starts) - 1:
            block = shape
        elif which == len(starts) - 2:
            block = (2 * CHUNK_ROWS, shape[1])
        down = shape[0] // block[0]

        def place(i, start=start, size=size, down=down):
            k = jnp.clip(i - start, 0, size - 1)
            return lax.rem(k, down), k // down

        specs.append(pl.BlockSpec(block, place))
    return pl.pallas_call(
        functools.partial(widen_body, starts),
        grid=(pool.shape[0],),
        in_specs=[pl.BlockSpec((1, CHUNK_ROWS, CHUNK_COLUMNS), lambda i: (i, 0, 0))],
        out_specs=specs,
        out_shape=[jax.ShapeDtypeStruct(shape, F32) for shape in shapes],
        compiler_params=pltpu.CompilerParams(vmem_limit_bytes=48 << 20),
        cost_estimate=kernel_cost(1, 45 << 20),
        name="widen",
    )(pool)


def tail_body(plan, *refs):
    heads, group, lead, starts, count = plan
    (
        pool_in, hidden_m_send, hidden_a_send, feed_chip, stored,
        pool_ref, sum_ref, near_ref, across_ref, feed_land, grad_ref, gain_out_ref,
        gate_land, up_land, hidden_m_land, hidden_a_land, branch_land, mixed_land, qkv_land,
        grad_mixed_ref, dq_ref, dkv_ref, kv_send, kv_land, qkv_grad_ref,
        first_ref, second_ref, core_land, chip_ref, y_land, total_ref, other_ref,
        middle_y, middle_total, middle_other, branch_ref, branch_send,
        gains_ref, gain_send, gain_land, gain_mine, gain_all, gain_send_sem, gain_recv_sem,
        own_buf, near_buf, part_buf, across_buf, total_buf, piece_buf,
        x_send, x_recv, tp_send, tp_recv, kv_send_sem, kv_recv_sem,
        send_sem, land_sem, cross_send, cross_land, keep_sem, load_sem, piece_sem,
        loaded, loaded_sem,
    ) = refs
    (
        gate_refs, up_refs, hidden_m_ref, hidden_a_ref, mixed_ref, out_refs,
        query_ref, keys_ref, log_ref, query_seg_ref, key_seg_ref, cosine_ref, sine_ref,
        qkv_refs, inputs_ref, scale_ref, gain_ref, grad_middle_ref,
        middle_chip, cotangent_ref, middle_scale, middle_gain,
    ) = loaded
    stored_gate, stored_up, stored_mixed = stored[0], stored[1], stored[4]
    rows, width = inputs_ref.shape
    half, part = width // 2, width // 4
    half_rows = rows // 2
    mesh_id = pl.DeviceIdType.MESH
    shard, ctx, tp = (lax.axis_index(name) for name in ("fsdp", "ctx", "tp"))
    sibling = lax.rem(tp, 2)
    core = tp + 1 - 2 * sibling
    across_y = lax.rem(tp + 2, 4)
    partner = 1 - shard
    pair = ctx + 1 - 2 * lax.rem(ctx, 2)
    across = 3 - ctx
    is_end = (ctx == 0) | (ctx == 3)
    is_middle = jnp.logical_not(is_end)

    kv_land[...] = jnp.zeros_like(kv_land)
    dkv_ref[...] = jnp.zeros_like(dkv_ref)
    gains_ref[...] = jnp.zeros_like(gains_ref)

    barrier = pltpu.get_barrier_semaphore()
    others = [{"fsdp": partner}, {"tp": core}, {"tp": across_y}]
    others += [{"ctx": lax.rem(ctx + step, 4)} for step in (1, 2, 3)]
    for other in others:
        pl.semaphore_signal(barrier, inc=1, device_id=other, device_id_type=mesh_id)
    pl.semaphore_wait(barrier, len(others))

    def x_copy(at, source, land):
        return pltpu.make_async_remote_copy(
            src_ref=source, dst_ref=land, send_sem=x_send.at[at], recv_sem=x_recv.at[at],
            device_id={"fsdp": partner}, device_id_type=mesh_id,
        )

    cuts = len(gate_refs)
    gate_copies = [x_copy(i, stored_gate[i], gate_land[i]) for i in range(cuts)]
    up_copies = [x_copy(cuts + i, stored_up[i], up_land[i]) for i in range(cuts)]
    hidden_m_copy = x_copy(2 * cuts, hidden_m_send, hidden_m_land)
    branch_copy = x_copy(2 * cuts + 1, branch_send, branch_land)
    mixed_copy = x_copy(2 * cuts + 2, stored_mixed, mixed_land)
    hidden_a_copy = x_copy(2 * cuts + 3, hidden_a_send, hidden_a_land)
    qkv_copy = x_copy(2 * cuts + 4, qkv_grad_ref, qkv_land)
    queue = gate_copies + [hidden_m_copy] + up_copies
    queue += [branch_copy, mixed_copy, qkv_copy, hidden_a_copy]

    def send_next(first, last):
        for at in range(first, last):
            if at >= 2:
                queue[at - 2].wait_send()
            queue[at].start()

    def tp_copy(at, source, land, target):
        return pltpu.make_async_remote_copy(
            src_ref=source, dst_ref=land, send_sem=tp_send.at[at], recv_sem=tp_recv.at[at],
            device_id={"tp": target}, device_id_type=mesh_id,
        )

    split = CHUNK_ROWS // own_buf.shape[0]
    count = count * split

    def share(ref, k):
        size = CHUNK_ROWS // split
        return ref.at[k // split, pl.ds(pl.multiple_of(lax.rem(k, split) * size, size), size), :]

    def to_pair(source, land, k):
        return pltpu.make_async_remote_copy(
            src_ref=source, dst_ref=share(land, k), send_sem=send_sem.at[k],
            recv_sem=land_sem.at[k], device_id={"ctx": pair}, device_id_type=mesh_id,
        )

    def inward_copy(k):
        return to_pair(share(pool_ref, k), near_ref, k)

    def outward_copy(k):
        return to_pair(total_buf.at[lax.rem(k, 2)], sum_ref, k)

    def cross_copy(k):
        return pltpu.make_async_remote_copy(
            src_ref=part_buf.at[lax.rem(k, 4)], dst_ref=share(across_ref, k),
            send_sem=cross_send.at[k], recv_sem=cross_land.at[k],
            device_id={"ctx": across}, device_id_type=mesh_id,
        )

    def keep_copy(k):
        return pltpu.make_async_copy(
            total_buf.at[lax.rem(k, 2)], share(sum_ref, k), keep_sem.at[k]
        )

    def load(source, buffer, at):
        return pltpu.make_async_copy(source, buffer, load_sem.at[at])

    lag = 2

    def inward(k):
        inward_copy(k).wait_recv()
        loads = [load(share(pool_ref, k), own_buf, 0), load(share(near_ref, k), near_buf, 1)]
        for copy in loads:
            copy.start()
        for copy in loads:
            copy.wait()
        part_buf[lax.rem(k, 4)] = (own_buf[...].astype(F32) + near_buf[...].astype(F32)).astype(
            BF16
        )
        cross_copy(k).start()

    def outward(k, reuse):
        cross_copy(k).wait_recv()
        copy = load(share(across_ref, k), across_buf, 2)
        copy.start()
        if reuse:
            keep_copy(k - 2).wait()
            outward_copy(k - 2).wait_send()
        copy.wait()
        total_buf[lax.rem(k, 2)] = (
            part_buf[lax.rem(k, 4)].astype(F32) + across_buf[...].astype(F32)
        ).astype(BF16)
        cross_copy(k).wait_send()
        outward_copy(k).start()
        keep_copy(k).start()

    ahead = 2 * split

    def send_piece(k, carry):
        inward_copy(k).wait_send()

        @pl.when(k + ahead < count)
        def _():
            inward_copy(k + ahead).start()

        return carry

    def pump(first, last):
        pump_steps(first * split, last * split)

    def pump_steps(first, last):

        @pl.when(is_end)
        def _():
            lax.fori_loop(min(first, count), min(last, count), send_piece, 0)

        @pl.when(is_middle)
        def _():
            k = first
            while k < min(last, lag + 2):
                inward(jnp.int32(k))
                if k >= lag:
                    outward(jnp.int32(k - lag), False)
                k += 1
            if k < min(last, count):

                def both(at, carry):
                    inward(at)
                    outward(at - lag, True)
                    return carry

                lax.fori_loop(k, min(last, count), both, 0)
            k = max(k, count)
            while k < min(last, count + lag):
                outward(jnp.int32(k - lag), True)
                k += 1

    @pl.when(is_end)
    def _():
        for k in range(ahead):
            inward_copy(jnp.int32(k)).start()

    send_next(0, 2)
    middle_y_copy = tp_copy(3, stored[-4], middle_y, across_y)
    middle_core_copy = tp_copy(4, middle_total, middle_other, core)
    feed_copy = tp_copy(5, feed_chip, feed_land, across_y)
    middle_y_copy.start()
    fills = [
        pltpu.make_async_copy(source, buffer, loaded_sem.at[at])
        for at, (source, buffer) in enumerate(
            zip(jax.tree.leaves(stored), jax.tree.leaves(loaded))
        )
    ]
    for fill in fills:
        fill.start()
    for fill in fills:
        fill.wait()
    pump_steps(0, 3)

    theirs = pl.multiple_of((1 - sibling) * half_rows, half_rows)
    mine = pl.multiple_of(sibling * half_rows, half_rows)
    step_rows = 64
    odd = lax.rem(ctx, 2)
    near_send = pl.multiple_of(odd * part, part)
    far_send = pl.multiple_of((1 - odd) * part, part)

    def middle_rows(source, base):
        def body(step, total):
            at = pl.multiple_of(step * step_rows, step_rows)
            here = pl.ds(pl.multiple_of(base + at, step_rows), step_rows)
            normed = grad_middle_ref[here, :]
            hidden = source[pl.ds(at, step_rows), :].astype(F32)
            grad = hidden * middle_gain[...]
            mean = jnp.sum(grad * normed, axis=-1, keepdims=True) * (1.0 / width)
            value = cotangent_ref[here, :].astype(F32) + middle_scale[here, :] * (
                grad - normed * mean
            )
            grad_middle_ref[here, :] = value
            low = value.astype(BF16)
            branch_ref[here, :] = low
            branch_send[here, pl.ds(near_send, part)] = low[:, half : half + part]
            branch_send[here, pl.ds(far_send, part)] = low[:, half + part :]
            return total + jnp.sum(hidden * normed, axis=0, keepdims=True)

        return lax.fori_loop(0, half_rows // step_rows, body, jnp.zeros((1, width), F32))

    middle_y_copy.wait_recv()
    middle_total[...] = (middle_chip[...].astype(F32) + middle_y[...].astype(F32)).astype(BF16)
    middle_core_copy.start()
    feed_gain = middle_rows(middle_total, mine)
    pump_steps(3, 4)
    middle_core_copy.wait_recv()
    gains_ref[1:2, :] = feed_gain + middle_rows(middle_other, theirs)
    send_next(2, 3)

    grad_mixed = None
    at = 0
    for piece in out_refs:
        value = dot_back(branch_ref[:, at : at + piece.shape[1]], piece[...])
        grad_mixed = value if grad_mixed is None else grad_mixed + value
        at += piece.shape[1]
    grad_mixed_ref[...] = grad_mixed.astype(BF16)

    tile = log_ref.shape[2]
    tiles = rows // tile
    reach = tile + lead

    def attend(step, carry):
        @pl.when(is_end)
        def _():
            send_piece(step + lag + 2, 0)

        @pl.when(is_middle)
        def _():
            inward(step + lag + 2)
            outward(step + 2, True)

        start = pl.multiple_of(step * tile, tile)
        distance = (
            lax.broadcasted_iota(jnp.int32, (reach, tile), 1)
            + lead
            - lax.broadcasted_iota(jnp.int32, (reach, tile), 0)
        )
        same = key_seg_ref[pl.ds(start, reach), :] == query_seg_ref[step]
        bias = jnp.where(same & (distance >= 0) & (distance < WINDOW), 0.0, MASK_FILL)
        query_grad, keys_grad = backward_tile(
            heads,
            group,
            lambda head: query_ref[pl.ds(start, tile), head * HD : (head + 1) * HD],
            lambda head: grad_mixed_ref[pl.ds(start, tile), head * HD : (head + 1) * HD],
            lambda head: log_ref[step, head : head + 1, :],
            lambda at: keys_ref[pl.ds(start, reach), at * HD : (at + 1) * HD],
            bias,
        )
        dq_ref[pl.ds(start, tile), :] = query_grad
        dkv_ref[pl.ds(start, reach), :] += keys_grad
        return carry

    lax.fori_loop(0, tiles, attend, 0)
    send_next(3, 4)

    for back in (1, 2):
        kv_send[back - 1] = dkv_ref[(2 - back) * rows : (3 - back) * rows, :].astype(BF16)

    def kv_copy(back):
        return pltpu.make_async_remote_copy(
            src_ref=kv_send.at[back - 1], dst_ref=kv_land.at[back - 1],
            send_sem=kv_send_sem.at[back - 1], recv_sem=kv_recv_sem.at[back - 1],
            device_id={"ctx": lax.rem(ctx + 4 - back, 4)}, device_id_type=mesh_id,
        )

    for back in (1, 2):

        @pl.when(ctx >= back)
        def _():
            kv_copy(back).start()

    def piece_copy(slot, k):
        return pltpu.make_async_copy(piece_buf.at[slot], pool_ref.at[k], piece_sem.at[slot])

    def put(first, values):
        for at, make in enumerate(values):
            slot = at % 2
            if at >= 2:
                piece_copy(slot, first + at - 2).wait()
            piece_buf[slot] = make()
            piece_copy(slot, first + at).start()
        for at in range(max(0, len(values) - 2), len(values)):
            piece_copy(at % 2, first + at).wait()

    def outer(left, left_other, right, right_other, block):
        columns = slice(block * CHUNK_ROWS, (block + 1) * CHUNK_ROWS)
        return (
            dot_outer(left[:, columns], right[...]) + dot_outer(left_other[:, columns], right_other[...])
        ).astype(BF16)

    def feed_pieces(rights, rights_other):
        return [
            functools.partial(outer, hidden_m_ref, hidden_m_land, right, right_other, block)
            for right, right_other in zip(rights, rights_other)
            for block in range(half // CHUNK_ROWS)
        ]

    pump(4, 5)
    for copy in gate_copies + [hidden_m_copy]:
        copy.wait_recv()
    put(starts[1], feed_pieces(gate_refs, gate_land))
    send_next(4, 5)
    pump(5, 6)

    for back in (1, 2):

        @pl.when(ctx + back < 4)
        def _():
            kv_copy(back).wait_recv()

    kv_width = dkv_ref.shape[1] // 2
    q_width = dq_ref.shape[1]
    cosine, sine = cosine_ref[...], sine_ref[...]
    front = lax.rem(lax.broadcasted_iota(jnp.int32, (rows, LANES), 1), HD) < HD // 2

    def unrotate(value):
        swapped = jnp.where(
            front, pltpu.roll(value, LANES - HD // 2, 1), pltpu.roll(value, HD // 2, 1)
        )
        return (value * cosine - swapped * sine).astype(BF16)

    for at in range(0, q_width, LANES):
        qkv_grad_ref[:, at : at + LANES] = unrotate(dq_ref[:, at : at + LANES])
    kv_sum = dkv_ref[2 * rows :, :]
    for back in range(2):
        kv_sum = kv_sum + kv_land[back].astype(F32)
    for at in range(0, kv_width, LANES):
        qkv_grad_ref[:, q_width + at : q_width + at + LANES] = unrotate(
            kv_sum[:, at : at + LANES]
        )
    qkv_grad_ref[:, q_width + kv_width :] = kv_sum[:, kv_width:].astype(BF16)

    first_copy = tp_copy(0, first_ref, core_land, core)
    y_copy = tp_copy(1, chip_ref, y_land, across_y)
    total_copy = tp_copy(2, total_ref, other_ref, core)

    def back_project(start, store):
        at = 0
        for piece in qkv_refs:
            size = piece.shape[0]
            store(at, size, dot_back(qkv_grad_ref[pl.ds(start, half_rows), :], piece[...]))
            at += size

    def store_first(at, size, value):
        first_ref[:, at : at + size] = value.astype(BF16)

    def store_second(at, size, value):
        second_ref[:, at : at + size] = value

    back_project(theirs, store_first)
    first_copy.start()
    back_project(mine, store_second)
    pump(6, 8)
    first_copy.wait_recv()
    chip_ref[...] = (second_ref[...] + core_land[...].astype(F32)).astype(BF16)
    y_copy.start()
    send_next(5, 6)
    pump(8, 10)


    y_copy.wait_recv()
    total_ref[...] = (chip_ref[...].astype(F32) + y_land[...].astype(F32)).astype(BF16)
    total_copy.start()
    feed_copy.start()
    gain = gain_ref[...]
    near_at = pl.multiple_of((1 - shard) * half + lax.rem(ctx, 2) * part, part)
    far_at = pl.multiple_of((1 - shard) * half + (1 - lax.rem(ctx, 2)) * part, part)
    own_at = pl.multiple_of(shard * half, half)

    def norm_rows(source, base):
        def body(step, total):
            at = pl.multiple_of(step * step_rows, step_rows)
            here = pl.ds(pl.multiple_of(base + at, step_rows), step_rows)
            scale = scale_ref[here, :]
            normed = inputs_ref[here, :].astype(F32) * scale
            hidden = source[pl.ds(at, step_rows), :].astype(F32)
            grad = hidden * gain
            mean = jnp.sum(grad * normed, axis=-1, keepdims=True) * (1.0 / width)
            value = (grad_middle_ref[here, :] + scale * (grad - normed * mean)).astype(BF16)
            grad_ref[here, pl.ds(own_at, half)] = value[:, :half]
            grad_ref[here, pl.ds(near_at, part)] = value[:, half : half + part]
            grad_ref[here, pl.ds(far_at, part)] = value[:, half + part :]
            return total + jnp.sum(hidden * normed, axis=0, keepdims=True)

        return lax.fori_loop(0, half_rows // step_rows, body, jnp.zeros((1, width), F32))

    gain_sum = norm_rows(total_ref, mine)
    pump(10, 11)
    send_next(6, 7)
    total_copy.wait_recv()
    gains_ref[0:1, :] = gain_sum + norm_rows(other_ref, theirs)
    gain_send[:, pl.ds(near_send, part)] = gains_ref[:, half : half + part]
    gain_send[:, pl.ds(far_send, part)] = gains_ref[:, half + part :]
    gain_copy = x_copy(2 * cuts + 5, gain_send, gain_land)
    gain_copy.start()
    pump(11, 12)
    for copy in up_copies:
        copy.wait_recv()
    put(starts[2], feed_pieces(up_refs, up_land))
    send_next(7, 8)
    gain_copy.wait_recv()
    gain_mine[...] = gains_ref[:, :half] + gain_land[...]
    gain_all[ctx] = gain_mine[...]

    def gain_to(by, slot):
        return pltpu.make_async_remote_copy(
            src_ref=gain_mine, dst_ref=gain_all.at[slot], send_sem=gain_send_sem.at[by - 1],
            recv_sem=gain_recv_sem.at[by - 1], device_id={"ctx": lax.rem(ctx + by, 4)},
            device_id_type=mesh_id,
        )

    for by in (1, 2, 3):
        gain_to(by, ctx).start()
    pump(12, 14)
    send_next(8, len(queue))
    branch_copy.wait_recv()
    mixed_copy.wait_recv()
    put(
        starts[3],
        [
            functools.partial(
                outer, mixed_ref, mixed_land, branch_ref.at[:, :half], branch_land, block
            )
            for block in range(q_width // CHUNK_ROWS)
        ],
    )
    pump(14, 17)
    hidden_a_copy.wait_recv()
    qkv_copy.wait_recv()

    def side_by_side(first, number, columns):
        return jnp.concatenate(
            [
                outer(
                    hidden_a_ref, hidden_a_land, qkv_grad_ref.at[:, columns],
                    qkv_land.at[:, columns], block,
                )
                for block in range(first, first + number)
            ],
            axis=1,
        )

    q_blocks = CHUNK_COLUMNS // q_width
    put(
        starts[4],
        [
            functools.partial(side_by_side, first, q_blocks, slice(0, q_width))
            for first in range(0, half // CHUNK_ROWS, q_blocks)
        ]
        + [
            functools.partial(
                side_by_side, 0, half // CHUNK_ROWS, slice(q_width, q_width + 2 * kv_width)
            )
        ],
    )
    pump(17, count // split + lag)

    for by in (1, 2, 3):
        gain_to(by, lax.rem(ctx + 4 - by, 4)).wait_recv()
    gain_out_ref[...] = (gain_all[0] + gain_all[1]) + (gain_all[2] + gain_all[3])
    for by in (1, 2, 3):
        gain_to(by, ctx).wait_send()
    gain_copy.wait_send()
    feed_copy.wait_recv()
    for copy in queue[-2:] + [first_copy, y_copy, total_copy]:
        copy.wait_send()
    for copy in (middle_y_copy, middle_core_copy, feed_copy):
        copy.wait_send()
    for back in (1, 2):

        @pl.when(ctx >= back)
        def _():
            kv_copy(back).wait_send()

    @pl.when(is_middle)
    def _():
        for k in (count - 2, count - 1):
            outward_copy(jnp.int32(k)).wait_send()
            keep_copy(jnp.int32(k)).wait()

    @pl.when(is_end)
    def _():
        def close(k, carry):
            to_pair(share(pool_ref, k), sum_ref, k).wait_recv()
            return carry

        lax.fori_loop(0, count, close, 0)


def flat_call(body, operands, **call):
    flat, tree = jax.tree.flatten(operands)

    def unflatten(*refs):
        body(*jax.tree.unflatten(tree, refs[: len(flat)]), *refs[len(flat) :])

    in_specs = [pl.BlockSpec(memory_space=pl.ANY)] * len(flat)
    return pl.pallas_call(unflatten, in_specs=in_specs, **call)(*flat)


def tail(plan, pool, v):
    heads, group, lead, starts, count = plan
    rows, width = v["inputs"].shape
    half = width // 2
    q_width, kv_width = v["query"].shape[1], v["keys_values"].shape[1] // 2
    qkv_width = q_width + 2 * kv_width
    piece = (CHUNK_ROWS, CHUNK_COLUMNS)
    split = 2
    step, steps = (CHUNK_ROWS // split, CHUNK_COLUMNS), count * split
    cuts, feed_part = len(v["grad_gate"]), v["grad_gate"][0].shape[1]

    stored = [
        v["grad_gate"], v["grad_up"], v["hidden_m"], v["hidden_a"], v["mixed"],
        v["out_pieces"], v["query"], v["keys_values"], v["log_sums"], v["query_segments"],
        v["key_segments"], v["cosine"], v["sine"], v["qkv_pieces"], v["inputs"], v["scale"],
        v["gain"], v["normed_m"], v["middle_chip"], v["cotangent"], v["middle_scale"],
        v["middle_gain"],
    ]
    operands = [pool, v["hidden_m_send"], v["hidden_a_send"], v["feed_chip"], stored]
    loaded = jax.tree.map(lambda value: pltpu.VMEM(value.shape, value.dtype), stored)
    any_space, vmem_space = pl.BlockSpec(memory_space=pl.ANY), pl.BlockSpec(memory_space=pltpu.VMEM)
    line = jax.ShapeDtypeStruct((count,) + piece, BF16)
    dma = pltpu.SemaphoreType.DMA
    low = lambda *shape: pltpu.VMEM(shape, BF16)
    wide = lambda *shape: pltpu.VMEM(shape, F32)
    scratch = [
        [low(rows, feed_part) for _ in range(cuts)],
        [low(rows, feed_part) for _ in range(cuts)],
        low(rows, half), low(rows, half), low(rows, half),
        low(rows, q_width), low(rows, qkv_width),
        low(rows, q_width), wide(rows, q_width), wide(3 * rows, 2 * kv_width),
        low(2, rows, 2 * kv_width), low(2, rows, 2 * kv_width), low(rows, qkv_width),
        low(rows // 2, width), wide(rows // 2, width), low(rows // 2, width),
        low(rows // 2, width), low(rows // 2, width), low(rows // 2, width),
        low(rows // 2, width),
        low(rows // 2, width), low(rows // 2, width), low(rows // 2, width),
        low(rows, width), low(rows, half),
        wide(8, width), wide(8, half), wide(8, half), wide(8, half), wide(4, 8, half),
        dma((3,)), dma((3,)),
        low(*step), low(*step), low(4, *step), low(*step), low(2, *step), low(2, *piece),
        dma((2 * cuts + 6,)), dma((2 * cuts + 6,)), dma((6,)), dma((6,)), dma((2,)), dma((2,)),
        dma((steps,)), dma((steps,)), dma((steps,)), dma((steps,)), dma((steps,)),
        dma((3,)), dma((2,)),
        loaded, dma((len(jax.tree.leaves(stored)),)),
    ]
    outs = flat_call(
        functools.partial(tail_body, plan),
        operands,
        out_specs=[any_space] * 5 + [vmem_space, vmem_space],
        out_shape=[
            line, line, line, line,
            jax.ShapeDtypeStruct((rows // 2, width), BF16),
            jax.ShapeDtypeStruct((rows, width), BF16),
            jax.ShapeDtypeStruct((8, half), F32),
        ],
        scratch_shapes=scratch,
        input_output_aliases={0: 0},
        compiler_params=pltpu.CompilerParams(
            collective_id=0, has_side_effects=True, vmem_limit_bytes=62 << 20
        ),
        cost_estimate=pl.CostEstimate(
            flops=400 << 30, bytes_accessed=30 << 20, transcendentals=0
        ),
        name="tail",
    )
    return outs[1], outs[4], outs[5], outs[6]


def swap(value, axis, size, bit):
    return lax.ppermute(value, axis, [(i, i ^ bit) for i in range(size)])


def shift(value, axis, size, by):
    if abs(by) >= size:
        return jnp.zeros_like(value)
    return lax.ppermute(
        value, axis, [(i, i + by) for i in range(size) if 0 <= i + by < size]
    )


class Lane:
    def __init__(self, move, depth=2):
        self.move, self.depth, self.done = move, depth, []

    def send(self, value):
        if len(self.done) >= self.depth:
            value, self.done[-self.depth] = tie(value, self.done[-self.depth])
        self.done.append(self.move(value))
        return len(self.done) - 1

    def get(self, at):
        return self.done[at]


def shards(
    sizes,
    block_input,
    segment_ids,
    attention_gain,
    query_weight,
    key_weight,
    value_weight,
    out_weight,
    feed_gain,
    gate_weight,
    up_weight,
    down_weight,
    cotangent,
):
    shard_count, ctx_count, tp_count = sizes
    seqs, span, width = block_input.shape
    rows = seqs * span
    seq_length = segment_ids.shape[1]
    half = width // 2
    part = half // 2
    q_width = query_weight.shape[1]
    kv_width = key_weight.shape[1]
    feed_width = gate_weight.shape[1]
    group = q_width // kv_width
    shard, ctx, tp = (lax.axis_index(name) for name in ("fsdp", "ctx", "tp"))
    odd = ctx % 2
    sibling = tp % 2

    own_at = shard * half
    near_at = (1 - shard) * half + odd * part
    far_at = (1 - shard) * half + (1 - odd) * part

    def to_local(value):
        return jnp.concatenate(
            [
                take(value, own_at, half, 1),
                take(value, near_at, part, 1),
                take(value, far_at, part, 1),
            ],
            axis=1,
        )

    def other_half(value):
        return jnp.concatenate(
            [
                take(value, half + odd * part, part, 1),
                take(value, half + (1 - odd) * part, part, 1),
            ],
            axis=1,
        )

    def from_local(value):
        own, other = value[:, :half], other_half(value)
        return jnp.where(
            shard == 0,
            jnp.concatenate([own, other], axis=1),
            jnp.concatenate([other, own], axis=1),
        )

    fsdp_lane = Lane(lambda value: swap(value, "fsdp", shard_count, 1))

    def over_fsdp(value):
        return swap(value, "fsdp", shard_count, 1)

    def over_ctx(value):
        return swap(value, "ctx", ctx_count, 1)

    def near_part(weight, axis):
        return take(weight, odd * part, part, axis)

    def core_half(value):
        return take(value, sibling * (rows // 2), rows // 2, 0)

    def join_cores(mine):
        other = swap(mine, "tp", tp_count, 1)
        return jnp.where(
            sibling == 0,
            jnp.concatenate([mine, other], axis=0),
            jnp.concatenate([other, mine], axis=0),
        )

    def chip_sum(first, second):
        return (second + swap(first, "tp", tp_count, 1).astype(F32)).astype(BF16)

    def finish_sum(chip):
        total = (chip.astype(F32) + swap(chip, "tp", tp_count, 2).astype(F32)).astype(BF16)
        return join_cores(total).astype(F32)

    def tp_sum(first, second):
        if tp_count != 4:
            whole_rows = jnp.where(
                sibling == 0,
                jnp.concatenate([second, first.astype(F32)], axis=0),
                jnp.concatenate([first.astype(F32), second], axis=0),
            )
            return lax.psum(whole_rows, "tp")
        return finish_sum(chip_sum(first, second))

    gains_own = jnp.stack([attention_gain, feed_gain])
    qkv_own = jnp.concatenate([query_weight, key_weight, value_weight], axis=1)
    feed_cuts = 2
    feed_part = feed_width // feed_cuts
    columns = [slice(cut * feed_part, (cut + 1) * feed_part) for cut in range(feed_cuts)]
    grad_rows = to_local(cotangent.reshape(rows, width))
    send_gate = [near_part(gate_weight[:, cut], 0) for cut in columns]
    send_up = [near_part(up_weight[:, cut], 0) for cut in columns]
    send_down = [near_part(down_weight[cut], 1) for cut in columns]
    send_grad = core_half(other_half(grad_rows))

    gains_other = over_fsdp(gains_own)
    near_qkv = over_fsdp(near_part(qkv_own, 0))
    gains_other, send_out = tie(gains_other, near_part(out_weight, 1))
    near_out = over_fsdp(send_out)

    span_start = ctx * span
    positions = take(doc_positions(segment_ids), span_start, span, 1).reshape(rows)
    query_segments = take(segment_ids, span_start, span, 1)
    cosine, sine = rope_tables(positions)
    blocks_back, base, lead = attention_plan(span, WINDOW)
    key_segments = take(
        jnp.pad(segment_ids, ((0, 0), (blocks_back * span, 0)), constant_values=-1),
        span_start,
        (blocks_back + 1) * span,
        1,
    )

    inputs = to_local(block_input.reshape(rows, width)).astype(F32)
    scale_a = row_scale_of(inputs)
    normed_a = inputs * scale_a
    gains = jnp.concatenate(
        [gains_own, take(gains_other, odd * part, part, 1), take(gains_other, (1 - odd) * part, part, 1)],
        axis=1,
    ).astype(F32)
    gain_a, gain_m = gains[0:1], gains[1:2]
    hidden_a = (normed_a * gain_a).astype(BF16)

    near_qkv, send_gate[0] = tie(near_qkv, send_gate[0])
    near_gate, near_up, far_gate, far_up = ([None] * feed_cuts for _ in range(4))
    near_gate[0] = over_fsdp(send_gate[0])
    far_qkv = over_ctx(near_qkv)
    near_out, send_up[0] = tie(near_out, send_up[0])
    near_up[0] = over_fsdp(send_up[0])
    far_qkv, near_out = tie(far_qkv, near_out)
    far_out = over_ctx(near_out)

    def dot_pieces(matrix, own, near, far):
        return (
            dot_rows(matrix[:, :half], own)
            + dot_rows(matrix[:, half : half + part], near)
            + dot_rows(matrix[:, half + part :], far)
        )

    def back_pieces(matrix, own, near, far):
        return jnp.concatenate(
            [dot_back(matrix, own), dot_back(matrix, near), dot_back(matrix, far)], axis=1
        )

    qkv = dot_pieces(hidden_a, qkv_own, near_qkv, far_qkv)
    key_low = rotate(qkv[:, q_width : q_width + kv_width], cosine, sine).astype(BF16)
    value_low = qkv[:, q_width + kv_width :].astype(BF16)
    keys_values = jnp.concatenate([key_low, value_low], axis=1).reshape(seqs, span, 2 * kv_width)
    query_low = (rotate(qkv[:, :q_width], cosine, sine).astype(BF16) * HD**-0.5).reshape(
        seqs, span, q_width
    )
    earlier = [shift(keys_values, "ctx", ctx_count, back) for back in range(blocks_back, 0, -1)]
    *earlier, query_low = tie(*earlier, query_low)
    keys_values = jnp.concatenate(earlier + [keys_values], axis=1)
    mixed, log_sums = attend_forward(
        query_low, keys_values, query_segments, key_segments, base, lead, group
    )
    mixed_low = mixed.reshape(rows, q_width)
    mixed_low, far_out, near_gate[0], near_up[0], send_gate[1], send_up[1] = tie(
        mixed_low, far_out, near_gate[0], near_up[0], send_gate[1], send_up[1]
    )
    near_gate[1] = over_fsdp(send_gate[1])
    far_gate[0] = over_ctx(near_gate[0])
    near_up[1] = over_fsdp(send_up[1])
    far_up[0] = over_ctx(near_up[0])

    def out_project(at):
        matrix = take(mixed_low, at * (rows // 2), rows // 2, 0)
        return jnp.concatenate(
            [dot_rows(matrix, out_weight), dot_rows(matrix, near_out), dot_rows(matrix, far_out)],
            axis=1,
        )

    first, second = out_project(1 - sibling).astype(BF16), out_project(sibling)
    if tp_count == 4:
        chip = chip_sum(first, second)
        total = (chip.astype(F32) + swap(chip, "tp", tp_count, 2).astype(F32)).astype(BF16)
        total, near_gate[1], far_gate[0] = tie(total, near_gate[1], far_gate[0])
        branch_a = join_cores(total).astype(F32)
    else:
        branch_a = tp_sum(first, second)
    far_gate[1] = over_ctx(near_gate[1])
    middle = inputs + branch_a

    scale_m = row_scale_of(middle)
    normed_m = middle * scale_m
    hidden_m = (normed_m * gain_m).astype(BF16)
    hidden_m, near_up[1], far_up[0], send_down[0] = tie(
        hidden_m, near_up[1], far_up[0], send_down[0]
    )
    near_down = [over_fsdp(send_down[0])]
    far_up[1] = over_ctx(near_up[1])
    gate_cuts, up_cuts, act_cuts = [], [], []

    def feed(cut):
        gate_value, up_value, activated = feed_forward(
            hidden_m,
            (gate_weight, near_gate[cut], far_gate[cut]),
            (up_weight, near_up[cut], far_up[cut]),
            cut,
            feed_part,
        )
        gate_cuts.append(gate_value)
        up_cuts.append(up_value)
        act_cuts.append(activated)

    feed(0)
    act_cuts[0], near_down[0], far_gate[1], send_down[1] = tie(
        act_cuts[0], near_down[0], far_gate[1], send_down[1]
    )
    near_down.append(over_fsdp(send_down[1]))
    far_down = [over_ctx(near_down[0])]
    feed(1)
    act_cuts[1], near_down[1], send_grad, act_cuts[0] = tie(
        act_cuts[1], near_down[1], send_grad, act_cuts[0]
    )
    other_grad = over_fsdp(send_grad)
    act_other = [over_fsdp(act_cuts[0]), over_fsdp(act_cuts[1])]
    far_down.append(over_ctx(near_down[1]))

    pieces = CHUNK_ROWS * CHUNK_COLUMNS
    down_count = feed_width * half // pieces
    starts, pool_size = [], 0
    for size in (feed_width * half,) * 3 + (q_width * half,) * 2 + (2 * kv_width * half,):
        starts.append(pool_size)
        pool_size += size // pieces
    grad_gate_cuts, grad_up_cuts = [], []
    for cut in range(feed_cuts):
        grad_gate, grad_up = feed_backward(
            grad_rows,
            (down_weight, near_down[cut], far_down[cut]),
            gate_cuts[cut],
            up_cuts[cut],
            cut,
        )
        grad_gate_cuts.append(grad_gate)
        grad_up_cuts.append(grad_up)

    grad_gate_cuts[1], act_other[0] = tie(grad_gate_cuts[1], act_other[0])
    first, second = project(
        sibling,
        list(zip(grad_gate_cuts, grad_up_cuts)),
        [
            (
                (gate_weight, near_gate[cut], far_gate[cut]),
                (up_weight, near_up[cut], far_up[cut]),
            )
            for cut in range(feed_cuts)
        ],
        width,
        True,
    )
    first, second, other_grad, *act_cuts = tie(first, second, other_grad, *act_cuts)
    grad_own, grad_other = grad_rows[:, :half], join_cores(other_grad)
    fused = (shard_count, ctx_count, tp_count) == (2, 4, 4)
    fused = fused and seqs == 1 and (blocks_back, base, span) == (2, 0, 4 * LANES)
    if fused:
        middle_chip = chip_sum(first, second)
    else:
        grad_hidden_m = tp_sum(first, second)
    fsdp_lane.done = list(act_other)
    pool = None
    for cut in range(feed_cuts):
        pool = outer_sum(
            pool,
            cut * down_count // feed_cuts,
            pool_size,
            act_cuts[cut],
            act_other[cut],
            [grad_own],
            [grad_other],
        )

    first, second = project(
        sibling,
        [(value,) for value in act_cuts],
        [((down_weight, near_down[cut], far_down[cut]),) for cut in range(feed_cuts)],
        width,
        False,
    )
    if fused:
        feed_chip = chip_sum(first, second)
    else:
        branch_m = tp_sum(first, second)

    if fused:
        tile = min(LANES, rows)
        log_rows = jnp.swapaxes(log_sums[0, :, : q_width // HD].reshape(rows // tile, tile, -1), 1, 2)
        pool, across, input_grad, gain_sums = tail(
            (
                q_width // HD,
                group,
                lead,
                tuple(starts),
                pool_size,
            ),
            pool,
            {
                "grad_gate": grad_gate_cuts,
                "grad_up": grad_up_cuts,
                "hidden_m": hidden_m[:, :half],
                "hidden_m_send": other_half(hidden_m),
                "hidden_a": hidden_a[:, :half],
                "hidden_a_send": other_half(hidden_a),
                "mixed": mixed_low,
                "out_pieces": [out_weight, near_out, far_out],
                "query": query_low[0],
                "keys_values": keys_values[0],
                "log_sums": log_rows,
                "query_segments": query_segments.reshape(rows // tile, 1, tile),
                "key_segments": key_segments.reshape(-1, 1),
                "cosine": cosine,
                "sine": sine,
                "qkv_pieces": [qkv_own, near_qkv, far_qkv],
                "inputs": inputs.astype(BF16),
                "scale": scale_a,
                "gain": gain_a,
                "normed_m": normed_m,
                "middle_chip": middle_chip,
                "cotangent": grad_rows,
                "middle_scale": scale_m,
                "middle_gain": gain_m,
                "feed_chip": feed_chip,
            },
        )
        input_grad = input_grad.reshape(seqs, span, width)
        total = (feed_chip.astype(F32) + across.astype(F32)).astype(BF16)
        branch_m = join_cores(total).astype(F32)
    else:
        feed_gain_part = jnp.sum(grad_hidden_m * normed_m, axis=0)
        grad_middle = norm_back(grad_hidden_m, gain_m, normed_m, scale_m, grad_rows.astype(F32))
        grad_branch = grad_middle.astype(BF16)
        gate_at = [fsdp_lane.send(value) for value in grad_gate_cuts]
        up_at = [fsdp_lane.send(value) for value in grad_up_cuts]
        hidden_m_at = fsdp_lane.send(core_half(other_half(hidden_m)))
        hidden_own, hidden_other = hidden_m[:, :half], join_cores(fsdp_lane.get(hidden_m_at))
        for which, (own, at) in enumerate(((grad_gate_cuts, gate_at), (grad_up_cuts, up_at))):
            pool = outer_sum(
                pool,
                starts[1 + which],
                pool_size,
                hidden_own,
                hidden_other,
                own,
                [fsdp_lane.get(i) for i in at],
            )

        grad_mixed = (
            dot_back(grad_branch[:, :half], out_weight)
            + dot_back(grad_branch[:, half : half + part], near_out)
            + dot_back(grad_branch[:, half + part :], far_out)
        ).astype(BF16)
        branch_at = fsdp_lane.send(core_half(other_half(grad_branch)))
        mixed_at = fsdp_lane.send(mixed_low)
        hidden_a_at = fsdp_lane.send(core_half(other_half(hidden_a)))
        grad_query, grad_keys_values = attend_backward(
            query_low,
            keys_values,
            grad_mixed.reshape(seqs, span, q_width),
            jnp.swapaxes(log_sums, 1, 2)[:, : q_width // HD],
            query_segments,
            key_segments,
            base,
            lead,
            group,
        )
        kv_sum = grad_keys_values[:, blocks_back * span :]
        for back in range(1, blocks_back + 1):
            at = (blocks_back - back) * span
            kv_sum = kv_sum + shift(
                grad_keys_values[:, at : at + span].astype(BF16), "ctx", ctx_count, -back
            ).astype(F32)
        kv_sum = kv_sum.reshape(rows, 2 * kv_width)
        grad_qkv = jnp.concatenate(
            [
                rotate(grad_query.reshape(rows, q_width), cosine, -sine),
                rotate(kv_sum[:, :kv_width], cosine, -sine),
                kv_sum[:, kv_width:],
            ],
            axis=1,
        ).astype(BF16)
        qkv_at = fsdp_lane.send(grad_qkv)
        first, second = (
            back_pieces(take(grad_qkv, at * (rows // 2), rows // 2, 0), qkv_own, near_qkv, far_qkv)
            for at in (1 - sibling, sibling)
        )
        grad_hidden_a = tp_sum(first.astype(BF16), second)
        attention_gain_part = jnp.sum(grad_hidden_a * normed_a, axis=0)
        input_grad = norm_back(grad_hidden_a, gain_a, normed_a, scale_a, grad_middle)
        input_grad = from_local(input_grad.astype(BF16)).reshape(seqs, span, width)

        pool = outer_sum(
            pool,
            starts[3],
            pool_size,
            mixed_low,
            fsdp_lane.get(mixed_at),
            [grad_branch[:, :half]],
            [join_cores(fsdp_lane.get(branch_at))],
        )
        qkv_other = fsdp_lane.get(qkv_at)
        hidden_own, hidden_other = hidden_a[:, :half], join_cores(fsdp_lane.get(hidden_a_at))
        for which, cut in ((4, slice(0, q_width)), (5, slice(q_width, None))):
            pool = outer_sum(
                pool,
                starts[which],
                pool_size,
                hidden_own,
                hidden_other,
                [grad_qkv[:, cut]],
                [qkv_other[:, cut]],
            )
        gain_parts = jnp.stack([attention_gain_part, feed_gain_part])
        gain_other = over_fsdp(other_half(gain_parts))
        gain_sums = lax.psum(gain_parts[:, :half] + gain_other, "ctx")
        pool = lax.psum(pool.astype(F32), "ctx")

    block_out = from_local((middle + branch_m).astype(BF16)).reshape(seqs, span, width)

    down_grad, gate_grad, up_grad, out_grad, query_grad, key_grad, value_grad = widen(
        pool,
        starts,
        [
            down_weight.shape,
            gate_weight.shape,
            up_weight.shape,
            out_weight.shape,
            query_weight.shape,
            key_weight.shape,
            value_weight.shape,
        ],
    )
    return (
        block_out,
        input_grad,
        gain_sums[0],
        query_grad,
        key_grad,
        value_grad,
        out_grad,
        gain_sums[1],
        gate_grad,
        up_grad,
        down_grad,
    )


def solution(mesh):
    sizes = tuple(mesh.shape[name] for name in ("fsdp", "ctx", "tp"))
    in_specs = (
        P("fsdp", "ctx", None),
        P("fsdp", None),
        P("fsdp"),
        P("fsdp", "tp"),
        P("fsdp", "tp"),
        P("fsdp", "tp"),
        P("tp", "fsdp"),
        P("fsdp"),
        P("fsdp", "tp"),
        P("fsdp", "tp"),
        P("tp", "fsdp"),
        P("fsdp", "ctx", None),
    )
    out_specs = (
        P("fsdp", "ctx", None),
        P("fsdp", "ctx", None),
        P("fsdp"),
        P("fsdp", "tp"),
        P("fsdp", "tp"),
        P("fsdp", "tp"),
        P("tp", "fsdp"),
        P("fsdp"),
        P("fsdp", "tp"),
        P("fsdp", "tp"),
        P("tp", "fsdp"),
    )
    return jax.shard_map(
        functools.partial(shards, sizes),
        mesh=mesh,
        in_specs=in_specs,
        out_specs=out_specs,
        check_vma=False,
    )
```

```python
import functools

import jax
import jax.numpy as jnp
from jax import lax
from jax.experimental import pallas as pl
from jax.experimental.pallas import tpu as pltpu
from jax.sharding import PartitionSpec as P

HD = 64
WINDOW = 1024
NORM_EPS = 1e-05
ROPE_BASE = 500000.0
MASK_FILL = -1e30
LANES = 128
F32 = jnp.float32
BF16 = jnp.bfloat16


def dot_rows(matrix, other_side):
    return jnp.dot(matrix, other_side, preferred_element_type=F32)


def dot_back(matrix, other_side):
    return lax.dot_general(matrix, other_side, (((1,), (1,)), ((), ())), preferred_element_type=F32)


def dot_outer(matrix, other_side):
    return lax.dot_general(matrix, other_side, (((0,), (0,)), ((), ())), preferred_element_type=F32)


def tie(*values):
    return lax.optimization_barrier(values)


def take(array, start, size, axis):
    return lax.dynamic_slice_in_dim(array, start, size, axis)


def doc_positions(segments):
    seq_count, seq_length = segments.shape
    index_grid = jnp.broadcast_to(jnp.arange(seq_length, dtype=jnp.int32)[None, :], segments.shape)
    begins = jnp.concatenate(
        [jnp.ones((seq_count, 1), dtype=bool), segments[:, 1:] != segments[:, :-1]], axis=1
    )
    return index_grid - lax.cummax(jnp.where(begins, index_grid, 0), axis=1)


def rope_tables(positions):
    half_size = HD // 2
    frequency = ROPE_BASE ** (-(jnp.arange(half_size, dtype=F32) * 2.0 / HD))
    angles = positions.astype(F32)[:, None] * frequency
    cosine, sine = jnp.cos(angles), jnp.sin(angles)
    return jnp.concatenate([cosine] * 4, axis=1), jnp.concatenate([-sine, sine] * 2, axis=1)


def rotate(vectors, cosine, signed_sine):
    width = vectors.shape[1]
    half = HD // 2
    ahead = jnp.concatenate([vectors[:, half:], vectors[:, :half]], axis=1)
    behind = jnp.concatenate([vectors[:, -half:], vectors[:, :-half]], axis=1)
    first = (jnp.arange(width) % HD < half)[None, :]
    reps = width // LANES
    return vectors * jnp.tile(cosine, (1, reps)) + jnp.where(first, ahead, behind) * jnp.tile(
        signed_sine, (1, reps)
    )


def row_scale_of(values):
    return lax.rsqrt(jnp.mean(values * values, axis=-1, keepdims=True) + NORM_EPS)


def norm_back(grad_hidden, gain, normed, row_scale, residual_grad):
    grad_normed = grad_hidden * gain
    return residual_grad + row_scale * (
        grad_normed - normed * jnp.mean(grad_normed * normed, axis=-1, keepdims=True)
    )


def attend_forward_body(lead, heads, group, q_ref, kv_ref, qseg_ref, kseg_ref, mixed_ref, lse_ref):
    block = q_ref.shape[1]
    reach = kseg_ref.shape[-1]
    start = pl.multiple_of(pl.program_id(1) * block, block)
    window = kv_ref.at[0, pl.ds(start, reach), :]
    distance = (
        lax.broadcasted_iota(jnp.int32, (block, reach), 0)
        + lead
        - lax.broadcasted_iota(jnp.int32, (block, reach), 1)
    )
    allowed = (qseg_ref[0] == kseg_ref[0, 0]) & (distance >= 0) & (distance < WINDOW)
    bias = jnp.where(allowed, 0.0, MASK_FILL)
    lane = lax.broadcasted_iota(jnp.int32, (block, LANES), 1)
    log_sums = jnp.zeros((block, LANES), F32)
    kv_width = heads // group * HD
    outs = []
    for head in range(heads):
        shared = head // group * HD
        keys = window[:, shared : shared + HD]
        values = window[:, kv_width + shared : kv_width + shared + HD]
        scores = dot_back(q_ref[0, :, head * HD : (head + 1) * HD], keys) + bias
        row_max = jnp.max(scores, axis=-1, keepdims=True)
        exponent = jnp.exp(scores - row_max)
        row_total = jnp.sum(exponent, axis=-1, keepdims=True)
        probs = (exponent * (1.0 / row_total)).astype(BF16)
        outs.append(dot_rows(probs, values))
        log_sums = jnp.where(lane == head, row_max + jnp.log(row_total), log_sums)
    mixed_ref[0] = jnp.concatenate(outs, axis=1).astype(BF16)
    lse_ref[0] = log_sums


def attend_backward_body(
    lead, heads, group, q_ref, kv_ref, grad_ref, lse_ref, qseg_ref, kseg_ref, dq_ref, dkv_ref
):
    block = q_ref.shape[1]
    reach = block + lead
    step = pl.program_id(1)
    start = pl.multiple_of(step * block, block)
    window = kv_ref.at[0, pl.ds(start, reach), :]

    @pl.when(step == 0)
    def _():
        dkv_ref[...] = jnp.zeros_like(dkv_ref)

    distance = (
        lax.broadcasted_iota(jnp.int32, (reach, block), 1)
        + lead
        - lax.broadcasted_iota(jnp.int32, (reach, block), 0)
    )
    same = kseg_ref[0, pl.ds(start, reach), :] == qseg_ref[0]
    bias = jnp.where(same & (distance >= 0) & (distance < WINDOW), 0.0, MASK_FILL)
    query_grad, keys_grad = backward_tile(
        heads,
        group,
        lambda head: q_ref[0, :, head * HD : (head + 1) * HD],
        lambda head: grad_ref[0, :, head * HD : (head + 1) * HD],
        lambda head: lse_ref[0, head : head + 1, :],
        lambda at: window[:, at * HD : (at + 1) * HD],
        bias,
    )
    dq_ref[0] = query_grad
    dkv_ref[0, pl.ds(start, reach), :] += keys_grad


def backward_tile(heads, group, query_of, grad_of, log_sum_of, window_of, bias):
    key_grads, value_grads, query_grads = [], [], []
    shared_heads = heads // group
    for shared in range(shared_heads):
        keys, values = window_of(shared), window_of(shared_heads + shared)
        key_sum = value_sum = None
        for member in range(group):
            head = shared * group + member
            query, grad = query_of(head), grad_of(head)
            probs = jnp.exp(dot_back(keys, query) + bias - log_sum_of(head))
            grad_probs = dot_back(values, grad)
            spread = jnp.sum(probs * grad_probs, axis=0, keepdims=True)
            grad_scores = (probs * (grad_probs - spread)).astype(BF16)
            value_part = dot_rows(probs.astype(BF16), grad)
            key_part = dot_rows(grad_scores, query)
            query_grads.append(dot_outer(grad_scores, keys) * HD**-0.5)
            value_sum = value_part if value_sum is None else value_sum + value_part
            key_sum = key_part if key_sum is None else key_sum + key_part
        key_grads.append(key_sum)
        value_grads.append(value_sum)
    return jnp.concatenate(query_grads, axis=1), jnp.concatenate(key_grads + value_grads, axis=1)


def attention_plan(span, window):
    blocks_back = -(-(window - 1) // span)
    base = (blocks_back * span - (window - 1)) // LANES * LANES
    return blocks_back, base, blocks_back * span - base


def key_tiles(key_segments, base, lead, block, span):
    return jnp.stack(
        [
            key_segments[:, base + at : base + at + block + lead]
            for at in range(0, span, block)
        ],
        axis=1,
    )[:, :, None, :]


def attend_forward(query, keys_values, query_segments, key_segments, base, lead, group):
    seqs, span, width = query.shape
    block = min(LANES, span)
    heads = width // HD
    reach = block + lead
    keys_used = keys_values[:, base:]
    return pl.pallas_call(
        functools.partial(attend_forward_body, lead, heads, group),
        grid=(seqs, span // block),
        in_specs=[
            pl.BlockSpec((1, block, width), lambda s, i: (s, i, 0)),
            pl.BlockSpec((1,) + keys_used.shape[1:], lambda s, i: (s, 0, 0)),
            pl.BlockSpec((1, block, 1), lambda s, i: (s, i, 0)),
            pl.BlockSpec((1, 1, 1, reach), lambda s, i: (s, i, 0, 0)),
        ],
        out_specs=[
            pl.BlockSpec((1, block, width), lambda s, i: (s, i, 0)),
            pl.BlockSpec((1, block, LANES), lambda s, i: (s, i, 0)),
        ],
        out_shape=[
            jax.ShapeDtypeStruct(query.shape, BF16),
            jax.ShapeDtypeStruct((seqs, span, LANES), F32),
        ],
        compiler_params=pltpu.CompilerParams(vmem_limit_bytes=40 << 20),
        cost_estimate=pl.CostEstimate(
            flops=70 * seqs * span * reach * width, bytes_accessed=4 << 20, transcendentals=0
        ),
        name="attend_forward",
    )(query, keys_used, query_segments[:, :, None], key_tiles(key_segments, base, lead, block, span))


def attend_backward(
    query, keys_values, grad_mixed, log_sums, query_segments, key_segments, base, lead, group
):
    seqs, span, width = query.shape
    block = min(LANES, span)
    heads = width // HD
    reach = block + lead
    keys_used = keys_values[:, base:]
    whole_keys = pl.BlockSpec((1,) + keys_used.shape[1:], lambda s, i: (s, 0, 0))
    rows = pl.BlockSpec((1, block, width), lambda s, i: (s, i, 0))
    grad_query, grad_keys_values = pl.pallas_call(
        functools.partial(attend_backward_body, lead, heads, group),
        grid=(seqs, span // block),
        in_specs=[
            rows,
            whole_keys,
            rows,
            pl.BlockSpec((1, heads, block), lambda s, i: (s, 0, i)),
            pl.BlockSpec((1, 1, block), lambda s, i: (s, 0, i)),
            pl.BlockSpec((1, keys_used.shape[1], 1), lambda s, i: (s, 0, 0)),
        ],
        out_specs=[rows, whole_keys],
        out_shape=[
            jax.ShapeDtypeStruct(query.shape, F32),
            jax.ShapeDtypeStruct(keys_used.shape, F32),
        ],
        compiler_params=pltpu.CompilerParams(vmem_limit_bytes=40 << 20),
        cost_estimate=pl.CostEstimate(
            flops=85 * seqs * span * reach * width, bytes_accessed=6 << 20, transcendentals=0
        ),
        name="attend_backward",
    )(
        query,
        keys_used,
        grad_mixed,
        log_sums,
        query_segments[:, None, :],
        key_segments[:, base:, None],
    )
    return grad_query, jnp.pad(grad_keys_values, ((0, 0), (base, 0), (0, 0)))


def whole(array):
    return pl.BlockSpec(array.shape, lambda *at: (0,) * array.ndim)


def kernel_cost(flops, moved):
    return pl.CostEstimate(flops=flops, bytes_accessed=moved, transcendentals=0)


def feed_forward_body(sizes, hidden_ref, *refs):
    count = len(sizes)
    gate_refs, up_refs = refs[:count], refs[count : 2 * count]
    gate_ref, up_ref, act_ref = refs[2 * count :]

    def project(pieces):
        total, at = None, 0
        for size, piece in zip(sizes, pieces):
            value = dot_rows(hidden_ref[:, at : at + size], piece[...])
            total = value if total is None else total + value
            at += size
        return total

    gate_value, up_value = project(gate_refs), project(up_refs)
    gate_ref[...] = gate_value
    up_ref[...] = up_value
    act_ref[...] = (gate_value * jax.nn.sigmoid(gate_value) * up_value).astype(BF16)


def feed_forward(hidden, gate_pieces, up_pieces, cut, columns):
    rows = hidden.shape[0]
    tile = min(512, columns)
    steps = columns // tile
    own = lambda w: pl.BlockSpec((w.shape[0], tile), lambda i: (0, cut * steps + i))
    rest = lambda w: pl.BlockSpec((w.shape[0], tile), lambda i: (0, i))
    specs = [own(gate_pieces[0])] + [rest(w) for w in gate_pieces[1:]]
    out = pl.BlockSpec((rows, tile), lambda i: (0, i))
    return pl.pallas_call(
        functools.partial(feed_forward_body, tuple(w.shape[0] for w in gate_pieces)),
        grid=(steps,),
        in_specs=[whole(hidden)] + specs + specs,
        out_specs=[out] * 3,
        out_shape=[
            jax.ShapeDtypeStruct((rows, columns), F32),
            jax.ShapeDtypeStruct((rows, columns), F32),
            jax.ShapeDtypeStruct((rows, columns), BF16),
        ],
        compiler_params=pltpu.CompilerParams(vmem_limit_bytes=40 << 20),
        cost_estimate=kernel_cost(6 * rows * columns * hidden.shape[1], 8 << 20),
        name="feed_forward",
    )(hidden, *gate_pieces, *up_pieces)


def feed_backward_body(sizes, grad_ref, *refs):
    count = len(sizes)
    gate_ref, up_ref, grad_gate_ref, grad_up_ref = refs[count:]
    grad_act, at = None, 0
    for size, piece in zip(sizes, refs[:count]):
        value = dot_back(grad_ref[:, at : at + size], piece[...])
        grad_act = value if grad_act is None else grad_act + value
        at += size
    gate_value = gate_ref[...]
    sigmoid_gate = jax.nn.sigmoid(gate_value)
    grad_up = grad_act * sigmoid_gate
    grad_gate_ref[...] = (
        grad_up * up_ref[...] * (1.0 + gate_value * (1.0 - sigmoid_gate))
    ).astype(BF16)
    grad_up_ref[...] = (grad_up * gate_value).astype(BF16)


def feed_backward(grad, down_pieces, gate_value, up_value, cut):
    rows, columns = gate_value.shape
    tile = min(512, columns)
    steps = columns // tile
    own = lambda w: pl.BlockSpec((tile, w.shape[1]), lambda i: (cut * steps + i, 0))
    rest = lambda w: pl.BlockSpec((tile, w.shape[1]), lambda i: (i, 0))
    out = pl.BlockSpec((rows, tile), lambda i: (0, i))
    return pl.pallas_call(
        functools.partial(feed_backward_body, tuple(w.shape[1] for w in down_pieces)),
        grid=(steps,),
        in_specs=[whole(grad), own(down_pieces[0])]
        + [rest(w) for w in down_pieces[1:]]
        + [out, out],
        out_specs=[out] * 2,
        out_shape=[jax.ShapeDtypeStruct((rows, columns), BF16)] * 2,
        compiler_params=pltpu.CompilerParams(vmem_limit_bytes=40 << 20),
        cost_estimate=kernel_cost(4 * rows * columns * grad.shape[1], 8 << 20),
        name="feed_backward",
    )(grad, *down_pieces, gate_value, up_value)


def project_body(cuts, steps, terms, pieces, transposed, sibling_ref, *refs):
    first_ref, second_ref, total_ref = refs[-3:]
    step = pl.program_id(0)
    lefts = refs[: cuts * terms]
    weights = refs[cuts * terms : -3]

    @pl.when(step == 0)
    def _():
        total_ref[...] = jnp.zeros_like(total_ref)

    for cut in range(cuts):

        @pl.when(step // steps == cut)
        def _():
            at = 0
            for piece in range(pieces):
                value = None
                for term in range(terms):
                    left = lefts[cut * terms + term][...]
                    weight = weights[(cut * terms + term) * pieces + piece][...]
                    part = dot_back(left, weight) if transposed else dot_rows(left, weight)
                    value = part if value is None else value + part
                total_ref[:, at : at + value.shape[1]] += value
                at += value.shape[1]

    @pl.when(step == cuts * steps - 1)
    def _():
        half = total_ref.shape[0] // 2
        mine = pl.multiple_of(sibling_ref[0] * half, half)
        theirs = pl.multiple_of((1 - sibling_ref[0]) * half, half)
        first_ref[...] = total_ref[pl.ds(theirs, half), :].astype(BF16)
        second_ref[...] = total_ref[pl.ds(mine, half), :]


def project(sibling, lefts, weights, width, transposed):
    cuts, terms, pieces = len(lefts), len(lefts[0]), len(weights[0][0])
    rows, columns = lefts[0][0].shape
    tile = min(512, columns)
    steps = columns // tile
    in_specs = [pl.BlockSpec(memory_space=pltpu.SMEM)]
    operands = []

    def clipped(cut):
        return lambda i: jnp.clip(i - cut * steps, 0, steps - 1)

    for cut in range(cuts):
        for left in lefts[cut]:
            in_specs.append(pl.BlockSpec((rows, tile), lambda i, f=clipped(cut): (0, f(i))))
            operands.append(left)
    for cut in range(cuts):
        for term in weights[cut]:
            for piece, weight in enumerate(term):
                offset = cut * steps if piece == 0 else 0
                if transposed:
                    spec = pl.BlockSpec(
                        (weight.shape[0], tile), lambda i, f=clipped(cut), o=offset: (0, o + f(i))
                    )
                else:
                    spec = pl.BlockSpec(
                        (tile, weight.shape[1]), lambda i, f=clipped(cut), o=offset: (o + f(i), 0)
                    )
                in_specs.append(spec)
                operands.append(weight)
    half_rows = jax.ShapeDtypeStruct((rows // 2, width), BF16)
    return pl.pallas_call(
        functools.partial(project_body, cuts, steps, terms, pieces, transposed),
        grid=(cuts * steps,),
        in_specs=in_specs,
        out_specs=[whole(half_rows)] * 2,
        out_shape=[half_rows, jax.ShapeDtypeStruct((rows // 2, width), F32)],
        scratch_shapes=[pltpu.VMEM((rows, width), F32)],
        compiler_params=pltpu.CompilerParams(vmem_limit_bytes=48 << 20),
        cost_estimate=kernel_cost(3 * terms * rows * columns * cuts * width, 16 << 20),
        name="project",
    )(sibling.reshape(1), *operands)


CHUNK_ROWS, CHUNK_COLUMNS = 256, 1024


def outer_sum_body(split, groups, left_ref, left_other_ref, *refs):
    out_ref = refs[-1]
    rights, others = refs[:groups], refs[groups : 2 * groups]
    blocks = left_ref.shape[1] // CHUNK_ROWS
    for group in range(groups):

        def emit():
            for block in range(blocks):
                rows = slice(block * CHUNK_ROWS, (block + 1) * CHUNK_ROWS)
                value = dot_outer(left_ref[:, rows], rights[group][...])
                value += dot_outer(left_other_ref[:, rows], others[group][...])
                width = value.shape[1]
                out_ref[0, :, block * width : (block + 1) * width] = value.astype(BF16)

        if groups == 1:
            emit()
        else:
            pl.when(pl.program_id(0) // split == group)(emit)


def outer_sum(pool, at, count, left, left_other, rights, rights_other):
    groups = len(rights)
    rows = left.shape[0]
    columns = CHUNK_ROWS * CHUNK_COLUMNS // rights[0].shape[1]
    split = left.shape[1] // columns
    left_spec = pl.BlockSpec((rows, columns), lambda i: (0, lax.rem(i, split)))
    operands = (left, left_other, *rights, *rights_other)
    in_specs = [left_spec] * 2 + [whole(value) for value in operands[2:]]
    aliases = {}
    if pool is not None:
        operands += (pool,)
        in_specs.append(pl.BlockSpec(memory_space=pl.ANY))
        aliases = {len(operands) - 1: 0}
    return pl.pallas_call(
        functools.partial(outer_sum_body, split, groups),
        grid=(split * groups,),
        in_specs=in_specs,
        out_specs=pl.BlockSpec((1, CHUNK_ROWS, CHUNK_COLUMNS), lambda i: (at + i, 0, 0)),
        out_shape=jax.ShapeDtypeStruct((count, CHUNK_ROWS, CHUNK_COLUMNS), BF16),
        input_output_aliases=aliases,
        compiler_params=pltpu.CompilerParams(vmem_limit_bytes=48 << 20),
        cost_estimate=kernel_cost(
            4 * split * groups * rows * CHUNK_ROWS * CHUNK_COLUMNS, 4 << 20
        ),
        name="outer_sum",
    )(*operands)


def widen_body(starts, pool_ref, *out_refs):
    step = pl.program_id(0)
    group = pool_ref.shape[0]
    last = len(starts) - 1
    for at, start in enumerate(starts):
        stop = starts[at + 1] // group if at < last else pl.num_programs(0)

        @pl.when((step >= start // group) & (step < stop))
        def _():
            if at < last - 1:
                for piece in range(group):
                    rows = slice(piece * CHUNK_ROWS, (piece + 1) * CHUNK_ROWS)
                    out_refs[at][rows] = pool_ref[piece].astype(F32)
            elif at == last - 1:
                half = CHUNK_COLUMNS // 2
                for side in range(2 * group):
                    rows = slice(side * CHUNK_ROWS, (side + 1) * CHUNK_ROWS)
                    columns = slice(side % 2 * half, (side % 2 + 1) * half)
                    out_refs[at][rows] = pool_ref[side // 2, :, columns].astype(F32)
            else:
                width = out_refs[at].shape[1]
                for block in range(CHUNK_COLUMNS // (2 * width)):
                    rows = slice(block * CHUNK_ROWS, (block + 1) * CHUNK_ROWS)
                    left = 2 * block * width
                    value = pool_ref[0, :, left : left + 2 * width].astype(F32)
                    out_refs[at][rows] = value[:, :width]
                    out_refs[at + 1][rows] = value[:, width:]


def widen(pool, starts, shapes, group):
    specs = []
    steps = pool.shape[0] // group
    for at, shape in enumerate(shapes):
        which = min(at, len(starts) - 1)
        first = starts[which] // group
        stop = starts[which + 1] // group if which + 1 < len(starts) else steps
        block = (group * CHUNK_ROWS, CHUNK_COLUMNS)
        if which == len(starts) - 1:
            block = shape
        elif which == len(starts) - 2:
            block = (2 * group * CHUNK_ROWS, shape[1])
        down = shape[0] // block[0]

        def place(i, first=first, size=stop - first, down=down):
            k = jnp.clip(i - first, 0, size - 1)
            return lax.rem(k, down), k // down

        specs.append(pl.BlockSpec(block, place))
    return pl.pallas_call(
        functools.partial(widen_body, starts),
        grid=(steps,),
        in_specs=[pl.BlockSpec((group, CHUNK_ROWS, CHUNK_COLUMNS), lambda i: (i, 0, 0))],
        out_specs=specs,
        out_shape=[jax.ShapeDtypeStruct(shape, F32) for shape in shapes],
        compiler_params=pltpu.CompilerParams(vmem_limit_bytes=48 << 20),
        cost_estimate=kernel_cost(1, 45 << 20),
        name="widen",
    )(pool)


def tail_body(plan, *refs):
    heads, group, lead, starts, count = plan
    (
        pool_in, hidden_m_send, hidden_a_send, feed_chip, stored,
        pool_ref, sum_ref, near_ref, across_ref, feed_land, grad_ref, gain_out_ref,
        gate_land, up_land, hidden_m_land, hidden_a_land, branch_land, mixed_land, qkv_land,
        grad_mixed_ref, dq_ref, dkv_ref, kv_send, kv_land, qkv_grad_ref,
        first_ref, second_ref, core_land, chip_ref, y_land, total_ref, other_ref,
        middle_y, middle_total, middle_other, branch_ref, branch_send,
        gains_ref, gain_send, gain_land, gain_mine, gain_all, gain_send_sem, gain_recv_sem,
        own_buf, near_buf, part_buf, across_buf, total_buf, piece_buf,
        x_send, x_recv, tp_send, tp_recv, kv_send_sem, kv_recv_sem,
        send_sem, land_sem, cross_send, cross_land, keep_sem, load_sem, piece_sem,
        loaded, loaded_sem,
    ) = refs
    (
        gate_refs, up_refs, hidden_m_ref, hidden_a_ref, mixed_ref, out_refs,
        query_ref, keys_ref, log_ref, query_seg_ref, key_seg_ref, cosine_ref, sine_ref,
        qkv_refs, inputs_ref, scale_ref, gain_ref, grad_middle_ref,
        middle_chip, cotangent_ref, middle_scale, middle_gain,
    ) = loaded
    stored_gate, stored_up, stored_mixed = stored[0], stored[1], stored[4]
    rows, width = inputs_ref.shape
    half, part = width // 2, width // 4
    half_rows = rows // 2
    mesh_id = pl.DeviceIdType.MESH
    shard, ctx, tp = (lax.axis_index(name) for name in ("fsdp", "ctx", "tp"))
    sibling = lax.rem(tp, 2)
    core = tp + 1 - 2 * sibling
    across_y = lax.rem(tp + 2, 4)
    partner = 1 - shard
    pair = ctx + 1 - 2 * lax.rem(ctx, 2)
    across = 3 - ctx
    is_end = (ctx == 0) | (ctx == 3)
    is_middle = jnp.logical_not(is_end)

    kv_land[...] = jnp.zeros_like(kv_land)
    dkv_ref[...] = jnp.zeros_like(dkv_ref)
    gains_ref[...] = jnp.zeros_like(gains_ref)

    barrier = pltpu.get_barrier_semaphore()
    others = [{"fsdp": partner}, {"tp": core}, {"tp": across_y}]
    others += [{"ctx": lax.rem(ctx + step, 4)} for step in (1, 2, 3)]
    for other in others:
        pl.semaphore_signal(barrier, inc=1, device_id=other, device_id_type=mesh_id)
    pl.semaphore_wait(barrier, len(others))

    def x_copy(at, source, land):
        return pltpu.make_async_remote_copy(
            src_ref=source, dst_ref=land, send_sem=x_send.at[at], recv_sem=x_recv.at[at],
            device_id={"fsdp": partner}, device_id_type=mesh_id,
        )

    cuts = len(gate_refs)
    gate_copies = [x_copy(i, stored_gate[i], gate_land[i]) for i in range(cuts)]
    up_copies = [x_copy(cuts + i, stored_up[i], up_land[i]) for i in range(cuts)]
    hidden_m_copy = x_copy(2 * cuts, hidden_m_send, hidden_m_land)
    branch_copy = x_copy(2 * cuts + 1, branch_send, branch_land)
    mixed_copy = x_copy(2 * cuts + 2, stored_mixed, mixed_land)
    hidden_a_copy = x_copy(2 * cuts + 3, hidden_a_send, hidden_a_land)
    qkv_copy = x_copy(2 * cuts + 4, qkv_grad_ref, qkv_land)
    queue = gate_copies + [hidden_m_copy] + up_copies
    queue += [branch_copy, mixed_copy, qkv_copy, hidden_a_copy]

    def send_next(first, last):
        for at in range(first, last):
            if at >= 2:
                queue[at - 2].wait_send()
            queue[at].start()

    def tp_copy(at, source, land, target):
        return pltpu.make_async_remote_copy(
            src_ref=source, dst_ref=land, send_sem=tp_send.at[at], recv_sem=tp_recv.at[at],
            device_id={"tp": target}, device_id_type=mesh_id,
        )

    split = CHUNK_ROWS // own_buf.shape[0]
    count = count * split

    def share(ref, k):
        size = CHUNK_ROWS // split
        return ref.at[k // split, pl.ds(pl.multiple_of(lax.rem(k, split) * size, size), size), :]

    def to_pair(source, land, k):
        return pltpu.make_async_remote_copy(
            src_ref=source, dst_ref=share(land, k), send_sem=send_sem.at[k],
            recv_sem=land_sem.at[k], device_id={"ctx": pair}, device_id_type=mesh_id,
        )

    def inward_copy(k):
        return to_pair(share(pool_ref, k), near_ref, k)

    def outward_copy(k):
        return to_pair(total_buf.at[lax.rem(k, 2)], sum_ref, k)

    def cross_copy(k):
        return pltpu.make_async_remote_copy(
            src_ref=part_buf.at[lax.rem(k, 4)], dst_ref=share(across_ref, k),
            send_sem=cross_send.at[k], recv_sem=cross_land.at[k],
            device_id={"ctx": across}, device_id_type=mesh_id,
        )

    def keep_copy(k):
        return pltpu.make_async_copy(
            total_buf.at[lax.rem(k, 2)], share(sum_ref, k), keep_sem.at[k]
        )

    def load(source, buffer, at):
        return pltpu.make_async_copy(source, buffer, load_sem.at[at])

    lag = 2

    def inward(k):
        inward_copy(k).wait_recv()
        loads = [load(share(pool_ref, k), own_buf, 0), load(share(near_ref, k), near_buf, 1)]
        for copy in loads:
            copy.start()
        for copy in loads:
            copy.wait()
        part_buf[lax.rem(k, 4)] = (own_buf[...].astype(F32) + near_buf[...].astype(F32)).astype(
            BF16
        )
        cross_copy(k).start()

    def outward(k, reuse):
        cross_copy(k).wait_recv()
        copy = load(share(across_ref, k), across_buf, 2)
        copy.start()
        if reuse:
            keep_copy(k - 2).wait()
            outward_copy(k - 2).wait_send()
        copy.wait()
        total_buf[lax.rem(k, 2)] = (
            part_buf[lax.rem(k, 4)].astype(F32) + across_buf[...].astype(F32)
        ).astype(BF16)
        cross_copy(k).wait_send()
        outward_copy(k).start()
        keep_copy(k).start()

    ahead = 2 * split

    def send_piece(k, carry):
        inward_copy(k).wait_send()

        @pl.when(k + ahead < count)
        def _():
            inward_copy(k + ahead).start()

        return carry

    def pump(first, last):
        pump_steps(first * split, last * split)

    def pump_steps(first, last):

        @pl.when(is_end)
        def _():
            lax.fori_loop(min(first, count), min(last, count), send_piece, 0)

        @pl.when(is_middle)
        def _():
            k = first
            while k < min(last, lag + 2):
                inward(jnp.int32(k))
                if k >= lag:
                    outward(jnp.int32(k - lag), False)
                k += 1
            if k < min(last, count):

                def both(at, carry):
                    inward(at)
                    outward(at - lag, True)
                    return carry

                lax.fori_loop(k, min(last, count), both, 0)
            k = max(k, count)
            while k < min(last, count + lag):
                outward(jnp.int32(k - lag), True)
                k += 1

    @pl.when(is_end)
    def _():
        for k in range(ahead):
            inward_copy(jnp.int32(k)).start()

    send_next(0, 2)
    middle_y_copy = tp_copy(3, stored[-4], middle_y, across_y)
    middle_core_copy = tp_copy(4, middle_total, middle_other, core)
    feed_copy = tp_copy(5, feed_chip, feed_land, across_y)
    middle_y_copy.start()
    fills = [
        pltpu.make_async_copy(source, buffer, loaded_sem.at[at])
        for at, (source, buffer) in enumerate(
            zip(jax.tree.leaves(stored), jax.tree.leaves(loaded))
        )
    ]
    for fill in fills:
        fill.start()
    for fill in fills:
        fill.wait()
    pump_steps(0, 3)

    theirs = pl.multiple_of((1 - sibling) * half_rows, half_rows)
    mine = pl.multiple_of(sibling * half_rows, half_rows)
    step_rows = 64
    odd = lax.rem(ctx, 2)
    near_send = pl.multiple_of(odd * part, part)
    far_send = pl.multiple_of((1 - odd) * part, part)

    def middle_rows(source, base):
        def body(step, total):
            at = pl.multiple_of(step * step_rows, step_rows)
            here = pl.ds(pl.multiple_of(base + at, step_rows), step_rows)
            normed = grad_middle_ref[here, :]
            hidden = source[pl.ds(at, step_rows), :].astype(F32)
            grad = hidden * middle_gain[...]
            mean = jnp.sum(grad * normed, axis=-1, keepdims=True) * (1.0 / width)
            value = cotangent_ref[here, :].astype(F32) + middle_scale[here, :] * (
                grad - normed * mean
            )
            grad_middle_ref[here, :] = value
            low = value.astype(BF16)
            branch_ref[here, :] = low
            branch_send[here, pl.ds(near_send, part)] = low[:, half : half + part]
            branch_send[here, pl.ds(far_send, part)] = low[:, half + part :]
            return total + jnp.sum(hidden * normed, axis=0, keepdims=True)

        return lax.fori_loop(0, half_rows // step_rows, body, jnp.zeros((1, width), F32))

    middle_y_copy.wait_recv()
    middle_total[...] = (middle_chip[...].astype(F32) + middle_y[...].astype(F32)).astype(BF16)
    middle_core_copy.start()
    feed_gain = middle_rows(middle_total, mine)
    pump_steps(3, 4)
    middle_core_copy.wait_recv()
    gains_ref[1:2, :] = feed_gain + middle_rows(middle_other, theirs)
    send_next(2, 3)

    grad_mixed = None
    at = 0
    for piece in out_refs:
        value = dot_back(branch_ref[:, at : at + piece.shape[1]], piece[...])
        grad_mixed = value if grad_mixed is None else grad_mixed + value
        at += piece.shape[1]
    grad_mixed_ref[...] = grad_mixed.astype(BF16)

    tile = log_ref.shape[2]
    tiles = rows // tile
    reach = tile + lead

    def attend(step, carry):
        @pl.when(is_end)
        def _():
            send_piece(step + lag + 2, 0)

        @pl.when(is_middle)
        def _():
            inward(step + lag + 2)
            outward(step + 2, True)

        start = pl.multiple_of(step * tile, tile)
        distance = (
            lax.broadcasted_iota(jnp.int32, (reach, tile), 1)
            + lead
            - lax.broadcasted_iota(jnp.int32, (reach, tile), 0)
        )
        same = key_seg_ref[pl.ds(start, reach), :] == query_seg_ref[step]
        bias = jnp.where(same & (distance >= 0) & (distance < WINDOW), 0.0, MASK_FILL)
        query_grad, keys_grad = backward_tile(
            heads,
            group,
            lambda head: query_ref[pl.ds(start, tile), head * HD : (head + 1) * HD],
            lambda head: grad_mixed_ref[pl.ds(start, tile), head * HD : (head + 1) * HD],
            lambda head: log_ref[step, head : head + 1, :],
            lambda at: keys_ref[pl.ds(start, reach), at * HD : (at + 1) * HD],
            bias,
        )
        dq_ref[pl.ds(start, tile), :] = query_grad
        dkv_ref[pl.ds(start, reach), :] += keys_grad
        return carry

    lax.fori_loop(0, tiles, attend, 0)
    send_next(3, 4)

    for back in (1, 2):
        kv_send[back - 1] = dkv_ref[(2 - back) * rows : (3 - back) * rows, :].astype(BF16)

    def kv_copy(back):
        return pltpu.make_async_remote_copy(
            src_ref=kv_send.at[back - 1], dst_ref=kv_land.at[back - 1],
            send_sem=kv_send_sem.at[back - 1], recv_sem=kv_recv_sem.at[back - 1],
            device_id={"ctx": lax.rem(ctx + 4 - back, 4)}, device_id_type=mesh_id,
        )

    for back in (1, 2):

        @pl.when(ctx >= back)
        def _():
            kv_copy(back).start()

    def piece_copy(slot, k):
        return pltpu.make_async_copy(piece_buf.at[slot], pool_ref.at[k], piece_sem.at[slot])

    def put(first, values):
        for at, make in enumerate(values):
            slot = at % 2
            if at >= 2:
                piece_copy(slot, first + at - 2).wait()
            piece_buf[slot] = make()
            piece_copy(slot, first + at).start()
        for at in range(max(0, len(values) - 2), len(values)):
            piece_copy(at % 2, first + at).wait()

    def outer(left, left_other, right, right_other, block):
        columns = slice(block * CHUNK_ROWS, (block + 1) * CHUNK_ROWS)
        return (
            dot_outer(left[:, columns], right[...]) + dot_outer(left_other[:, columns], right_other[...])
        ).astype(BF16)

    def feed_pieces(rights, rights_other):
        return [
            functools.partial(outer, hidden_m_ref, hidden_m_land, right, right_other, block)
            for right, right_other in zip(rights, rights_other)
            for block in range(half // CHUNK_ROWS)
        ]

    pump(4, 5)
    for copy in gate_copies + [hidden_m_copy]:
        copy.wait_recv()
    put(starts[1], feed_pieces(gate_refs, gate_land))
    send_next(4, 5)
    pump(5, 6)

    for back in (1, 2):

        @pl.when(ctx + back < 4)
        def _():
            kv_copy(back).wait_recv()

    kv_width = dkv_ref.shape[1] // 2
    q_width = dq_ref.shape[1]
    cosine, sine = cosine_ref[...], sine_ref[...]
    front = lax.rem(lax.broadcasted_iota(jnp.int32, (rows, LANES), 1), HD) < HD // 2

    def unrotate(value):
        swapped = jnp.where(
            front, pltpu.roll(value, LANES - HD // 2, 1), pltpu.roll(value, HD // 2, 1)
        )
        return (value * cosine - swapped * sine).astype(BF16)

    for at in range(0, q_width, LANES):
        qkv_grad_ref[:, at : at + LANES] = unrotate(dq_ref[:, at : at + LANES])
    kv_sum = dkv_ref[2 * rows :, :]
    for back in range(2):
        kv_sum = kv_sum + kv_land[back].astype(F32)
    for at in range(0, kv_width, LANES):
        qkv_grad_ref[:, q_width + at : q_width + at + LANES] = unrotate(
            kv_sum[:, at : at + LANES]
        )
    qkv_grad_ref[:, q_width + kv_width :] = kv_sum[:, kv_width:].astype(BF16)

    first_copy = tp_copy(0, first_ref, core_land, core)
    y_copy = tp_copy(1, chip_ref, y_land, across_y)
    total_copy = tp_copy(2, total_ref, other_ref, core)

    def back_project(start, store):
        at = 0
        for piece in qkv_refs:
            size = piece.shape[0]
            store(at, size, dot_back(qkv_grad_ref[pl.ds(start, half_rows), :], piece[...]))
            at += size

    def store_first(at, size, value):
        first_ref[:, at : at + size] = value.astype(BF16)

    def store_second(at, size, value):
        second_ref[:, at : at + size] = value

    back_project(theirs, store_first)
    first_copy.start()
    back_project(mine, store_second)
    pump(6, 8)
    first_copy.wait_recv()
    chip_ref[...] = (second_ref[...] + core_land[...].astype(F32)).astype(BF16)
    y_copy.start()
    send_next(5, 6)
    pump(8, 10)


    y_copy.wait_recv()
    total_ref[...] = (chip_ref[...].astype(F32) + y_land[...].astype(F32)).astype(BF16)
    total_copy.start()
    feed_copy.start()
    gain = gain_ref[...]
    near_at = pl.multiple_of((1 - shard) * half + lax.rem(ctx, 2) * part, part)
    far_at = pl.multiple_of((1 - shard) * half + (1 - lax.rem(ctx, 2)) * part, part)
    own_at = pl.multiple_of(shard * half, half)

    def norm_rows(source, base):
        def body(step, total):
            at = pl.multiple_of(step * step_rows, step_rows)
            here = pl.ds(pl.multiple_of(base + at, step_rows), step_rows)
            scale = scale_ref[here, :]
            normed = inputs_ref[here, :].astype(F32) * scale
            hidden = source[pl.ds(at, step_rows), :].astype(F32)
            grad = hidden * gain
            mean = jnp.sum(grad * normed, axis=-1, keepdims=True) * (1.0 / width)
            value = (grad_middle_ref[here, :] + scale * (grad - normed * mean)).astype(BF16)
            grad_ref[here, pl.ds(own_at, half)] = value[:, :half]
            grad_ref[here, pl.ds(near_at, part)] = value[:, half : half + part]
            grad_ref[here, pl.ds(far_at, part)] = value[:, half + part :]
            return total + jnp.sum(hidden * normed, axis=0, keepdims=True)

        return lax.fori_loop(0, half_rows // step_rows, body, jnp.zeros((1, width), F32))

    gain_sum = norm_rows(total_ref, mine)
    pump(10, 11)
    send_next(6, 7)
    total_copy.wait_recv()
    gains_ref[0:1, :] = gain_sum + norm_rows(other_ref, theirs)
    gain_send[:, pl.ds(near_send, part)] = gains_ref[:, half : half + part]
    gain_send[:, pl.ds(far_send, part)] = gains_ref[:, half + part :]
    gain_copy = x_copy(2 * cuts + 5, gain_send, gain_land)
    gain_copy.start()
    pump(11, 12)
    for copy in up_copies:
        copy.wait_recv()
    put(starts[2], feed_pieces(up_refs, up_land))
    send_next(7, 8)
    gain_copy.wait_recv()
    gain_mine[...] = gains_ref[:, :half] + gain_land[...]
    gain_all[ctx] = gain_mine[...]

    def gain_to(by, slot):
        return pltpu.make_async_remote_copy(
            src_ref=gain_mine, dst_ref=gain_all.at[slot], send_sem=gain_send_sem.at[by - 1],
            recv_sem=gain_recv_sem.at[by - 1], device_id={"ctx": lax.rem(ctx + by, 4)},
            device_id_type=mesh_id,
        )

    for by in (1, 2, 3):
        gain_to(by, ctx).start()
    pump(12, 14)
    send_next(8, len(queue))
    branch_copy.wait_recv()
    mixed_copy.wait_recv()
    put(
        starts[3],
        [
            functools.partial(
                outer, mixed_ref, mixed_land, branch_ref.at[:, :half], branch_land, block
            )
            for block in range(q_width // CHUNK_ROWS)
        ],
    )
    pump(14, 17)
    hidden_a_copy.wait_recv()
    qkv_copy.wait_recv()

    def side_by_side(first, number, columns):
        return jnp.concatenate(
            [
                outer(
                    hidden_a_ref, hidden_a_land, qkv_grad_ref.at[:, columns],
                    qkv_land.at[:, columns], block,
                )
                for block in range(first, first + number)
            ],
            axis=1,
        )

    q_blocks = CHUNK_COLUMNS // q_width
    put(
        starts[4],
        [
            functools.partial(side_by_side, first, q_blocks, slice(0, q_width))
            for first in range(0, half // CHUNK_ROWS, q_blocks)
        ]
        + [
            functools.partial(
                side_by_side, 0, half // CHUNK_ROWS, slice(q_width, q_width + 2 * kv_width)
            )
        ],
    )
    pump(17, count // split + lag)

    for by in (1, 2, 3):
        gain_to(by, lax.rem(ctx + 4 - by, 4)).wait_recv()
    gain_out_ref[...] = (gain_all[0] + gain_all[1]) + (gain_all[2] + gain_all[3])
    for by in (1, 2, 3):
        gain_to(by, ctx).wait_send()
    gain_copy.wait_send()
    feed_copy.wait_recv()
    for copy in queue[-2:] + [first_copy, y_copy, total_copy]:
        copy.wait_send()
    for copy in (middle_y_copy, middle_core_copy, feed_copy):
        copy.wait_send()
    for back in (1, 2):

        @pl.when(ctx >= back)
        def _():
            kv_copy(back).wait_send()

    @pl.when(is_middle)
    def _():
        for k in (count - 2, count - 1):
            outward_copy(jnp.int32(k)).wait_send()
            keep_copy(jnp.int32(k)).wait()

    @pl.when(is_end)
    def _():
        def close(k, carry):
            to_pair(share(pool_ref, k), sum_ref, k).wait_recv()
            return carry

        lax.fori_loop(0, count, close, 0)


def flat_call(body, operands, **call):
    flat, tree = jax.tree.flatten(operands)

    def unflatten(*refs):
        body(*jax.tree.unflatten(tree, refs[: len(flat)]), *refs[len(flat) :])

    in_specs = [pl.BlockSpec(memory_space=pl.ANY)] * len(flat)
    return pl.pallas_call(unflatten, in_specs=in_specs, **call)(*flat)


def tail(plan, pool, v):
    heads, group, lead, starts, count = plan
    rows, width = v["inputs"].shape
    half = width // 2
    q_width, kv_width = v["query"].shape[1], v["keys_values"].shape[1] // 2
    qkv_width = q_width + 2 * kv_width
    piece = (CHUNK_ROWS, CHUNK_COLUMNS)
    split = 2
    step, steps = (CHUNK_ROWS // split, CHUNK_COLUMNS), count * split
    cuts, feed_part = len(v["grad_gate"]), v["grad_gate"][0].shape[1]

    stored = [
        v["grad_gate"], v["grad_up"], v["hidden_m"], v["hidden_a"], v["mixed"],
        v["out_pieces"], v["query"], v["keys_values"], v["log_sums"], v["query_segments"],
        v["key_segments"], v["cosine"], v["sine"], v["qkv_pieces"], v["inputs"], v["scale"],
        v["gain"], v["normed_m"], v["middle_chip"], v["cotangent"], v["middle_scale"],
        v["middle_gain"],
    ]
    operands = [pool, v["hidden_m_send"], v["hidden_a_send"], v["feed_chip"], stored]
    loaded = jax.tree.map(lambda value: pltpu.VMEM(value.shape, value.dtype), stored)
    any_space, vmem_space = pl.BlockSpec(memory_space=pl.ANY), pl.BlockSpec(memory_space=pltpu.VMEM)
    line = jax.ShapeDtypeStruct(pool.shape, BF16)
    dma = pltpu.SemaphoreType.DMA
    low = lambda *shape: pltpu.VMEM(shape, BF16)
    wide = lambda *shape: pltpu.VMEM(shape, F32)
    scratch = [
        [low(rows, feed_part) for _ in range(cuts)],
        [low(rows, feed_part) for _ in range(cuts)],
        low(rows, half), low(rows, half), low(rows, half),
        low(rows, q_width), low(rows, qkv_width),
        low(rows, q_width), wide(rows, q_width), wide(3 * rows, 2 * kv_width),
        low(2, rows, 2 * kv_width), low(2, rows, 2 * kv_width), low(rows, qkv_width),
        low(rows // 2, width), wide(rows // 2, width), low(rows // 2, width),
        low(rows // 2, width), low(rows // 2, width), low(rows // 2, width),
        low(rows // 2, width),
        low(rows // 2, width), low(rows // 2, width), low(rows // 2, width),
        low(rows, width), low(rows, half),
        wide(8, width), wide(8, half), wide(8, half), wide(8, half), wide(4, 8, half),
        dma((3,)), dma((3,)),
        low(*step), low(*step), low(4, *step), low(*step), low(2, *step), low(2, *piece),
        dma((2 * cuts + 6,)), dma((2 * cuts + 6,)), dma((6,)), dma((6,)), dma((2,)), dma((2,)),
        dma((steps,)), dma((steps,)), dma((steps,)), dma((steps,)), dma((steps,)),
        dma((3,)), dma((2,)),
        loaded, dma((len(jax.tree.leaves(stored)),)),
    ]
    outs = flat_call(
        functools.partial(tail_body, plan),
        operands,
        out_specs=[any_space] * 5 + [vmem_space, vmem_space],
        out_shape=[
            line, line, line, line,
            jax.ShapeDtypeStruct((rows // 2, width), BF16),
            jax.ShapeDtypeStruct((rows, width), BF16),
            jax.ShapeDtypeStruct((8, half), F32),
        ],
        scratch_shapes=scratch,
        input_output_aliases={0: 0},
        compiler_params=pltpu.CompilerParams(
            collective_id=0, has_side_effects=True, vmem_limit_bytes=62 << 20
        ),
        cost_estimate=pl.CostEstimate(
            flops=400 << 30, bytes_accessed=30 << 20, transcendentals=0
        ),
        name="tail",
    )
    return outs[1], outs[4], outs[5], outs[6]


def swap(value, axis, size, bit):
    return lax.ppermute(value, axis, [(i, i ^ bit) for i in range(size)])


def shift(value, axis, size, by):
    if abs(by) >= size:
        return jnp.zeros_like(value)
    return lax.ppermute(
        value, axis, [(i, i + by) for i in range(size) if 0 <= i + by < size]
    )


class Lane:
    def __init__(self, move, depth=2):
        self.move, self.depth, self.done = move, depth, []

    def send(self, value):
        if len(self.done) >= self.depth:
            value, self.done[-self.depth] = tie(value, self.done[-self.depth])
        self.done.append(self.move(value))
        return len(self.done) - 1

    def get(self, at):
        return self.done[at]


def shards(
    sizes,
    block_input,
    segment_ids,
    attention_gain,
    query_weight,
    key_weight,
    value_weight,
    out_weight,
    feed_gain,
    gate_weight,
    up_weight,
    down_weight,
    cotangent,
):
    shard_count, ctx_count, tp_count = sizes
    seqs, span, width = block_input.shape
    rows = seqs * span
    seq_length = segment_ids.shape[1]
    half = width // 2
    part = half // 2
    q_width = query_weight.shape[1]
    kv_width = key_weight.shape[1]
    feed_width = gate_weight.shape[1]
    group = q_width // kv_width
    shard, ctx, tp = (lax.axis_index(name) for name in ("fsdp", "ctx", "tp"))
    odd = ctx % 2
    sibling = tp % 2

    own_at = shard * half
    near_at = (1 - shard) * half + odd * part
    far_at = (1 - shard) * half + (1 - odd) * part

    def to_local(value):
        return jnp.concatenate(
            [
                take(value, own_at, half, 1),
                take(value, near_at, part, 1),
                take(value, far_at, part, 1),
            ],
            axis=1,
        )

    def other_half(value):
        return jnp.concatenate(
            [
                take(value, half + odd * part, part, 1),
                take(value, half + (1 - odd) * part, part, 1),
            ],
            axis=1,
        )

    def from_local(value):
        own, other = value[:, :half], other_half(value)
        return jnp.where(
            shard == 0,
            jnp.concatenate([own, other], axis=1),
            jnp.concatenate([other, own], axis=1),
        )

    fsdp_lane = Lane(lambda value: swap(value, "fsdp", shard_count, 1))

    def over_fsdp(value):
        return swap(value, "fsdp", shard_count, 1)

    def over_ctx(value):
        return swap(value, "ctx", ctx_count, 1)

    def near_part(weight, axis):
        return take(weight, odd * part, part, axis)

    def core_half(value):
        return take(value, sibling * (rows // 2), rows // 2, 0)

    def join_cores(mine):
        other = swap(mine, "tp", tp_count, 1)
        return jnp.where(
            sibling == 0,
            jnp.concatenate([mine, other], axis=0),
            jnp.concatenate([other, mine], axis=0),
        )

    def chip_sum(first, second):
        return (second + swap(first, "tp", tp_count, 1).astype(F32)).astype(BF16)

    def finish_sum(chip):
        total = (chip.astype(F32) + swap(chip, "tp", tp_count, 2).astype(F32)).astype(BF16)
        return join_cores(total).astype(F32)

    def tp_sum(first, second):
        if tp_count != 4:
            whole_rows = jnp.where(
                sibling == 0,
                jnp.concatenate([second, first.astype(F32)], axis=0),
                jnp.concatenate([first.astype(F32), second], axis=0),
            )
            return lax.psum(whole_rows, "tp")
        return finish_sum(chip_sum(first, second))

    gains_own = jnp.stack([attention_gain, feed_gain])
    qkv_own = jnp.concatenate([query_weight, key_weight, value_weight], axis=1)
    feed_cuts = 2
    feed_part = feed_width // feed_cuts
    columns = [slice(cut * feed_part, (cut + 1) * feed_part) for cut in range(feed_cuts)]
    grad_rows = to_local(cotangent.reshape(rows, width))
    send_gate = [near_part(gate_weight[:, cut], 0) for cut in columns]
    send_up = [near_part(up_weight[:, cut], 0) for cut in columns]
    send_down = [near_part(down_weight[cut], 1) for cut in columns]
    send_grad = core_half(other_half(grad_rows))

    gains_other = over_fsdp(gains_own)
    near_qkv = over_fsdp(near_part(qkv_own, 0))
    gains_other, send_out = tie(gains_other, near_part(out_weight, 1))
    near_out = over_fsdp(send_out)

    span_start = ctx * span
    positions = take(doc_positions(segment_ids), span_start, span, 1).reshape(rows)
    query_segments = take(segment_ids, span_start, span, 1)
    cosine, sine = rope_tables(positions)
    blocks_back, base, lead = attention_plan(span, WINDOW)
    key_segments = take(
        jnp.pad(segment_ids, ((0, 0), (blocks_back * span, 0)), constant_values=-1),
        span_start,
        (blocks_back + 1) * span,
        1,
    )

    inputs = to_local(block_input.reshape(rows, width)).astype(F32)
    scale_a = row_scale_of(inputs)
    normed_a = inputs * scale_a
    gains = jnp.concatenate(
        [gains_own, take(gains_other, odd * part, part, 1), take(gains_other, (1 - odd) * part, part, 1)],
        axis=1,
    ).astype(F32)
    gain_a, gain_m = gains[0:1], gains[1:2]
    hidden_a = (normed_a * gain_a).astype(BF16)

    near_qkv, send_gate[0] = tie(near_qkv, send_gate[0])
    near_gate, near_up, far_gate, far_up = ([None] * feed_cuts for _ in range(4))
    near_gate[0] = over_fsdp(send_gate[0])
    far_qkv = over_ctx(near_qkv)
    near_out, send_up[0] = tie(near_out, send_up[0])
    near_up[0] = over_fsdp(send_up[0])
    far_qkv, near_out = tie(far_qkv, near_out)
    far_out = over_ctx(near_out)

    def dot_pieces(matrix, own, near, far):
        return (
            dot_rows(matrix[:, :half], own)
            + dot_rows(matrix[:, half : half + part], near)
            + dot_rows(matrix[:, half + part :], far)
        )

    def back_pieces(matrix, own, near, far):
        return jnp.concatenate(
            [dot_back(matrix, own), dot_back(matrix, near), dot_back(matrix, far)], axis=1
        )

    qkv = dot_pieces(hidden_a, qkv_own, near_qkv, far_qkv)
    key_low = rotate(qkv[:, q_width : q_width + kv_width], cosine, sine).astype(BF16)
    value_low = qkv[:, q_width + kv_width :].astype(BF16)
    keys_values = jnp.concatenate([key_low, value_low], axis=1).reshape(seqs, span, 2 * kv_width)
    query_low = (rotate(qkv[:, :q_width], cosine, sine).astype(BF16) * HD**-0.5).reshape(
        seqs, span, q_width
    )
    earlier = [shift(keys_values, "ctx", ctx_count, back) for back in range(blocks_back, 0, -1)]
    *earlier, query_low, near_up[0] = tie(*earlier, query_low, near_up[0])
    far_up[0] = over_ctx(near_up[0])
    keys_values = jnp.concatenate(earlier + [keys_values], axis=1)
    mixed, log_sums = attend_forward(
        query_low, keys_values, query_segments, key_segments, base, lead, group
    )
    mixed_low = mixed.reshape(rows, q_width)
    mixed_low, far_out, near_gate[0], send_gate[1] = tie(
        mixed_low, far_out, near_gate[0], send_gate[1]
    )
    near_gate[1] = over_fsdp(send_gate[1])
    far_gate[0] = over_ctx(near_gate[0])

    def out_project(at):
        matrix = take(mixed_low, at * (rows // 2), rows // 2, 0)
        return jnp.concatenate(
            [dot_rows(matrix, out_weight), dot_rows(matrix, near_out), dot_rows(matrix, far_out)],
            axis=1,
        )

    first, second = out_project(1 - sibling).astype(BF16), out_project(sibling)
    if tp_count == 4:
        chip = chip_sum(first, second)
        chip, near_gate[1], far_up[0], send_up[1] = tie(
            chip, near_gate[1], far_up[0], send_up[1]
        )
        near_up[1] = over_fsdp(send_up[1])
        far_gate[1] = over_ctx(near_gate[1])
        total = (chip.astype(F32) + swap(chip, "tp", tp_count, 2).astype(F32)).astype(BF16)
        total, near_up[1], far_gate[0], send_down[0] = tie(
            total, near_up[1], far_gate[0], send_down[0]
        )
        branch_a = join_cores(total).astype(F32)
    else:
        branch_a = tp_sum(first, second)
        near_up[1] = over_fsdp(send_up[1])
        far_gate[1] = over_ctx(near_gate[1])
    near_down = [over_fsdp(send_down[0])]
    far_up[1] = over_ctx(near_up[1])
    middle = inputs + branch_a

    scale_m = row_scale_of(middle)
    normed_m = middle * scale_m
    hidden_m = (normed_m * gain_m).astype(BF16)
    gate_cuts, up_cuts, act_cuts = [], [], []

    def feed(cut):
        gate_value, up_value, activated = feed_forward(
            hidden_m,
            (gate_weight, near_gate[cut], far_gate[cut]),
            (up_weight, near_up[cut], far_up[cut]),
            cut,
            feed_part,
        )
        gate_cuts.append(gate_value)
        up_cuts.append(up_value)
        act_cuts.append(activated)

    feed(0)
    act_cuts[0], near_down[0], far_gate[1], send_down[1] = tie(
        act_cuts[0], near_down[0], far_gate[1], send_down[1]
    )
    near_down.append(over_fsdp(send_down[1]))
    far_down = [over_ctx(near_down[0])]
    feed(1)
    act_cuts[1], near_down[1], send_grad, act_cuts[0] = tie(
        act_cuts[1], near_down[1], send_grad, act_cuts[0]
    )
    other_grad = over_fsdp(send_grad)
    act_other = [over_fsdp(act_cuts[0]), over_fsdp(act_cuts[1])]
    far_down.append(over_ctx(near_down[1]))

    pieces = CHUNK_ROWS * CHUNK_COLUMNS
    down_count = feed_width * half // pieces
    starts, pool_size = [], 0
    for size in (feed_width * half,) * 3 + (q_width * half,) * 2 + (2 * kv_width * half,):
        starts.append(pool_size)
        pool_size += size // pieces
    piece_count = pool_size
    widen_group = 1 if any(start % 2 for start in starts) else 2
    pool_size += -pool_size % widen_group
    grad_gate_cuts, grad_up_cuts = [], []
    for cut in range(feed_cuts):
        grad_gate, grad_up = feed_backward(
            grad_rows,
            (down_weight, near_down[cut], far_down[cut]),
            gate_cuts[cut],
            up_cuts[cut],
            cut,
        )
        grad_gate_cuts.append(grad_gate)
        grad_up_cuts.append(grad_up)

    grad_gate_cuts[1], act_other[0] = tie(grad_gate_cuts[1], act_other[0])
    first, second = project(
        sibling,
        list(zip(grad_gate_cuts, grad_up_cuts)),
        [
            (
                (gate_weight, near_gate[cut], far_gate[cut]),
                (up_weight, near_up[cut], far_up[cut]),
            )
            for cut in range(feed_cuts)
        ],
        width,
        True,
    )
    first, second, other_grad, *act_cuts = tie(first, second, other_grad, *act_cuts)
    grad_own, grad_other = grad_rows[:, :half], join_cores(other_grad)
    fused = (shard_count, ctx_count, tp_count) == (2, 4, 4)
    fused = fused and seqs == 1 and (blocks_back, base, span) == (2, 0, 4 * LANES)
    if fused:
        middle_chip = chip_sum(first, second)
    else:
        grad_hidden_m = tp_sum(first, second)
    fsdp_lane.done = list(act_other)
    pool = None
    for cut in range(feed_cuts):
        pool = outer_sum(
            pool,
            cut * down_count // feed_cuts,
            pool_size,
            act_cuts[cut],
            act_other[cut],
            [grad_own],
            [grad_other],
        )

    first, second = project(
        sibling,
        [(value,) for value in act_cuts],
        [((down_weight, near_down[cut], far_down[cut]),) for cut in range(feed_cuts)],
        width,
        False,
    )
    if fused:
        feed_chip = chip_sum(first, second)
    else:
        branch_m = tp_sum(first, second)

    if fused:
        tile = min(LANES, rows)
        log_rows = jnp.swapaxes(log_sums[0, :, : q_width // HD].reshape(rows // tile, tile, -1), 1, 2)
        pool, across, input_grad, gain_sums = tail(
            (
                q_width // HD,
                group,
                lead,
                tuple(starts),
                piece_count,
            ),
            pool,
            {
                "grad_gate": grad_gate_cuts,
                "grad_up": grad_up_cuts,
                "hidden_m": hidden_m[:, :half],
                "hidden_m_send": other_half(hidden_m),
                "hidden_a": hidden_a[:, :half],
                "hidden_a_send": other_half(hidden_a),
                "mixed": mixed_low,
                "out_pieces": [out_weight, near_out, far_out],
                "query": query_low[0],
                "keys_values": keys_values[0],
                "log_sums": log_rows,
                "query_segments": query_segments.reshape(rows // tile, 1, tile),
                "key_segments": key_segments.reshape(-1, 1),
                "cosine": cosine,
                "sine": sine,
                "qkv_pieces": [qkv_own, near_qkv, far_qkv],
                "inputs": inputs.astype(BF16),
                "scale": scale_a,
                "gain": gain_a,
                "normed_m": normed_m,
                "middle_chip": middle_chip,
                "cotangent": grad_rows,
                "middle_scale": scale_m,
                "middle_gain": gain_m,
                "feed_chip": feed_chip,
            },
        )
        input_grad = input_grad.reshape(seqs, span, width)
        total = (feed_chip.astype(F32) + across.astype(F32)).astype(BF16)
        branch_m = join_cores(total).astype(F32)
    else:
        feed_gain_part = jnp.sum(grad_hidden_m * normed_m, axis=0)
        grad_middle = norm_back(grad_hidden_m, gain_m, normed_m, scale_m, grad_rows.astype(F32))
        grad_branch = grad_middle.astype(BF16)
        gate_at = [fsdp_lane.send(value) for value in grad_gate_cuts]
        up_at = [fsdp_lane.send(value) for value in grad_up_cuts]
        hidden_m_at = fsdp_lane.send(core_half(other_half(hidden_m)))
        hidden_own, hidden_other = hidden_m[:, :half], join_cores(fsdp_lane.get(hidden_m_at))
        for which, (own, at) in enumerate(((grad_gate_cuts, gate_at), (grad_up_cuts, up_at))):
            pool = outer_sum(
                pool,
                starts[1 + which],
                pool_size,
                hidden_own,
                hidden_other,
                own,
                [fsdp_lane.get(i) for i in at],
            )

        grad_mixed = (
            dot_back(grad_branch[:, :half], out_weight)
            + dot_back(grad_branch[:, half : half + part], near_out)
            + dot_back(grad_branch[:, half + part :], far_out)
        ).astype(BF16)
        branch_at = fsdp_lane.send(core_half(other_half(grad_branch)))
        mixed_at = fsdp_lane.send(mixed_low)
        hidden_a_at = fsdp_lane.send(core_half(other_half(hidden_a)))
        grad_query, grad_keys_values = attend_backward(
            query_low,
            keys_values,
            grad_mixed.reshape(seqs, span, q_width),
            jnp.swapaxes(log_sums, 1, 2)[:, : q_width // HD],
            query_segments,
            key_segments,
            base,
            lead,
            group,
        )
        kv_sum = grad_keys_values[:, blocks_back * span :]
        for back in range(1, blocks_back + 1):
            at = (blocks_back - back) * span
            kv_sum = kv_sum + shift(
                grad_keys_values[:, at : at + span].astype(BF16), "ctx", ctx_count, -back
            ).astype(F32)
        kv_sum = kv_sum.reshape(rows, 2 * kv_width)
        grad_qkv = jnp.concatenate(
            [
                rotate(grad_query.reshape(rows, q_width), cosine, -sine),
                rotate(kv_sum[:, :kv_width], cosine, -sine),
                kv_sum[:, kv_width:],
            ],
            axis=1,
        ).astype(BF16)
        qkv_at = fsdp_lane.send(grad_qkv)
        first, second = (
            back_pieces(take(grad_qkv, at * (rows // 2), rows // 2, 0), qkv_own, near_qkv, far_qkv)
            for at in (1 - sibling, sibling)
        )
        grad_hidden_a = tp_sum(first.astype(BF16), second)
        attention_gain_part = jnp.sum(grad_hidden_a * normed_a, axis=0)
        input_grad = norm_back(grad_hidden_a, gain_a, normed_a, scale_a, grad_middle)
        input_grad = from_local(input_grad.astype(BF16)).reshape(seqs, span, width)

        pool = outer_sum(
            pool,
            starts[3],
            pool_size,
            mixed_low,
            fsdp_lane.get(mixed_at),
            [grad_branch[:, :half]],
            [join_cores(fsdp_lane.get(branch_at))],
        )
        qkv_other = fsdp_lane.get(qkv_at)
        hidden_own, hidden_other = hidden_a[:, :half], join_cores(fsdp_lane.get(hidden_a_at))
        for which, cut in ((4, slice(0, q_width)), (5, slice(q_width, None))):
            pool = outer_sum(
                pool,
                starts[which],
                pool_size,
                hidden_own,
                hidden_other,
                [grad_qkv[:, cut]],
                [qkv_other[:, cut]],
            )
        gain_parts = jnp.stack([attention_gain_part, feed_gain_part])
        gain_other = over_fsdp(other_half(gain_parts))
        gain_sums = lax.psum(gain_parts[:, :half] + gain_other, "ctx")
        pool = lax.psum(pool.astype(F32), "ctx")

    block_out = from_local((middle + branch_m).astype(BF16)).reshape(seqs, span, width)

    down_grad, gate_grad, up_grad, out_grad, query_grad, key_grad, value_grad = widen(
        pool,
        starts,
        [
            down_weight.shape,
            gate_weight.shape,
            up_weight.shape,
            out_weight.shape,
            query_weight.shape,
            key_weight.shape,
            value_weight.shape,
        ],
        widen_group,
    )
    return (
        block_out,
        input_grad,
        gain_sums[0],
        query_grad,
        key_grad,
        value_grad,
        out_grad,
        gain_sums[1],
        gate_grad,
        up_grad,
        down_grad,
    )


def solution(mesh):
    sizes = tuple(mesh.shape[name] for name in ("fsdp", "ctx", "tp"))
    in_specs = (
        P("fsdp", "ctx", None),
        P("fsdp", None),
        P("fsdp"),
        P("fsdp", "tp"),
        P("fsdp", "tp"),
        P("fsdp", "tp"),
        P("tp", "fsdp"),
        P("fsdp"),
        P("fsdp", "tp"),
        P("fsdp", "tp"),
        P("tp", "fsdp"),
        P("fsdp", "ctx", None),
    )
    out_specs = (
        P("fsdp", "ctx", None),
        P("fsdp", "ctx", None),
        P("fsdp"),
        P("fsdp", "tp"),
        P("fsdp", "tp"),
        P("fsdp", "tp"),
        P("tp", "fsdp"),
        P("fsdp"),
        P("fsdp", "tp"),
        P("fsdp", "tp"),
        P("tp", "fsdp"),
    )
    return jax.shard_map(
        functools.partial(shards, sizes),
        mesh=mesh,
        in_specs=in_specs,
        out_specs=out_specs,
        check_vma=False,
    )
```
